32 devices in a mesh: section: 4 (over x, core), dp: 8 (over z, y).
Axes of the slice: x: 2, y: 2, z: 4, core: 2. Of those that a mesh axis runs over, the one named last changes fastest.
Arguments:
- inputs: bfloat16 [2, 4096, 768], P(None, 'dp'), may hold values from -6 to 6
- segment_ids: int32 [2, 4096], P(None, 'dp'), may hold values from 0 to 31, never falling along the last dimension, each value on 1 to 512 neighbouring positions
- w_in: bfloat16 [4, 768, 3072], P('section'), may hold values from -3 to 3
- w_down: bfloat16 [4, 3072, 768], P('section'), may hold values from -0.109375 to 0.109375
- vec_in: float32 [4, 3072], P('section'), may hold values from -3 to 3
- vec_out: float32 [4, 2304], P('section'), may hold values from -2 to 2
- cotangent: bfloat16 [2, 4096, 768], P(None, 'dp'), may hold values from -6 to 6
Outputs:
- mixed: bfloat16 [2, 4096, 768], P(None, 'dp', 'section')
- input_grad: bfloat16 [2, 4096, 768], P(None, 'dp', 'section')
- grad_w_in: float32 [4, 768, 3072], P('section', 'dp')
- grad_w_down: float32 [4, 3072, 768], P('section', 'dp')
- grad_vec_in: float32 [4, 3072], P('section', 'dp')
- grad_vec_out: float32 [4, 2304], P('section', 'dp')
The draws below stay inside these ranges and needn't reach their ends.
Inputs may be any that keep to these rules, and one draw needn't show every extreme that they name: Along a row of segment_ids the ids never fall; one id covers at most 512 rows, and some id covers exactly 512.
All inputs are finite; a program needn't handle non-finite values.
Results may differ from the reference program's by a relative error of at most 0.024.
Values may be sent and summed in bfloat16 or wider, within the bound.
A program may use at most 384 MiB of HBM per device.

```python
import math
import jax
import jax.numpy as jnp
import numpy as np
from jax import lax

D = 768
HEADS = 12
HEAD_DIM = 64
FF = 3072
BLK = 512
MICRO = 2
ROWS_MB = 4096
N_SECTION = 4


def draw_w_in(key, part):
    key = jax.random.fold_in(key, 7)
    base = jax.random.truncated_normal(key, -4.0, 4.0, (N_SECTION, D, FF), jnp.float32)
    columns = jnp.arange(FF)[None, None, :]
    section_num = jnp.arange(N_SECTION)[:, None, None]
    boost = jnp.where((section_num % 2 == 0) & (columns >= 3 * D), 6.0, 1.0)
    return (base * boost * D ** (-0.5)).astype(jnp.bfloat16)


def draw_vec_out(key, part):
    key = jax.random.fold_in(key, 19)
    base = jax.random.truncated_normal(key, -2.0, 2.0, (N_SECTION, 3 * D), jnp.float32) * 0.5
    columns = jnp.arange(3 * D)[None, :]
    return jnp.where(columns < D, 1.0 + 0.5 * base, 1.2 * base)


def shard_levels(rng, dims, cuts, least, high):
    level = 1.0
    for position, shards_of in cuts:
        heights = jax.random.uniform(jax.random.fold_in(jax.random.fold_in(rng, 6), position), (shards_of,), jnp.float32, least / len(cuts), high / len(cuts))
        level = level * jnp.repeat(jnp.exp(heights), dims[position] // shards_of).reshape((-1,) + (1,) * (len(dims) - 1 - position))
    return level


def split_up(count, total, limit, lean):
    weights = [(1 << 20) // math.isqrt(rank ** lean) + 1 for rank in range(2, count + 1)]
    spare, holding = total - limit - (count - 1), [1] * (count - 1)
    while spare > 0:
        free = [i for i in range(count - 1) if holding[i] < limit]
        mass, remaining = sum([weights[i] for i in free]), spare
        for i in free:
            addition = min(limit - holding[i], max(1, remaining * weights[i] // mass), spare)
            holding[i] = holding[i] + addition
            spare = spare - addition
    return np.array([limit] + holding)


def uneven(stream_key, number_of, total, reach, lean):
    if number_of == 2:
        one = jax.random.randint(stream_key, (), max(1, total - reach), min(reach, total - 1) + 1)
        return jnp.stack([one, total - one])
    sizes = jnp.asarray(split_up(number_of, total, reach, lean), jnp.int32)
    twos = (number_of - 1) // 2
    source_of, sink = sizes[1:1 + 2 * twos:2], sizes[2:2 + 2 * twos:2]
    slack = jnp.minimum(source_of - 1, reach - sink)
    passed = jax.random.randint(jax.random.fold_in(stream_key, 1), (twos,), 0, 1 << 20) % (slack + 1)
    sizes = sizes.at[1:1 + 2 * twos:2].set(source_of - passed).at[2:2 + 2 * twos:2].set(sink + passed)
    return sizes[jax.random.permutation(jax.random.fold_in(stream_key, 2), number_of)]


def gaussian(rng, dims, width, most, split=(), kind=jnp.bfloat16):
    values = width * jax.random.normal(rng, dims, jnp.float32)
    if split:
        values = values * shard_levels(rng, dims, split, -0.22, 0.18)
    return jnp.clip(values, -most, most).astype(kind)


def setup_inputs(seed: int = 0) -> dict:
    key_of = jax.random.split(jax.random.key(seed), 8)
    return {
        "inputs": gaussian(key_of[0], (MICRO, ROWS_MB, D), 1.0, 6.0, ((1, 8),)),
        "segment_ids": jax.vmap(lambda own: jnp.searchsorted(jnp.cumsum(uneven(own, ROWS_MB // (BLK // 4), ROWS_MB, BLK, 2)), jnp.arange(ROWS_MB), side="right"))(jax.random.split(key_of[1], MICRO)).reshape((MICRO, ROWS_MB)).astype(jnp.int32),
        "w_in": draw_w_in(jax.random.fold_in(key_of[7], 71), 0),
        "w_down": gaussian(key_of[3], (N_SECTION, FF, D), FF ** -0.5, 0.109375, ((0, 4),)),
        "vec_in": gaussian(key_of[4], (N_SECTION, FF), 0.5, 3.0, ((0, 4),), jnp.float32),
        "vec_out": draw_vec_out(jax.random.fold_in(key_of[7], 71), 0),
        "cotangent": gaussian(key_of[6], (MICRO, ROWS_MB, D), 1.0, 6.0, ((1, 8),)),
    }


@jax.custom_vjp
def low(v):
    return lax.optimization_barrier(v.astype(jnp.bfloat16)).astype(jnp.float32)

@jax.custom_vjp
def low_back(v):
    return v

def low_keep(v):
    return (low(v), None)

def low_pass(kept, grad):
    return (grad,)

def back_keep(v):
    return (v, None)

def back_low(kept, grad):
    return (low(grad),)
low.defvjp(low_keep, low_pass)
low_back.defvjp(back_keep, back_low)
EPS = 1e-06
NEG = -1e+30
HIGH = lax.Precision.HIGHEST

def product(left, right):
    return jnp.dot(left, right, precision=HIGH, preferred_element_type=jnp.float32)

def layer_norm(summed, norm_gain, norm_bias):
    average = lax.optimization_barrier(jnp.mean(summed, axis=-1, keepdims=True))
    centred = summed - average
    spread = lax.optimization_barrier(jnp.mean(centred * centred, axis=-1, keepdims=True))
    return centred * lax.rsqrt(spread + EPS) * norm_gain + norm_bias

def rotary_tables(seg_rows, head_dim):
    blocks = seg_rows.reshape(-1, BLK)
    offsets = jnp.arange(BLK, dtype=jnp.int32)
    same_doc = blocks[:, :, None] == blocks[:, None, :]
    opener = lax.optimization_barrier(jnp.min(jnp.where(same_doc, offsets[None, None, :], BLK), axis=2))
    places = (offsets[None, :] - opener).astype(jnp.float32).reshape(-1)
    frequency = jnp.exp(jnp.arange(head_dim // 2, dtype=jnp.float32) * (-2.0 * math.log(10000.0) / head_dim))
    angles = places[:, None] * frequency[None, :]
    return (jnp.cos(angles)[:, None, :], jnp.sin(angles)[:, None, :])

def rotate(values, cos_tab, sin_tab):
    half_dim = values.shape[-1] // 2
    front_half = values[..., :half_dim]
    back_half = values[..., half_dim:]
    return jnp.concatenate([front_half * cos_tab - back_half * sin_tab, back_half * cos_tab + front_half * sin_tab], axis=-1)

def attention_section(section_in, seg_rows, w_main, bias_in, bias_out):
    row_count = section_in.shape[0]
    score_scale = HEAD_DIM ** (-0.5)
    cos_tab, sin_tab = rotary_tables(seg_rows, HEAD_DIM)
    project = product(section_in, w_main[:, :3 * D]) + bias_in[:3 * D]
    heads_shape = (row_count, HEADS, HEAD_DIM)
    queries = low(rotate(low_back(project[:, :D]).reshape(heads_shape), cos_tab, sin_tab))
    keys_rot = low(rotate(low_back(project[:, D:2 * D]).reshape(heads_shape), cos_tab, sin_tab))
    values = low_back(low(project[:, 2 * D:3 * D])).reshape(heads_shape)

    def attend(pieces):
        q_blk, k_blk, v_blk, seg_blk = pieces
        scores = low_back(jnp.einsum('qhd,khd->hqk', q_blk, k_blk, precision=HIGH) * score_scale)
        same_doc = (seg_blk[:, None] == seg_blk[None, :])[None]
        scores = jnp.where(same_doc, scores, NEG)
        row_peak = lax.optimization_barrier(jnp.max(scores, axis=-1, keepdims=True))
        exp_scores = jnp.exp(scores - row_peak)
        probs_low = low(exp_scores / lax.optimization_barrier(jnp.sum(exp_scores, axis=-1, keepdims=True)))
        return jnp.einsum('hqk,khd->qhd', probs_low, v_blk, precision=HIGH).reshape(BLK, D)
    block_shape = (-1, BLK, HEADS, HEAD_DIM)
    attended = lax.map(jax.checkpoint(attend), (queries.reshape(block_shape), keys_rot.reshape(block_shape), values.reshape(block_shape), seg_rows.reshape(-1, BLK)))
    attended = low_back(low(attended.reshape(row_count, D)))
    branch = low_back(product(attended, w_main[:, 3 * D:]) + bias_out[2 * D:])
    return layer_norm(branch + section_in, bias_out[:D], bias_out[D:2 * D])

def feed_section(section_in, w_main, w_low, bias_in, bias_out):
    hidden = low_back(product(section_in, w_main) + bias_in)
    active = low(jax.nn.gelu(hidden, approximate=True))
    branch = low_back(product(active, w_low) + bias_out[2 * D:])
    return layer_norm(branch + section_in, bias_out[:D], bias_out[D:2 * D])

def forward(section_in, seg_rows, w_in, w_down, vec_in, vec_out):
    result = section_in
    for section_num in range(N_SECTION):
        if section_num % 2 == 0:
            result = attention_section(section_in, seg_rows, w_in[section_num], vec_in[section_num], vec_out[section_num])
        else:
            result = feed_section(section_in, w_in[section_num], w_down[section_num], vec_in[section_num], vec_out[section_num])
        if section_num < N_SECTION - 1:
            section_in = low_back(low(result))
    return result

def reference(inputs, segment_ids, w_in, w_down, vec_in, vec_out, cotangent):
    group_rows = 8 * BLK
    act_groups = inputs.astype(jnp.float32).reshape(-1, group_rows, D)
    seg_groups = segment_ids.reshape(-1, group_rows)
    cot_groups = cotangent.astype(jnp.float32).reshape(-1, group_rows, D)
    weights = (w_in.astype(jnp.float32), w_down.astype(jnp.float32), vec_in, vec_out)

    def scan_step(running, pieces):
        act_group, seg_group, cot_group = pieces

        def local_forward(section_in, w_one, w_two, v_one, v_two):
            return forward(section_in, seg_group, w_one, w_two, v_one, v_two)
        result, pull_back = jax.vjp(local_forward, act_group, *weights)
        grads = pull_back(cot_group)
        running = tuple((total + term for total, term in zip(running, grads[1:])))
        return (running, (result.astype(jnp.bfloat16), grads[0].astype(jnp.bfloat16)))
    zeros_init = tuple((jnp.zeros_like(weight) for weight in weights))
    totals, (outputs, in_grads) = lax.scan(scan_step, zeros_init, (act_groups, seg_groups, cot_groups))
    return (outputs.reshape(MICRO, ROWS_MB, D), in_grads.reshape(MICRO, ROWS_MB, D), totals[0], totals[1], totals[2], totals[3])
```

```python
import functools
import math

import jax
import jax.numpy as jnp
from jax import lax
from jax.experimental import pallas as pl
from jax.experimental.pallas import tpu as pltpu
from jax.sharding import PartitionSpec as P

D = 768
HEADS = 12
HEAD_DIM = 64
FF = 3072
BLK = 512
MICRO = 2
CH = 256
GROUP = 8
EPS = 1e-06
NEG = -1e30
K0 = math.sqrt(2.0 / math.pi)
K1 = K0 * 0.044715
MIB = 1 << 20
bf16, f32 = jnp.bfloat16, jnp.float32
MESH = pl.DeviceIdType.MESH
NN = (((1,), (0,)), ((), ()))
NT = (((1,), (1,)), ((), ()))
TN = (((0,), (0,)), ((), ()))
TT = (((0,), (1,)), ((), ()))
PARTS_IN = ((0, 2304, (0, 1, 2)), (2304, 768, (1, 0, 2)))
PARTS_DOWN = ((0, 512, (0, 1, 2)), (512, 256, (1, 0, 2)))


def dot(a, b, dims):
    return lax.dot_general(a, b, dims, preferred_element_type=f32)


def bit(value, b):
    return (value // (1 << b)) % 2


def chunks(me, order, step, flip):
    base = sum(bit(me, order[i]) * (1 << order[i]) for i in range(step))
    own = bit(me, order[step])
    base = base + ((1 - own) if flip else own) * (1 << order[step])
    free = order[step + 1 :]
    out = []
    for k in range(1 << len(free)):
        out.append(base + sum(((k >> i) & 1) << free[i] for i in range(len(free))))
    return out


FIRST_SLOT = (0, 4, 6)


def kernel(
    low,
    inputs,
    seg,
    w_in,
    w_down,
    vec_in,
    vec_out,
    cotangent,
    mixed,
    in_grad,
    out_in,
    out_down,
    out_vec,
    wi,
    wd,
    a_buf,
    d_buf,
    y_buf,
    e_buf,
    q_buf,
    p_buf,
    xh,
    rstd,
    bias,
    rope,
    inv,
    bias_t,
    dw,
    dv,
    split,
    acc,
    db,
    vec_send,
    vec_recv,
    w_sem,
    load_sem,
    fwd_send,
    fwd_recv,
    bwd_send,
    bwd_recv,
    mix_send,
    mix_recv,
    grad_recv,
    vec_ssem,
    vec_rsem,
    free_sem,
    rs_send,
    rs_recv,
    out_sem,
):
    sec = lax.axis_index("section")
    dp = lax.axis_index("dp")
    me = dp // low
    even = sec % 2 == 0
    odd = sec % 2 == 1

    def peer(b):
        return dp + (1 - 2 * bit(me, b)) * (1 << b) * low

    load_wi = pltpu.make_async_copy(w_in.at[0], wi, w_sem.at[0])
    load_wd = pltpu.make_async_copy(w_down.at[0], wd, w_sem.at[1])

    def load_a(m):
        return pltpu.make_async_copy(inputs.at[m], a_buf.at[m], load_sem.at[m])

    def load_d(m):
        return pltpu.make_async_copy(cotangent.at[m], d_buf.at[m], load_sem.at[m])

    @pl.when(sec == 0)
    def _():
        for m in range(MICRO):
            load_a(m).start()

    load_wi.start()

    @pl.when(odd)
    def _():
        load_wd.start()

    @pl.when(sec == 3)
    def _():
        for m in range(MICRO):
            load_d(m).start()

    barrier = pltpu.get_barrier_semaphore()
    for k in range(1, 4):
        pl.semaphore_signal(barrier, inc=1, device_id={"section": (sec + k) % 4}, device_id_type=MESH)
    for k in range(1, GROUP):
        pl.semaphore_signal(barrier, inc=1, device_id={"dp": (dp + k * low) % (GROUP * low)}, device_id_type=MESH)

    acc[...] = jnp.zeros_like(acc)
    db[...] = jnp.zeros_like(db)

    def clear(i, _):
        rows = pl.ds(pl.multiple_of(i * 96, 96), 96)
        dw[rows, :] = jnp.zeros((96, FF), bf16)
        return 0

    lax.fori_loop(0, 8, clear, 0)

    def clear_down(i, _):
        rows = pl.ds(pl.multiple_of(i * 384, 384), 384)
        dv[rows, :] = jnp.zeros((384, D), bf16)
        return 0

    @pl.when(odd)
    def _():
        lax.fori_loop(0, 8, clear_down, 0)

    def rows_of(c):
        return pl.ds(pl.multiple_of(c * CH, CH), CH)

    def forward_copy(m, c):
        rows = rows_of(c)
        return pltpu.make_async_remote_copy(
            src_ref=y_buf.at[m, rows],
            dst_ref=a_buf.at[m, rows],
            send_sem=fwd_send.at[m, c],
            recv_sem=fwd_recv.at[m, c],
            device_id={"section": sec + 1},
            device_id_type=MESH,
        )

    def backward_copy(m, c):
        rows = rows_of(c)
        return pltpu.make_async_remote_copy(
            src_ref=d_buf.at[m, rows],
            dst_ref=d_buf.at[m, rows],
            send_sem=bwd_send.at[m, c],
            recv_sem=bwd_recv.at[m, c],
            device_id={"section": sec - 1},
            device_id_type=MESH,
        )

    def share_copy(m, c, k, out, recv):
        rows = rows_of(c)
        return pltpu.make_async_remote_copy(
            src_ref=split.at[k, m, rows],
            dst_ref=out.at[m, rows],
            send_sem=mix_send.at[k, m, c],
            recv_sem=recv.at[m, c],
            device_id={"section": k},
            device_id_type=MESH,
        )

    def own_copy(m, c, k, out):
        rows = rows_of(c)
        return pltpu.make_async_copy(split.at[k, m, rows], out.at[m, rows], mix_send.at[k, m, c])

    def share(m, c, value, own, out, recv):
        for k in range(4):
            split[k, m, rows_of(c), :] = value[:, 192 * k : 192 * (k + 1)]
        for k in range(4):
            if k == own:
                own_copy(m, c, k, out).start()
            else:
                share_copy(m, c, k, out, recv).start()

    def arrive(m, c):
        @pl.when(sec == 0)
        def _():
            @pl.when(c == 0)
            def _():
                load_a(m).wait()

        @pl.when(sec > 0)
        def _():
            forward_copy(m, c).wait_recv()

    def arrive_back(m, c):
        @pl.when(sec == 3)
        def _():
            @pl.when(c == 0)
            def _():
                load_d(m).wait()

        @pl.when(sec < 3)
        def _():
            backward_copy(m, c).wait_recv()

    def finish_forward(m, c, z):
        rows = rows_of(c)
        mean = jnp.mean(z, axis=1, keepdims=True)
        centred = z - mean
        spread = jnp.mean(centred * centred, axis=1, keepdims=True)
        r = lax.rsqrt(spread + EPS)
        unit = centred * r
        xh[m, rows, :] = unit
        rstd[m, rows, :] = r
        y = (unit * vec_out[:, 0:D] + vec_out[:, D : 2 * D]).astype(bf16)

        @pl.when(sec < 3)
        def _():
            y_buf[m, rows, :] = y
            forward_copy(m, c).start()

        @pl.when(sec == 3)
        def _():
            share(m, c, y, 3, mixed, mix_recv)

    def start_backward(m, c):
        rows = rows_of(c)
        dy = d_buf[m, rows, :].astype(f32)
        unit = xh[m, rows, :]
        dyg = dy * vec_out[:, 0:D]
        m1 = jnp.mean(dyg, axis=1, keepdims=True)
        m2 = jnp.mean(dyg * unit, axis=1, keepdims=True)
        dz = rstd[m, rows, :] * (dyg - m1 - unit * m2)
        du = dz.astype(bf16)

        @pl.when(sec < 3)
        def _():
            forward_copy(m, c).wait_send()

        y_buf[m, rows, :] = du
        acc[0:1, :] += jnp.sum(dy * unit, axis=0, keepdims=True)
        acc[1:2, :] += jnp.sum(dy, axis=0, keepdims=True)
        acc[2:3, :] += jnp.sum(du.astype(f32), axis=0, keepdims=True)
        return dz, du

    def finish_backward(m, c, da):
        rows = rows_of(c)

        @pl.when(sec > 0)
        def _():
            d_buf[m, rows, :] = da
            backward_copy(m, c).start()

        @pl.when(sec == 0)
        def _():
            share(m, c, da, 0, in_grad, grad_recv)

    def attention_tables(m):
        row = seg[m].astype(f32)
        column = jnp.concatenate([jnp.broadcast_to(row, (128, BLK)).T] * 4, axis=1)
        same = column == jnp.broadcast_to(row, (BLK, BLK))
        bias[...] = jnp.where(same, 0.0, NEG)
        index = lax.broadcasted_iota(jnp.int32, (BLK, BLK), 0).astype(f32)
        opener = jnp.min(jnp.where(same, index, float(BLK)), axis=0, keepdims=True)
        place = lax.broadcasted_iota(jnp.int32, (1, BLK), 1).astype(f32) - opener
        number = lax.broadcasted_iota(jnp.int32, (HEAD_DIM // 2, BLK), 0).astype(f32)
        angle = place * jnp.exp(number * (-2.0 * math.log(10000.0) / HEAD_DIM))
        rope[m, 0] = jnp.cos(angle)
        rope[m, 1] = jnp.sin(angle)

    def project(m, c):
        arrive(m, c)
        rows = rows_of(c)
        a = a_buf[m, rows, :]
        co, si = rope[m, 0, :, rows], rope[m, 1, :, rows]
        for part in range(3):
            p = dot(wi[:, D * part : D * (part + 1)], a, TT)
            b = bias_t[D * part : D * (part + 1), :]
            p = p + jnp.concatenate([b, b], axis=1)
            if part < 2:
                p4 = p.reshape(HEADS, 2, 32, CH)
                t1, t2 = p4[:, 0], p4[:, 1]
                r1 = t1 * co[None] - t2 * si[None]
                r2 = t2 * co[None] + t1 * si[None]
                if part == 0:
                    r1, r2 = r1 * 0.125, r2 * 0.125
                p = jnp.concatenate([r1[:, None], r2[:, None]], axis=1).reshape(D, CH)
            p = p.astype(bf16)
            for j in range(3):
                q_buf[m, (3 * part + j) * 2 + c] = p[256 * j : 256 * (j + 1), :]

    def both(buf, m, block, rows):
        return jnp.concatenate([buf[m, block * 2, rows, :], buf[m, block * 2 + 1, rows, :]], axis=1)

    def head_forward(m, g, hh):
        h = g * 4 + hh
        rows = slice(64 * hh, 64 * (hh + 1))
        st = dot(both(q_buf, m, 3 + g, rows), both(q_buf, m, g, rows), TN) + bias[...]
        peak = jnp.max(st, axis=0, keepdims=True)
        e = jnp.exp(st - peak)
        total = jnp.sum(e, axis=0, keepdims=True)
        eb = e.astype(bf16)
        e_buf[m, h * 2] = eb[:, 0:256]
        e_buf[m, h * 2 + 1] = eb[:, 256:512]
        r = 1.0 / total
        inv[m, h] = jnp.broadcast_to(r, (8, BLK))
        o = (dot(both(q_buf, m, 6 + g, rows), eb, NN) * r).astype(bf16)
        q_buf[m, (9 + g) * 2, rows, :] = o[:, 0:256]
        q_buf[m, (9 + g) * 2 + 1, rows, :] = o[:, 256:512]

    def heads_forward(m, g):
        for hh in range(4):
            head_forward(m, g, hh)

    def attended(m, c):
        return jnp.concatenate([q_buf[m, (9 + j) * 2 + c] for j in range(3)], axis=0)

    def close(m, c):
        rows = rows_of(c)
        u = dot(attended(m, c), wi[:, 3 * D :], TN) + vec_out[:, 2 * D :]
        finish_forward(m, c, u + a_buf[m, rows, :].astype(f32))

    def attention_forward(m):
        attention_tables(m)

        @pl.when(m == 0)
        def _():
            for i in range(3):
                b = jnp.broadcast_to(vec_in[:, D * i : D * (i + 1)], (128, D))
                bias_t[D * i : D * (i + 1), :] = b.T
            load_wi.wait()

        lax.fori_loop(0, 2, lambda c, _: (project(m, c), 0)[1], 0)
        lax.fori_loop(0, 3, lambda g, _: (heads_forward(m, g), 0)[1], 0)
        lax.fori_loop(0, 2, lambda c, _: (close(m, c), 0)[1], 0)

    def open_back(m, c):
        arrive_back(m, c)
        rows = rows_of(c)
        dz, du = start_backward(m, c)
        xh[m, rows, :] = dz
        do = dot(wi[:, 3 * D :], du, NT).astype(bf16)
        for j in range(3):
            p_buf[m, (9 + j) * 2 + c] = do[256 * j : 256 * (j + 1), :]

    def head_backward(m, g, hh):
        h = g * 4 + hh
        rows = slice(64 * hh, 64 * (hh + 1))
        do = (both(p_buf, m, 9 + g, rows).astype(f32) * inv[m, h, 0:1, :]).astype(bf16)
        o = both(q_buf, m, 9 + g, rows)
        inner = jnp.sum(do.astype(f32) * o.astype(f32), axis=0, keepdims=True)
        e = jnp.concatenate([e_buf[m, h * 2], e_buf[m, h * 2 + 1]], axis=1)
        dr = dot(both(q_buf, m, 6 + g, rows), do, TN)
        ds = e * (dr - inner).astype(bf16)
        dq = dot(both(q_buf, m, 3 + g, rows), ds, NN)
        dk = dot(both(q_buf, m, g, rows), ds, NT)
        dvv = dot(do, e, NT)
        co, si = rope[m, 0], rope[m, 1]
        for part, t in ((0, dq * 0.125), (1, dk)):
            t1, t2 = t[:32], t[32:]
            t = jnp.concatenate([t1 * co + t2 * si, t2 * co - t1 * si], axis=0).astype(bf16)
            p_buf[m, (3 * part + g) * 2, rows, :] = t[:, 0:256]
            p_buf[m, (3 * part + g) * 2 + 1, rows, :] = t[:, 256:512]
        dvv = dvv.astype(bf16)
        p_buf[m, (6 + g) * 2, rows, :] = dvv[:, 0:256]
        p_buf[m, (6 + g) * 2 + 1, rows, :] = dvv[:, 256:512]

    def heads_backward(m, g):
        for hh in range(4):
            head_backward(m, g, hh)

    def close_back(m, c):
        rows = rows_of(c)
        dp_t = jnp.concatenate([p_buf[m, fb * 2 + c] for fb in range(9)], axis=0)
        da = dot(dp_t, wi[:, 0 : 3 * D], TT) + xh[m, rows, :]
        finish_backward(m, c, da.astype(bf16))

    def attention_weights(m):
        a_t = a_buf[m].T

        def part(n, _):
            cols = pl.ds(pl.multiple_of(n * D, D), D)
            d = jnp.concatenate(
                [jnp.concatenate([p_buf[m, (3 * n + j) * 2], p_buf[m, (3 * n + j) * 2 + 1]], axis=1) for j in range(3)],
                axis=0,
            )
            dw[:, cols] = (dw[:, cols].astype(f32) + dot(a_t, d, NT)).astype(bf16)
            db[:, cols] += dot(jnp.ones((8, BLK), bf16), d, NT)
            return 0

        lax.fori_loop(0, 3, part, 0)
        o = jnp.concatenate([attended(m, 0), attended(m, 1)], axis=1)
        dw[:, 3 * D :] = (dw[:, 3 * D :].astype(f32) + dot(o, y_buf[m], NN)).astype(bf16)

    def feed_rows(m, c):
        arrive(m, c)
        rows = rows_of(c)
        a = a_buf[m, rows, :]
        u = None
        for n in range(4):
            cols = slice(D * n, D * (n + 1))
            h = dot(a, wi[:, cols], NN) + vec_in[:, cols]
            h2 = h * h
            s = 0.5 * jnp.tanh(h * (K0 + K1 * h2)) + 0.5
            g = h * s
            slope = (s + g * (1.0 - s) * (2.0 * K0 + 6.0 * K1 * h2)).astype(bf16)
            g = g.astype(bf16)
            for j in range(3):
                q_buf[m, c * 12 + 3 * n + j] = g[:, 256 * j : 256 * (j + 1)]
                e_buf[m, 3 * n + j, rows, :] = slope[:, 256 * j : 256 * (j + 1)]
            t = dot(g, wd[cols, :], NN)
            u = t if u is None else u + t
        finish_forward(m, c, u + vec_out[:, 2 * D :] + a.astype(f32))

    def feed_forward(m):
        @pl.when(m == 0)
        def _():
            load_wi.wait()
            load_wd.wait()

        lax.fori_loop(0, 2, lambda c, _: (feed_rows(m, c), 0)[1], 0)

    def feed_rows_back(m, c):
        arrive_back(m, c)
        rows = rows_of(c)
        dz, du = start_backward(m, c)
        da = dz
        for n in range(4):
            cols = slice(D * n, D * (n + 1))
            dg = dot(du, wd[cols, :], NT)
            slope = jnp.concatenate([e_buf[m, 3 * n + j, rows, :] for j in range(3)], axis=1)
            dh = (dg * slope.astype(f32)).astype(bf16)
            for j in range(3):
                p_buf[m, c * 12 + 3 * n + j] = dh[:, 256 * j : 256 * (j + 1)]
            da = da + dot(dh, wi[:, cols], NT)
        finish_backward(m, c, da.astype(bf16))

    def tile(buf, m, n):
        return jnp.concatenate(
            [jnp.concatenate([buf[m, c * 12 + 3 * n + j] for j in range(3)], axis=1) for c in range(2)], axis=0
        )

    def feed_weights_down(m):
        def part(n, _):
            rows = pl.ds(pl.multiple_of(n * D, D), D)
            dv[rows, :] = (dv[rows, :].astype(f32) + dot(tile(q_buf, m, n), y_buf[m], TN)).astype(bf16)
            return 0

        lax.fori_loop(0, 4, part, 0)

    def feed_weights_in(m):
        def part(n, _):
            cols = pl.ds(pl.multiple_of(n * D, D), D)
            dh = tile(p_buf, m, n)
            dw[:, cols] = (dw[:, cols].astype(f32) + dot(a_buf[m], dh, TN)).astype(bf16)
            db[:, cols] += jnp.broadcast_to(jnp.sum(dh.astype(f32), axis=0, keepdims=True), (8, D))
            return 0

        lax.fori_loop(0, 4, part, 0)

    def part_copy(grad, land, size, number, first, width, order, step, k, j):
        slot = FIRST_SLOT[step] + k
        return pltpu.make_async_remote_copy(
            src_ref=grad.at[pl.ds(pl.multiple_of(j * size, size), size), pl.ds(first, width)],
            dst_ref=land.at[pl.ds(slot * size, size), pl.ds(first, width)],
            send_sem=rs_send.at[number, slot],
            recv_sem=rs_recv.at[number, slot],
            device_id={"dp": peer(order[step])},
            device_id_type=MESH,
        )

    def step_copies(grad, land, size, number, part, step):
        first, width, order = part
        return [
            part_copy(grad, land, size, number, first, width, order, step, k, j)
            for k, j in enumerate(chunks(me, order, step, True))
        ]

    def send_step(*args):
        for copy in step_copies(*args):
            copy.start()

    def take_step(grad, land, size, number, part, step):
        first, width, order = part
        cols = pl.ds(first, width)
        copies = step_copies(grad, land, size, number, part, step)
        for k, j in enumerate(chunks(me, order, step, False)):
            copies[k].wait_recv()
            slot = FIRST_SLOT[step] + k
            rows = pl.ds(pl.multiple_of(j * size, size), size)
            total = grad[rows, cols].astype(f32) + land[slot * size : (slot + 1) * size, cols].astype(f32)
            if step < 2:
                grad[rows, cols] = total.astype(bf16)
        return total

    def wait_sends(grad, land, size, number, part):
        for step in range(3):
            for copy in step_copies(grad, land, size, number, part, step):
                copy.wait_send()

    down_parts = [(dv, wd, 384, i, part) for i, part in enumerate(PARTS_DOWN)]
    in_parts = [(dw, wi, 96, len(PARTS_DOWN) + i, part) for i, part in enumerate(PARTS_IN)]

    def weights_free():
        for b in range(3):
            pl.semaphore_signal(free_sem.at[b], inc=1, device_id={"dp": peer(b)}, device_id_type=MESH)

    def await_free():
        for b in range(3):
            pl.semaphore_wait(free_sem.at[b], 1)

    def attention_backward(m):
        lax.fori_loop(0, 2, lambda c, _: (open_back(m, c), 0)[1], 0)
        lax.fori_loop(0, 3, lambda g, _: (heads_backward(m, g), 0)[1], 0)
        lax.fori_loop(0, 2, lambda c, _: (close_back(m, c), 0)[1], 0)

        @pl.when(m == MICRO - 1)
        def _():
            weights_free()

        attention_weights(m)

    def feed_backward(m):
        lax.fori_loop(0, 2, lambda c, _: (feed_rows_back(m, c), 0)[1], 0)

        @pl.when(m == MICRO - 1)
        def _():
            weights_free()

        begin = jnp.where(sec == 3, 0, m)
        end = jnp.where((sec == 3) & (m == 0), 0, m + 1)
        lax.fori_loop(begin, end, lambda i, _: (feed_weights_down(i), 0)[1], 0)

        @pl.when(m == MICRO - 1)
        def _():
            await_free()
            for p in down_parts:
                send_step(*p, 0)

        lax.fori_loop(begin, end, lambda i, _: (feed_weights_in(i), 0)[1], 0)

    pl.semaphore_wait(barrier, 3 + GROUP - 1)

    def task(t, _):
        forward = jnp.where(sec == 3, t % 2 == 0, t < 2)
        m = jnp.where(sec == 3, t // 2, t % 2)

        @pl.when(forward & even)
        def _():
            attention_forward(m)

        @pl.when(forward & odd)
        def _():
            feed_forward(m)

        @pl.when(jnp.logical_not(forward) & even)
        def _():
            attention_backward(m)

        @pl.when(jnp.logical_not(forward) & odd)
        def _():
            feed_backward(m)

        return 0

    lax.fori_loop(0, 2 * MICRO, task, 0)

    @pl.when(even)
    def _():
        await_free()

    for p in in_parts:
        send_step(*p, 0)

    vec_send[...] = jnp.zeros_like(vec_send)
    outer = jnp.concatenate([acc[0:1, :], acc[1:2, :], acc[2:3, :]], axis=1)
    for j in range(GROUP):
        vec_send[j, 0:1, :] = db[0:1, 384 * j : 384 * (j + 1)]
        vec_send[j, 1:2, 0:288] = outer[:, 288 * j : 288 * (j + 1)]

    def vec_copy(k):
        there = (me + k) % GROUP
        return pltpu.make_async_remote_copy(
            src_ref=vec_send.at[there],
            dst_ref=vec_recv.at[k],
            send_sem=vec_ssem.at[k],
            recv_sem=vec_rsem.at[k],
            device_id={"dp": there * low + dp % low},
            device_id_type=MESH,
        )

    for k in range(1, GROUP):
        vec_copy(k).start()

    for step in range(3):

        @pl.when(odd)
        def _():
            for p in down_parts:
                total = take_step(*p, step)
                if step < 2:
                    send_step(*p, step + 1)
                else:
                    first, width, _ = p[4]
                    xh[1, 0:384, first : first + width] = total

        for p in in_parts:
            total = take_step(*p, step)
            if step < 2:
                send_step(*p, step + 1)
            else:
                first, width, _ = p[4]
                for i in range(width // D):
                    xh[0, 96 * (first // D + i) : 96 * (first // D + i + 1), :] = total[:, D * i : D * (i + 1)]

    @pl.when(even)
    def _():
        xh[1, 0:384, :] = jnp.zeros((384, D), f32)

    outs = [pltpu.make_async_copy(xh.at[1, pl.ds(0, 384)], out_down, out_sem.at[4])]
    for i in range(4):
        outs.append(
            pltpu.make_async_copy(xh.at[0, pl.ds(96 * i, 96)], out_in.at[:, pl.ds(D * i, D)], out_sem.at[i])
        )
    for copy in outs:
        copy.start()
    total = vec_send[me]
    for k in range(1, GROUP):
        vec_copy(k).wait_recv()
        total = total + vec_recv[k]
    out_vec[...] = total

    for k in range(1, GROUP):
        vec_copy(k).wait_send()
    for p in in_parts:
        wait_sends(*p)

    @pl.when(odd)
    def _():
        for p in down_parts:
            wait_sends(*p)

    for m in range(MICRO):
        for c in range(2):

            @pl.when(sec > 0)
            def _():
                backward_copy(m, c).wait_send()
                share_copy(m, c, 0, in_grad, grad_recv).wait_recv()

            @pl.when(sec < 3)
            def _():
                share_copy(m, c, 0, mixed, mix_recv).wait_recv()

            @pl.when(sec == 0)
            def _():
                own_copy(m, c, 0, in_grad).wait()
                for k in range(1, 4):
                    share_copy(m, c, k, in_grad, grad_recv).wait_send()

            @pl.when(sec == 3)
            def _():
                own_copy(m, c, 3, mixed).wait()
                for k in range(3):
                    share_copy(m, c, k, mixed, mix_recv).wait_send()

    for copy in outs:
        copy.wait()


def on_device(inputs, segment_ids, w_in, w_down, vec_in, vec_out, cotangent):
    world = lax.axis_size("dp")
    low = world // GROUP
    hbm = pl.BlockSpec(memory_space=pl.ANY)
    vmem = pl.BlockSpec(memory_space=pltpu.VMEM)
    V, S = pltpu.VMEM, pltpu.SemaphoreType.DMA
    parts = len(PARTS_IN) + len(PARTS_DOWN)
    mixed, in_grad, grad_in, grad_down, grad_vec = pl.pallas_call(
        functools.partial(kernel, low),
        out_shape=(
            jax.ShapeDtypeStruct((MICRO, BLK, D // 4), bf16),
            jax.ShapeDtypeStruct((MICRO, BLK, D // 4), bf16),
            jax.ShapeDtypeStruct((D // GROUP, FF), f32),
            jax.ShapeDtypeStruct((FF // GROUP, D), f32),
            jax.ShapeDtypeStruct((8, 384), f32),
        ),
        in_specs=[hbm, vmem, hbm, hbm, vmem, vmem, hbm],
        out_specs=(hbm, hbm, hbm, hbm, vmem),
        scratch_shapes=[
            V((D, FF), bf16),
            V((FF, D), bf16),
            V((MICRO, BLK, D), bf16),
            V((MICRO, BLK, D), bf16),
            V((MICRO, BLK, D), bf16),
            V((MICRO, 24, 512, 256), bf16),
            V((MICRO, 24, 256, 256), bf16),
            V((MICRO, 24, 256, 256), bf16),
            V((MICRO, BLK, D), f32),
            V((MICRO, BLK, 1), f32),
            V((BLK, BLK), f32),
            V((MICRO, 2, HEAD_DIM // 2, BLK), f32),
            V((MICRO, HEADS, 8, BLK), f32),
            V((3 * D, 128), f32),
            V((D, FF), bf16),
            V((FF, D), bf16),
            V((4, MICRO, BLK, D // 4), bf16),
            V((8, D), f32),
            V((8, FF), f32),
            V((GROUP, 8, 384), f32),
            V((GROUP, 8, 384), f32),
            S((2,)),
            S((MICRO,)),
            S((MICRO, 2)),
            S((MICRO, 2)),
            S((MICRO, 2)),
            S((MICRO, 2)),
            S((4, MICRO, 2)),
            S((MICRO, 2)),
            S((MICRO, 2)),
            S((GROUP,)),
            S((GROUP,)),
            pltpu.SemaphoreType.REGULAR((3,)),
            S((parts, 7)),
            S((parts, 7)),
            S((5,)),
        ],
        compiler_params=pltpu.CompilerParams(
            collective_id=0, has_side_effects=True, vmem_limit_bytes=63 * MIB
        ),
    )(inputs, segment_ids[:, None, :], w_in, w_down, vec_in, vec_out, cotangent)
    vec_a, vec_b = grad_vec[0], grad_vec[1, :288]
    if low > 1:
        groups = [[g * low + i for i in range(low)] for g in range(GROUP)]

        def rest(value):
            return lax.psum_scatter(
                value, "dp", scatter_dimension=0, axis_index_groups=groups, tiled=True
            )

        grad_in, grad_down, vec_a, vec_b = rest(grad_in), rest(grad_down), rest(vec_a), rest(vec_b)
    return mixed, in_grad, grad_in[None], grad_down[None], vec_a[None], vec_b[None]


def solution(mesh):
    placed = (
        P(None, "dp", None),
        P(None, "dp"),
        P("section", None, None),
        P("section", None, None),
        P("section", None),
        P("section", None),
        P(None, "dp", None),
    )
    return jax.shard_map(
        on_device,
        mesh=mesh,
        in_specs=placed,
        out_specs=(
            P(None, "dp", "section"),
            P(None, "dp", "section"),
            P("section", "dp", None),
            P("section", "dp", None),
            P("section", "dp"),
            P("section", "dp"),
        ),
        check_vma=False,
    )
```

```python
import functools
import math

import jax
import jax.numpy as jnp
from jax import lax
from jax.experimental import pallas as pl
from jax.experimental.pallas import tpu as pltpu
from jax.sharding import PartitionSpec as P

D = 768
HEADS = 12
HEAD_DIM = 64
FF = 3072
BLK = 512
MICRO = 2
CH = 256
GROUP = 8
EPS = 1e-06
NEG = -1e30
K0 = math.sqrt(2.0 / math.pi)
K1 = K0 * 0.044715
MIB = 1 << 20
bf16, f32 = jnp.bfloat16, jnp.float32
MESH = pl.DeviceIdType.MESH
NN = (((1,), (0,)), ((), ()))
NT = (((1,), (1,)), ((), ()))
TN = (((0,), (0,)), ((), ()))
TT = (((0,), (1,)), ((), ()))
ORDER_A, ORDER_B = (0, 1, 2), (1, 0, 2)
DOWN_PARTS = [(True, 128 * i, 128, ORDER_A if i % 3 else ORDER_B) for i in range(6)]
IN_PARTS = [(False, 256 * i, 256, ORDER_A if i % 3 else ORDER_B) for i in range(12)]


def dot(a, b, dims):
    return lax.dot_general(a, b, dims, preferred_element_type=f32)


def bit(value, b):
    return (value // (1 << b)) % 2


def chunks(me, order, step, flip):
    base = sum(bit(me, order[i]) * (1 << order[i]) for i in range(step))
    own = bit(me, order[step])
    base = base + ((1 - own) if flip else own) * (1 << order[step])
    free = order[step + 1 :]
    out = []
    for k in range(1 << len(free)):
        out.append(base + sum(((k >> i) & 1) << free[i] for i in range(len(free))))
    return out


FIRST_SLOT = (0, 4, 6)
PARTS = DOWN_PARTS + IN_PARTS
DOWN = list(range(len(DOWN_PARTS)))
IN = list(range(len(DOWN_PARTS), len(PARTS)))


def kernel(
    low,
    inputs,
    seg,
    w_in,
    w_down,
    vec_in,
    vec_out,
    cotangent,
    mixed,
    in_grad,
    out_in,
    out_down,
    out_vec_in,
    out_vec_out,
    wi,
    wd,
    a_buf,
    d_buf,
    y_buf,
    e_buf,
    q_buf,
    p_buf,
    xh,
    rstd,
    bias,
    rope,
    inv,
    bias_t,
    dw,
    dv,
    split,
    acc,
    db,
    vec_send,
    vec_recv,
    w_sem,
    load_sem,
    fwd_send,
    fwd_recv,
    bwd_send,
    bwd_recv,
    mix_send,
    mix_recv,
    grad_recv,
    vec_ssem,
    vec_rsem,
    free_sem,
    rs_send,
    rs_recv,
    out_sem,
):
    sec = lax.axis_index("section")
    dp = lax.axis_index("dp")
    me = dp // low
    even = sec % 2 == 0
    odd = sec % 2 == 1

    def peer(b):
        return dp + (1 - 2 * bit(me, b)) * (1 << b) * low

    load_wi = pltpu.make_async_copy(w_in.at[0], wi, w_sem.at[0])
    load_wd = pltpu.make_async_copy(w_down.at[0], wd, w_sem.at[1])

    def load_a(m):
        return pltpu.make_async_copy(inputs.at[m], a_buf.at[m], load_sem.at[m])

    def load_d(m):
        return pltpu.make_async_copy(cotangent.at[m], d_buf.at[m], load_sem.at[m])

    @pl.when(sec == 0)
    def _():
        for m in range(MICRO):
            load_a(m).start()

    load_wi.start()

    @pl.when(odd)
    def _():
        load_wd.start()

    @pl.when(sec == 3)
    def _():
        for m in range(MICRO):
            load_d(m).start()

    barrier = pltpu.get_barrier_semaphore()
    for k in range(1, 4):
        pl.semaphore_signal(barrier, inc=1, device_id={"section": (sec + k) % 4}, device_id_type=MESH)
    for k in range(1, GROUP):
        pl.semaphore_signal(barrier, inc=1, device_id={"dp": (dp + k * low) % (GROUP * low)}, device_id_type=MESH)

    acc[...] = jnp.zeros_like(acc)
    db[...] = jnp.zeros_like(db)

    def rows_of(c):
        return pl.ds(pl.multiple_of(c * CH, CH), CH)

    def forward_copy(m, c):
        rows = rows_of(c)
        return pltpu.make_async_remote_copy(
            src_ref=y_buf.at[m, rows],
            dst_ref=a_buf.at[m, rows],
            send_sem=fwd_send.at[m, c],
            recv_sem=fwd_recv.at[m, c],
            device_id={"section": sec + 1},
            device_id_type=MESH,
        )

    def backward_copy(m, c):
        rows = rows_of(c)
        return pltpu.make_async_remote_copy(
            src_ref=d_buf.at[m, rows],
            dst_ref=d_buf.at[m, rows],
            send_sem=bwd_send.at[m, c],
            recv_sem=bwd_recv.at[m, c],
            device_id={"section": sec - 1},
            device_id_type=MESH,
        )

    def share_copy(m, c, k, out, recv):
        cols = rows_of(c)
        return pltpu.make_async_remote_copy(
            src_ref=split.at[k, m, :, cols],
            dst_ref=out.at[m, :, cols],
            send_sem=mix_send.at[k, m, c],
            recv_sem=recv.at[m, c],
            device_id={"section": k},
            device_id_type=MESH,
        )

    def own_copy(m, c, k, out):
        cols = rows_of(c)
        return pltpu.make_async_copy(split.at[k, m, :, cols], out.at[m, :, cols], mix_send.at[k, m, c])

    def share(m, c, value, own, out, recv):
        flipped = value.T
        for k in range(4):
            split[k, m, :, rows_of(c)] = flipped[192 * k : 192 * (k + 1), :]
        for k in range(4):
            if k == own:
                own_copy(m, c, k, out).start()
            else:
                share_copy(m, c, k, out, recv).start()

    def arrive(m, c):
        @pl.when(sec == 0)
        def _():
            @pl.when(c == 0)
            def _():
                load_a(m).wait()

        @pl.when(sec > 0)
        def _():
            forward_copy(m, c).wait_recv()

    def arrive_back(m, c):
        @pl.when(sec == 3)
        def _():
            @pl.when(c == 0)
            def _():
                load_d(m).wait()

        @pl.when(sec < 3)
        def _():
            backward_copy(m, c).wait_recv()

    def finish_forward(m, c, z):
        rows = rows_of(c)
        mean = jnp.mean(z, axis=1, keepdims=True)
        centred = z - mean
        spread = jnp.mean(centred * centred, axis=1, keepdims=True)
        r = lax.rsqrt(spread + EPS)
        unit = centred * r
        xh[m, rows, :] = unit
        rstd[m, rows, :] = r
        y = (unit * vec_out[:, 0:D] + vec_out[:, D : 2 * D]).astype(bf16)

        @pl.when(sec < 3)
        def _():
            y_buf[m, rows, :] = y
            forward_copy(m, c).start()

        @pl.when(sec == 3)
        def _():
            share(m, c, y, 3, mixed, mix_recv)

    def start_backward(m, c):
        rows = rows_of(c)
        dy = d_buf[m, rows, :].astype(f32)
        unit = xh[m, rows, :]
        dyg = dy * vec_out[:, 0:D]
        m1 = jnp.mean(dyg, axis=1, keepdims=True)
        m2 = jnp.mean(dyg * unit, axis=1, keepdims=True)
        dz = rstd[m, rows, :] * (dyg - m1 - unit * m2)
        du = dz.astype(bf16)

        @pl.when(sec < 3)
        def _():
            forward_copy(m, c).wait_send()

        y_buf[m, rows, :] = du
        acc[0:1, :] += jnp.sum(dy * unit, axis=0, keepdims=True)
        acc[1:2, :] += jnp.sum(dy, axis=0, keepdims=True)
        acc[2:3, :] += jnp.sum(du.astype(f32), axis=0, keepdims=True)
        xh[m, rows, :] = dz
        return du

    def finish_backward(m, c, da):
        rows = rows_of(c)

        @pl.when(sec > 0)
        def _():
            d_buf[m, rows, :] = da
            backward_copy(m, c).start()

        @pl.when(sec == 0)
        def _():
            share(m, c, da, 0, in_grad, grad_recv)

    def attention_tables(m):
        row = seg[pl.ds(m, 1), :].astype(f32)
        column = jnp.concatenate([jnp.broadcast_to(row, (128, BLK)).T] * 4, axis=1)
        same = column == jnp.broadcast_to(row, (BLK, BLK))
        bias[...] = jnp.where(same, 0.0, NEG)
        index = lax.broadcasted_iota(jnp.int32, (BLK, BLK), 0).astype(f32)
        opener = jnp.min(jnp.where(same, index, float(BLK)), axis=0, keepdims=True)
        place = lax.broadcasted_iota(jnp.int32, (1, BLK), 1).astype(f32) - opener
        number = lax.broadcasted_iota(jnp.int32, (HEAD_DIM // 2, BLK), 0).astype(f32)
        angle = place * jnp.exp(number * (-2.0 * math.log(10000.0) / HEAD_DIM))
        rope[m, 0] = jnp.cos(angle)
        rope[m, 1] = jnp.sin(angle)

    def project(m, c):
        arrive(m, c)
        rows = rows_of(c)
        a = a_buf[m, rows, :]
        co, si = rope[m, 0, :, rows], rope[m, 1, :, rows]
        for part in range(3):
            p = dot(wi[:, D * part : D * (part + 1)], a, TT)
            b = bias_t[D * part : D * (part + 1), :]
            p = p + jnp.concatenate([b, b], axis=1)
            if part < 2:
                p4 = p.reshape(HEADS, 2, 32, CH)
                t1, t2 = p4[:, 0], p4[:, 1]
                r1 = t1 * co[None] - t2 * si[None]
                r2 = t2 * co[None] + t1 * si[None]
                if part == 0:
                    r1, r2 = r1 * 0.125, r2 * 0.125
                p = jnp.concatenate([r1[:, None], r2[:, None]], axis=1).reshape(D, CH)
            p = p.astype(bf16)
            for j in range(3):
                q_buf[m, (3 * part + j) * 2 + c] = p[256 * j : 256 * (j + 1), :]

    def both(buf, m, block, rows):
        return jnp.concatenate([buf[m, block * 2, rows, :], buf[m, block * 2 + 1, rows, :]], axis=1)

    def heads_forward(m):
        scores, weights = {}, {}
        for t in range(HEADS + 2):
            if t < HEADS:
                g, rows = t // 4, slice(64 * (t % 4), 64 * (t % 4) + 64)
                scores[t] = dot(both(q_buf, m, 3 + g, rows), both(q_buf, m, g, rows), TN) + bias[...]
            h = t - 1
            if 0 <= h < HEADS:
                st = scores.pop(h)
                peak = jnp.max(st, axis=0, keepdims=True)
                e = jnp.exp(st - peak)
                r = 1.0 / jnp.sum(e, axis=0, keepdims=True)
                e = e.astype(bf16)
                e_buf[m, h * 2] = e[:, 0:256]
                e_buf[m, h * 2 + 1] = e[:, 256:512]
                inv[m, h] = jnp.broadcast_to(r, (8, BLK))
                weights[h] = (e, r)
            h = t - 2
            if 0 <= h:
                e, r = weights.pop(h)
                g, rows = h // 4, slice(64 * (h % 4), 64 * (h % 4) + 64)
                o = (dot(both(q_buf, m, 6 + g, rows), e, NN) * r).astype(bf16)
                q_buf[m, (9 + g) * 2, rows, :] = o[:, 0:256]
                q_buf[m, (9 + g) * 2 + 1, rows, :] = o[:, 256:512]

    def attended(m, c):
        return jnp.concatenate([q_buf[m, (9 + j) * 2 + c] for j in range(3)], axis=0)

    def close(m, c):
        rows = rows_of(c)
        u = dot(attended(m, c), wi[:, 3 * D :], TN) + vec_out[:, 2 * D :]
        finish_forward(m, c, u + a_buf[m, rows, :].astype(f32))

    def attention_forward(m):
        @pl.when(m == 0)
        def _():
            load_wi.wait()

        @pl.when(m > 0)
        def _():
            attention_tables(m)

        lax.fori_loop(0, 2, lambda c, _: (project(m, c), 0)[1], 0)
        heads_forward(m)
        lax.fori_loop(0, 2, lambda c, _: (close(m, c), 0)[1], 0)

    def open_back(m, c):
        arrive_back(m, c)
        rows = rows_of(c)
        du = start_backward(m, c)
        do = dot(wi[:, 3 * D :], du, NT).astype(bf16)
        for j in range(3):
            p_buf[m, (9 + j) * 2 + c] = do[256 * j : 256 * (j + 1), :]

    def heads_backward(m):
        co, si = rope[m, 0], rope[m, 1]
        pending = {}
        for t in range(HEADS + 1):
            if t < HEADS:
                g, rows = t // 4, slice(64 * (t % 4), 64 * (t % 4) + 64)
                do = (both(p_buf, m, 9 + g, rows).astype(f32) * inv[m, t, 0:1, :]).astype(bf16)
                o = both(q_buf, m, 9 + g, rows)
                inner = jnp.sum(do.astype(f32) * o.astype(f32), axis=0, keepdims=True)
                pending[t] = (do, inner, dot(both(q_buf, m, 6 + g, rows), do, TN))
            h = t - 1
            if 0 <= h:
                g, rows = h // 4, slice(64 * (h % 4), 64 * (h % 4) + 64)
                do, inner, dr = pending.pop(h)
                e = jnp.concatenate([e_buf[m, h * 2], e_buf[m, h * 2 + 1]], axis=1)
                ds = e * (dr - inner).astype(bf16)
                dvv = dot(do, e, NT)
                dq = dot(both(q_buf, m, 3 + g, rows), ds, NN)
                dk = dot(both(q_buf, m, g, rows), ds, NT)
                for part, x in ((0, dq * 0.125), (1, dk)):
                    t1, t2 = x[:32], x[32:]
                    x = jnp.concatenate([t1 * co + t2 * si, t2 * co - t1 * si], axis=0).astype(bf16)
                    p_buf[m, (3 * part + g) * 2, rows, :] = x[:, 0:256]
                    p_buf[m, (3 * part + g) * 2 + 1, rows, :] = x[:, 256:512]
                dvv = dvv.astype(bf16)
                p_buf[m, (6 + g) * 2, rows, :] = dvv[:, 0:256]
                p_buf[m, (6 + g) * 2 + 1, rows, :] = dvv[:, 256:512]

    def close_back(m, c):
        rows = rows_of(c)
        dp_t = jnp.concatenate([p_buf[m, fb * 2 + c] for fb in range(9)], axis=0)
        da = dot(dp_t, wi[:, 0 : 3 * D], TT) + xh[m, rows, :]
        finish_backward(m, c, da.astype(bf16))

    def add(m, held, new):
        return jnp.where(m == 0, new, held.astype(f32) + new).astype(bf16)

    def attention_weights(m):
        a_t = a_buf[m].T

        def part(n, _):
            cols = pl.ds(pl.multiple_of(n * D, D), D)
            d = jnp.concatenate(
                [jnp.concatenate([p_buf[m, (3 * n + j) * 2], p_buf[m, (3 * n + j) * 2 + 1]], axis=1) for j in range(3)],
                axis=0,
            )
            dw[:, cols] = add(m, dw[:, cols], dot(a_t, d, NT))
            db[:, cols] += dot(jnp.ones((8, BLK), bf16), d, NT)
            return 0

        lax.fori_loop(0, 3, part, 0)
        o = jnp.concatenate([attended(m, 0), attended(m, 1)], axis=1)
        dw[:, 3 * D :] = add(m, dw[:, 3 * D :], dot(o, y_buf[m], NN))

    def feed_rows(m, c):
        arrive(m, c)
        rows = rows_of(c)
        a = a_buf[m, rows, :]
        u, hidden = None, {}
        for t in range(8):
            if t < 6:
                cols = slice(512 * t, 512 * (t + 1))
                hidden[t] = dot(a, wi[:, cols], NN) + vec_in[:, cols]
            n = t - 2
            if n >= 0:
                h = hidden.pop(n)
                h2 = h * h
                s = 0.5 * jnp.tanh(h * (K0 + K1 * h2)) + 0.5
                g = h * s
                slope = (s + g * (1.0 - s) * (2.0 * K0 + 6.0 * K1 * h2)).astype(bf16)
                g = g.astype(bf16)
                for j in range(2):
                    q_buf[m, c * 12 + 2 * n + j] = g[:, 256 * j : 256 * (j + 1)]
                    e_buf[m, 2 * n + j, rows, :] = slope[:, 256 * j : 256 * (j + 1)]
                x = dot(g, wd[512 * n : 512 * (n + 1), :], NN)
                u = x if u is None else u + x
        finish_forward(m, c, u + vec_out[:, 2 * D :] + a.astype(f32))

    def feed_forward(m):
        @pl.when(m == 0)
        def _():
            load_wi.wait()
            load_wd.wait()

        lax.fori_loop(0, 2, lambda c, _: (feed_rows(m, c), 0)[1], 0)

    def feed_open_back(m, c):
        arrive_back(m, c)
        start_backward(m, c)

    def feed_rows_back(m, c):
        rows = rows_of(c)
        du = y_buf[m, rows, :]
        da, grads = xh[m, rows, :], {}
        for t in range(5):
            if t < 4:
                grads[t] = dot(du, wd[D * t : D * (t + 1), :], NT)
            n = t - 1
            if n >= 0:
                slope = jnp.concatenate([e_buf[m, 3 * n + j, rows, :] for j in range(3)], axis=1)
                dh = (grads.pop(n) * slope.astype(f32)).astype(bf16)
                for j in range(3):
                    p_buf[m, c * 12 + 3 * n + j] = dh[:, 256 * j : 256 * (j + 1)]
                da = da + dot(dh, wi[:, D * n : D * (n + 1)], NT)
        finish_backward(m, c, da.astype(bf16))

    def tile(buf, m, n):
        return jnp.concatenate(
            [jnp.concatenate([buf[m, c * 12 + 3 * n + j] for j in range(3)], axis=1) for c in range(2)], axis=0
        )

    def feed_weights_down(m):
        def part(n, _):
            rows = pl.ds(pl.multiple_of(n * D, D), D)
            dv[rows, :] = add(m, dv[rows, :], dot(tile(q_buf, m, n), y_buf[m], TN))
            return 0

        lax.fori_loop(0, 4, part, 0)

    def feed_weights_in(m):
        def part(n, _):
            cols = pl.ds(pl.multiple_of(n * D, D), D)
            dh = tile(p_buf, m, n)
            dw[:, cols] = add(m, dw[:, cols], dot(a_buf[m], dh, TN))
            db[:, cols] += jnp.broadcast_to(jnp.sum(dh.astype(f32), axis=0, keepdims=True), (8, D))
            return 0

        lax.fori_loop(0, 4, part, 0)

    def landing(part, number, slot):
        down, first, width, _ = part
        if not down:
            return wi.at[pl.ds(96 * slot, 96), pl.ds(first, width)]
        piece = (number // 2) * 7 + slot
        return e_buf.at[piece // 12, 12 + piece % 12, pl.ds(0, 384), pl.ds(128 * (number % 2), 128)]

    def own_rows(part, j):
        size = 384 if part[0] else 96
        return pl.ds(pl.multiple_of(j * size, size), size), pl.ds(part[1], part[2])

    def step_copies(number, step):
        part = PARTS[number]
        grad = dv if part[0] else dw
        copies = []
        for k, j in enumerate(chunks(me, part[3], step, True)):
            slot = FIRST_SLOT[step] + k
            copies.append(
                pltpu.make_async_remote_copy(
                    src_ref=grad.at[own_rows(part, j)],
                    dst_ref=landing(part, number, slot),
                    send_sem=rs_send.at[number, slot],
                    recv_sem=rs_recv.at[number, slot],
                    device_id={"dp": peer(part[3][step])},
                    device_id_type=MESH,
                )
            )
        return copies

    def send_step(number, step):
        for copy in step_copies(number, step):
            copy.start()

    def take_step(number, step):
        part = PARTS[number]
        grad = dv if part[0] else dw
        copies = step_copies(number, step)
        for k, j in enumerate(chunks(me, part[3], step, False)):
            copies[k].wait_recv()
            index = own_rows(part, j)
            total = grad[index].astype(f32) + landing(part, number, FIRST_SLOT[step] + k)[...].astype(f32)
            if step < 2:
                grad[index] = total.astype(bf16)
        down, first, width, _ = part
        if step < 2:
            send_step(number, step + 1)
        elif down:
            xh[1, 0:384, first : first + width] = total
        else:
            q, off = first // D, first % D
            xh[0, 96 * q : 96 * (q + 1), off : off + width] = total

    def exchange(numbers, ahead, lag, started):
        n = len(numbers)
        for t in range(started, n + ahead + 2 * lag):
            for step in (2, 1, 0):
                i = t - ahead - lag * step
                if 0 <= i < n:
                    take_step(numbers[i], step)
            if t < n:
                send_step(numbers[t], 0)
        for number in numbers:
            for step in range(3):
                for copy in step_copies(number, step):
                    copy.wait_send()

    def weights_free():
        for b in range(3):
            pl.semaphore_signal(free_sem.at[b], inc=1, device_id={"dp": peer(b)}, device_id_type=MESH)

    def await_free():
        for b in range(3):
            pl.semaphore_wait(free_sem.at[b], 1)

    late = sec >= 2

    def span(m):
        return jnp.where(late, 0, m), jnp.where(late & (m == 0), 0, m + 1)

    def attention_backward(m):
        lax.fori_loop(0, 2, lambda c, _: (open_back(m, c), 0)[1], 0)
        heads_backward(m)
        lax.fori_loop(0, 2, lambda c, _: (close_back(m, c), 0)[1], 0)

        @pl.when(m == MICRO - 1)
        def _():
            weights_free()

        lax.fori_loop(*span(m), lambda i, _: (attention_weights(i), 0)[1], 0)

    def feed_backward(m):
        early = (sec == 1) & (m == MICRO - 1)
        begin, end = span(m)

        def down_products(begin, end):
            lax.fori_loop(begin, end, lambda i, _: (feed_weights_down(i), 0)[1], 0)

            @pl.when((begin < end) & (m == MICRO - 1))
            def _():
                for number in DOWN:
                    send_step(number, 0)

        lax.fori_loop(0, 2, lambda c, _: (feed_open_back(m, c), 0)[1], 0)
        down_products(begin, jnp.where(early, end, begin))
        lax.fori_loop(0, 2, lambda c, _: (feed_rows_back(m, c), 0)[1], 0)

        @pl.when(m == MICRO - 1)
        def _():
            weights_free()

        down_products(begin, jnp.where(early, begin, end))
        lax.fori_loop(begin, end, lambda i, _: (feed_weights_in(i), 0)[1], 0)

    @pl.when(even)
    def _():
        attention_tables(0)
        for i in range(3):
            b = jnp.broadcast_to(vec_in[:, D * i : D * (i + 1)], (128, D))
            bias_t[D * i : D * (i + 1), :] = b.T

    pl.semaphore_wait(barrier, 3 + GROUP - 1)

    def task(t, _):
        forward = jnp.where(sec == 3, t % 2 == 0, t < 2)
        m = jnp.where(sec == 3, t // 2, t % 2)

        @pl.when(forward & even)
        def _():
            attention_forward(m)

        @pl.when(forward & odd)
        def _():
            feed_forward(m)

        @pl.when(jnp.logical_not(forward) & even)
        def _():
            attention_backward(m)

        @pl.when(jnp.logical_not(forward) & odd)
        def _():
            feed_backward(m)

        return 0

    lax.fori_loop(0, 2 * MICRO, task, 0)

    await_free()

    vec_send[...] = jnp.zeros_like(vec_send)
    outer = jnp.concatenate([acc[0:1, :], acc[1:2, :], acc[2:3, :]], axis=1)
    for j in range(GROUP):
        vec_send[j, 0:1, :] = db[0:1, 384 * j : 384 * (j + 1)]
        vec_send[j, 1:2, 0:288] = outer[:, 288 * j : 288 * (j + 1)]

    def vec_copy(k):
        there = (me + k) % GROUP
        return pltpu.make_async_remote_copy(
            src_ref=vec_send.at[there],
            dst_ref=vec_recv.at[k],
            send_sem=vec_ssem.at[k],
            recv_sem=vec_rsem.at[k],
            device_id={"dp": there * low + dp % low},
            device_id_type=MESH,
        )

    for k in range(1, GROUP):
        vec_copy(k).start()

    @pl.when(odd)
    def _():
        exchange(DOWN + IN, 6, 6, len(DOWN))

    @pl.when(even)
    def _():
        exchange(IN, 4, 4, 0)

    @pl.when(even)
    def _():
        xh[1, 0:384, :] = jnp.zeros((384, D), f32)

    outs = [pltpu.make_async_copy(xh.at[1, pl.ds(0, 384)], out_down.at[0], out_sem.at[4])]
    for i in range(4):
        outs.append(
            pltpu.make_async_copy(xh.at[0, pl.ds(96 * i, 96)], out_in.at[0, :, pl.ds(D * i, D)], out_sem.at[i])
        )
    for copy in outs:
        copy.start()
    total = vec_send[me]
    for k in range(1, GROUP):
        vec_copy(k).wait_recv()
        total = total + vec_recv[k]
    out_vec_in[...] = total[0:1, :]
    out_vec_out[...] = total[1:2, 0:288]

    for k in range(1, GROUP):
        vec_copy(k).wait_send()

    for m in range(MICRO):
        for c in range(2):

            @pl.when(sec > 0)
            def _():
                backward_copy(m, c).wait_send()
                share_copy(m, c, 0, in_grad, grad_recv).wait_recv()

            @pl.when(sec < 3)
            def _():
                share_copy(m, c, 0, mixed, mix_recv).wait_recv()

            @pl.when(sec == 0)
            def _():
                own_copy(m, c, 0, in_grad).wait()
                for k in range(1, 4):
                    share_copy(m, c, k, in_grad, grad_recv).wait_send()

            @pl.when(sec == 3)
            def _():
                own_copy(m, c, 3, mixed).wait()
                for k in range(3):
                    share_copy(m, c, k, mixed, mix_recv).wait_send()

    for copy in outs:
        copy.wait()


def on_device(inputs, segment_ids, w_in, w_down, vec_in, vec_out, cotangent):
    world = lax.axis_size("dp")
    low = world // GROUP
    hbm = pl.BlockSpec(memory_space=pl.ANY)
    vmem = pl.BlockSpec(memory_space=pltpu.VMEM)
    V, S = pltpu.VMEM, pltpu.SemaphoreType.DMA
    parts = len(PARTS)
    mixed, in_grad, grad_in, grad_down, vec_a, vec_b = pl.pallas_call(
        functools.partial(kernel, low),
        out_shape=(
            jax.ShapeDtypeStruct((MICRO, D // 4, BLK), bf16),
            jax.ShapeDtypeStruct((MICRO, D // 4, BLK), bf16),
            jax.ShapeDtypeStruct((1, D // GROUP, FF), f32),
            jax.ShapeDtypeStruct((1, FF // GROUP, D), f32),
            jax.ShapeDtypeStruct((1, FF // GROUP), f32),
            jax.ShapeDtypeStruct((1, 3 * D // GROUP), f32),
        ),
        in_specs=[hbm, vmem, hbm, hbm, vmem, vmem, hbm],
        out_specs=(hbm, hbm, hbm, hbm, vmem, vmem),
        scratch_shapes=[
            V((D, FF), bf16),
            V((FF, D), bf16),
            V((MICRO, BLK, D), bf16),
            V((MICRO, BLK, D), bf16),
            V((MICRO, BLK, D), bf16),
            V((MICRO, 24, 512, 256), bf16),
            V((MICRO, 24, 256, 256), bf16),
            V((MICRO, 24, 256, 256), bf16),
            V((MICRO, BLK, D), f32),
            V((MICRO, BLK, 1), f32),
            V((BLK, BLK), f32),
            V((MICRO, 2, HEAD_DIM // 2, BLK), f32),
            V((MICRO, HEADS, 8, BLK), f32),
            V((3 * D, 128), f32),
            V((D, FF), bf16),
            V((FF, D), bf16),
            V((4, MICRO, D // 4, BLK), bf16),
            V((8, D), f32),
            V((8, FF), f32),
            V((GROUP, 8, 384), f32),
            V((GROUP, 8, 384), f32),
            S((2,)),
            S((MICRO,)),
            S((MICRO, 2)),
            S((MICRO, 2)),
            S((MICRO, 2)),
            S((MICRO, 2)),
            S((4, MICRO, 2)),
            S((MICRO, 2)),
            S((MICRO, 2)),
            S((GROUP,)),
            S((GROUP,)),
            pltpu.SemaphoreType.REGULAR((3,)),
            S((parts, 7)),
            S((parts, 7)),
            S((5,)),
        ],
        compiler_params=pltpu.CompilerParams(
            collective_id=0, has_side_effects=True, vmem_limit_bytes=63 * MIB
        ),
    )(inputs, segment_ids, w_in, w_down, vec_in, vec_out, cotangent)
    if low > 1:
        groups = [[g * low + i for i in range(low)] for g in range(GROUP)]

        def rest(value):
            return lax.psum_scatter(
                value, "dp", scatter_dimension=1, axis_index_groups=groups, tiled=True
            )

        grad_in, grad_down, vec_a, vec_b = rest(grad_in), rest(grad_down), rest(vec_a), rest(vec_b)
    mixed, in_grad = jnp.swapaxes(mixed, 1, 2), jnp.swapaxes(in_grad, 1, 2)
    return mixed, in_grad, grad_in, grad_down, vec_a, vec_b


def solution(mesh):
    placed = (
        P(None, "dp", None),
        P(None, "dp"),
        P("section", None, None),
        P("section", None, None),
        P("section", None),
        P("section", None),
        P(None, "dp", None),
    )
    return jax.shard_map(
        on_device,
        mesh=mesh,
        in_specs=placed,
        out_specs=(
            P(None, "dp", "section"),
            P(None, "dp", "section"),
            P("section", "dp", None),
            P("section", "dp", None),
            P("section", "dp"),
            P("section", "dp"),
        ),
        check_vma=False,
    )
```

```python
import functools
import math

import jax
import jax.numpy as jnp
from jax import lax
from jax.experimental import pallas as pl
from jax.experimental.pallas import tpu as pltpu
from jax.sharding import PartitionSpec as P

D = 768
HEADS = 12
HEAD_DIM = 64
FF = 3072
BLK = 512
MICRO = 2
CH = 256
GROUP = 8
EPS = 1e-06
NEG = -1e30
K0 = math.sqrt(2.0 / math.pi)
K1 = K0 * 0.044715
MIB = 1 << 20
bf16, f32 = jnp.bfloat16, jnp.float32
MESH = pl.DeviceIdType.MESH
NN = (((1,), (0,)), ((), ()))
NT = (((1,), (1,)), ((), ()))
TN = (((0,), (0,)), ((), ()))
TT = (((0,), (1,)), ((), ()))
ORDER_A, ORDER_B = (0, 1, 2), (1, 0, 2)
DOWN_PARTS = [(True, 128 * i, 128, ORDER_A if i % 3 else ORDER_B) for i in range(6)]
IN_PARTS = [(False, 256 * i, 256, ORDER_A if i % 3 else ORDER_B) for i in range(12)]


def dot(a, b, dims):
    return lax.dot_general(a, b, dims, preferred_element_type=f32)


def bit(value, b):
    return (value // (1 << b)) % 2


def chunks(me, order, step, flip):
    base = sum(bit(me, order[i]) * (1 << order[i]) for i in range(step))
    own = bit(me, order[step])
    base = base + ((1 - own) if flip else own) * (1 << order[step])
    free = order[step + 1 :]
    out = []
    for k in range(1 << len(free)):
        out.append(base + sum(((k >> i) & 1) << free[i] for i in range(len(free))))
    return out


FIRST_SLOT = (0, 4, 6)
PARTS = DOWN_PARTS + IN_PARTS
DOWN = list(range(len(DOWN_PARTS)))
IN = list(range(len(DOWN_PARTS), len(PARTS)))
MOVED = 3
AWAY = list(range(len(PARTS), len(PARTS) + MOVED))


def kernel(
    low,
    inputs,
    seg,
    w_in,
    w_down,
    vec_in,
    vec_out,
    cotangent,
    mixed,
    in_grad,
    out_in,
    out_down,
    out_vec_in,
    out_vec_out,
    wi,
    wd,
    a_buf,
    d_buf,
    y_buf,
    e_buf,
    q_buf,
    p_buf,
    xh,
    rstd,
    bias,
    rope,
    inv,
    bias_t,
    dw,
    dv,
    split,
    acc,
    db,
    vec_send,
    vec_recv,
    w_sem,
    load_sem,
    fwd_send,
    fwd_recv,
    bwd_send,
    bwd_recv,
    mix_send,
    mix_recv,
    grad_recv,
    vec_ssem,
    vec_rsem,
    free_sem,
    rs_send,
    rs_recv,
    out_sem,
    back,
    move_send,
    move_recv,
    back_send,
    back_recv,
    room_sem,
):
    sec = lax.axis_index("section")
    dp = lax.axis_index("dp")
    me = dp // low
    even = sec % 2 == 0
    odd = sec % 2 == 1

    def peer(b):
        return dp + (1 - 2 * bit(me, b)) * (1 << b) * low

    load_wi = pltpu.make_async_copy(w_in.at[0], wi, w_sem.at[0])
    load_wd = pltpu.make_async_copy(w_down.at[0], wd, w_sem.at[1])

    def load_a(m):
        return pltpu.make_async_copy(inputs.at[m], a_buf.at[m], load_sem.at[m])

    def load_d(m):
        return pltpu.make_async_copy(cotangent.at[m], d_buf.at[m], load_sem.at[m])

    @pl.when(sec == 0)
    def _():
        for m in range(MICRO):
            load_a(m).start()

    load_wi.start()

    @pl.when(odd)
    def _():
        load_wd.start()

    @pl.when(sec == 3)
    def _():
        for m in range(MICRO):
            load_d(m).start()

    barrier = pltpu.get_barrier_semaphore()
    for k in range(1, 4):
        pl.semaphore_signal(barrier, inc=1, device_id={"section": (sec + k) % 4}, device_id_type=MESH)
    for k in range(1, GROUP):
        pl.semaphore_signal(barrier, inc=1, device_id={"dp": (dp + k * low) % (GROUP * low)}, device_id_type=MESH)

    acc[...] = jnp.zeros_like(acc)
    db[...] = jnp.zeros_like(db)

    def rows_of(c):
        return pl.ds(pl.multiple_of(c * CH, CH), CH)

    def forward_copy(m, c):
        rows = rows_of(c)
        return pltpu.make_async_remote_copy(
            src_ref=y_buf.at[m, rows],
            dst_ref=a_buf.at[m, rows],
            send_sem=fwd_send.at[m, c],
            recv_sem=fwd_recv.at[m, c],
            device_id={"section": sec + 1},
            device_id_type=MESH,
        )

    def backward_copy(m, c):
        rows = rows_of(c)
        return pltpu.make_async_remote_copy(
            src_ref=d_buf.at[m, rows],
            dst_ref=d_buf.at[m, rows],
            send_sem=bwd_send.at[m, c],
            recv_sem=bwd_recv.at[m, c],
            device_id={"section": sec - 1},
            device_id_type=MESH,
        )

    def share_copy(m, c, k, out, recv):
        cols = rows_of(c)
        return pltpu.make_async_remote_copy(
            src_ref=split.at[k, m, :, cols],
            dst_ref=out.at[m, :, cols],
            send_sem=mix_send.at[k, m, c],
            recv_sem=recv.at[m, c],
            device_id={"section": k},
            device_id_type=MESH,
        )

    def own_copy(m, c, k, out):
        cols = rows_of(c)
        return pltpu.make_async_copy(split.at[k, m, :, cols], out.at[m, :, cols], mix_send.at[k, m, c])

    def share(m, c, value, own, out, recv):
        flipped = value.T
        for k in range(4):
            split[k, m, :, rows_of(c)] = flipped[192 * k : 192 * (k + 1), :]
        for k in range(4):
            if k == own:
                own_copy(m, c, k, out).start()
            else:
                share_copy(m, c, k, out, recv).start()

    def arrive(m, c):
        @pl.when(sec == 0)
        def _():
            @pl.when(c == 0)
            def _():
                load_a(m).wait()

        @pl.when(sec > 0)
        def _():
            forward_copy(m, c).wait_recv()

    def arrive_back(m, c):
        @pl.when(sec == 3)
        def _():
            @pl.when(c == 0)
            def _():
                load_d(m).wait()

        @pl.when(sec < 3)
        def _():
            backward_copy(m, c).wait_recv()

    def finish_forward(m, c, z):
        rows = rows_of(c)
        mean = jnp.mean(z, axis=1, keepdims=True)
        centred = z - mean
        spread = jnp.mean(centred * centred, axis=1, keepdims=True)
        r = lax.rsqrt(spread + EPS)
        unit = centred * r
        xh[m, rows, :] = unit
        rstd[m, rows, :] = r
        y = (unit * vec_out[:, 0:D] + vec_out[:, D : 2 * D]).astype(bf16)

        @pl.when(sec < 3)
        def _():
            y_buf[m, rows, :] = y
            forward_copy(m, c).start()

        @pl.when(sec == 3)
        def _():
            share(m, c, y, 3, mixed, mix_recv)

    def start_backward(m, c):
        rows = rows_of(c)
        dy = d_buf[m, rows, :].astype(f32)
        unit = xh[m, rows, :]
        dyg = dy * vec_out[:, 0:D]
        m1 = jnp.mean(dyg, axis=1, keepdims=True)
        m2 = jnp.mean(dyg * unit, axis=1, keepdims=True)
        dz = rstd[m, rows, :] * (dyg - m1 - unit * m2)
        du = dz.astype(bf16)

        @pl.when(sec < 3)
        def _():
            forward_copy(m, c).wait_send()

        y_buf[m, rows, :] = du
        acc[0:1, :] += jnp.sum(dy * unit, axis=0, keepdims=True)
        acc[1:2, :] += jnp.sum(dy, axis=0, keepdims=True)
        acc[2:3, :] += jnp.sum(du.astype(f32), axis=0, keepdims=True)
        xh[m, rows, :] = dz
        return du

    def finish_backward(m, c, da):
        rows = rows_of(c)

        @pl.when(sec > 0)
        def _():
            d_buf[m, rows, :] = da
            backward_copy(m, c).start()

        @pl.when(sec == 0)
        def _():
            share(m, c, da, 0, in_grad, grad_recv)

    def attention_tables(m):
        row = seg[pl.ds(m, 1), :].astype(f32)
        column = jnp.concatenate([jnp.broadcast_to(row, (128, BLK)).T] * 4, axis=1)
        same = column == jnp.broadcast_to(row, (BLK, BLK))
        bias[...] = jnp.where(same, 0.0, NEG)
        index = lax.broadcasted_iota(jnp.int32, (BLK, BLK), 0).astype(f32)
        opener = jnp.min(jnp.where(same, index, float(BLK)), axis=0, keepdims=True)
        place = lax.broadcasted_iota(jnp.int32, (1, BLK), 1).astype(f32) - opener
        number = lax.broadcasted_iota(jnp.int32, (HEAD_DIM // 2, BLK), 0).astype(f32)
        angle = place * jnp.exp(number * (-2.0 * math.log(10000.0) / HEAD_DIM))
        rope[m, 0] = jnp.cos(angle)
        rope[m, 1] = jnp.sin(angle)

    def project(m, c):
        arrive(m, c)
        rows = rows_of(c)
        a = a_buf[m, rows, :]
        co, si = rope[m, 0, :, rows], rope[m, 1, :, rows]
        for part in range(3):
            p = dot(wi[:, D * part : D * (part + 1)], a, TT)
            b = bias_t[D * part : D * (part + 1), :]
            p = p + jnp.concatenate([b, b], axis=1)
            if part < 2:
                p4 = p.reshape(HEADS, 2, 32, CH)
                t1, t2 = p4[:, 0], p4[:, 1]
                r1 = t1 * co[None] - t2 * si[None]
                r2 = t2 * co[None] + t1 * si[None]
                if part == 0:
                    r1, r2 = r1 * 0.125, r2 * 0.125
                p = jnp.concatenate([r1[:, None], r2[:, None]], axis=1).reshape(D, CH)
            p = p.astype(bf16)
            for j in range(3):
                q_buf[m, (3 * part + j) * 2 + c] = p[256 * j : 256 * (j + 1), :]

    def both(buf, m, block, rows):
        return jnp.concatenate([buf[m, block * 2, rows, :], buf[m, block * 2 + 1, rows, :]], axis=1)

    def heads_forward(m):
        scores, weights = {}, {}
        for t in range(HEADS + 2):
            if t < HEADS:
                g, rows = t // 4, slice(64 * (t % 4), 64 * (t % 4) + 64)
                scores[t] = dot(both(q_buf, m, 3 + g, rows), both(q_buf, m, g, rows), TN) + bias[...]
            h = t - 1
            if 0 <= h < HEADS:
                st = scores.pop(h)
                peak = jnp.max(st, axis=0, keepdims=True)
                e = jnp.exp(st - peak)
                r = 1.0 / jnp.sum(e, axis=0, keepdims=True)
                e = e.astype(bf16)
                e_buf[m, h * 2] = e[:, 0:256]
                e_buf[m, h * 2 + 1] = e[:, 256:512]
                inv[m, h] = jnp.broadcast_to(r, (8, BLK))
                weights[h] = (e, r)
            h = t - 2
            if 0 <= h:
                e, r = weights.pop(h)
                g, rows = h // 4, slice(64 * (h % 4), 64 * (h % 4) + 64)
                o = (dot(both(q_buf, m, 6 + g, rows), e, NN) * r).astype(bf16)
                q_buf[m, (9 + g) * 2, rows, :] = o[:, 0:256]
                q_buf[m, (9 + g) * 2 + 1, rows, :] = o[:, 256:512]

    def attended(m, c):
        return jnp.concatenate([q_buf[m, (9 + j) * 2 + c] for j in range(3)], axis=0)

    def close(m, c):
        rows = rows_of(c)
        u = dot(attended(m, c), wi[:, 3 * D :], TN) + vec_out[:, 2 * D :]
        finish_forward(m, c, u + a_buf[m, rows, :].astype(f32))

    def attention_forward(m):
        @pl.when(m == 0)
        def _():
            load_wi.wait()

        @pl.when(m > 0)
        def _():
            attention_tables(m)

        lax.fori_loop(0, 2, lambda c, _: (project(m, c), 0)[1], 0)
        heads_forward(m)
        lax.fori_loop(0, 2, lambda c, _: (close(m, c), 0)[1], 0)

    def open_back(m, c):
        arrive_back(m, c)
        rows = rows_of(c)
        du = start_backward(m, c)
        do = dot(wi[:, 3 * D :], du, NT).astype(bf16)
        for j in range(3):
            p_buf[m, (9 + j) * 2 + c] = do[256 * j : 256 * (j + 1), :]

    def heads_backward(m):
        co, si = rope[m, 0], rope[m, 1]
        pending = {}
        for t in range(HEADS + 1):
            if t < HEADS:
                g, rows = t // 4, slice(64 * (t % 4), 64 * (t % 4) + 64)
                do = (both(p_buf, m, 9 + g, rows).astype(f32) * inv[m, t, 0:1, :]).astype(bf16)
                o = both(q_buf, m, 9 + g, rows)
                inner = jnp.sum(do.astype(f32) * o.astype(f32), axis=0, keepdims=True)
                pending[t] = (do, inner, dot(both(q_buf, m, 6 + g, rows), do, TN))
            h = t - 1
            if 0 <= h:
                g, rows = h // 4, slice(64 * (h % 4), 64 * (h % 4) + 64)
                do, inner, dr = pending.pop(h)
                e = jnp.concatenate([e_buf[m, h * 2], e_buf[m, h * 2 + 1]], axis=1)
                ds = e * (dr - inner).astype(bf16)
                dvv = dot(do, e, NT)
                dq = dot(both(q_buf, m, 3 + g, rows), ds, NN)
                dk = dot(both(q_buf, m, g, rows), ds, NT)
                for part, x in ((0, dq * 0.125), (1, dk)):
                    t1, t2 = x[:32], x[32:]
                    x = jnp.concatenate([t1 * co + t2 * si, t2 * co - t1 * si], axis=0).astype(bf16)
                    p_buf[m, (3 * part + g) * 2, rows, :] = x[:, 0:256]
                    p_buf[m, (3 * part + g) * 2 + 1, rows, :] = x[:, 256:512]
                dvv = dvv.astype(bf16)
                p_buf[m, (6 + g) * 2, rows, :] = dvv[:, 0:256]
                p_buf[m, (6 + g) * 2 + 1, rows, :] = dvv[:, 256:512]

    def close_back(m, c):
        rows = rows_of(c)
        dp_t = jnp.concatenate([p_buf[m, fb * 2 + c] for fb in range(9)], axis=0)
        da = dot(dp_t, wi[:, 0 : 3 * D], TT) + xh[m, rows, :]
        finish_backward(m, c, da.astype(bf16))

    def add(m, held, new):
        return jnp.where(m == 0, new, held.astype(f32) + new).astype(bf16)

    def attention_weights(m):
        a_t = a_buf[m].T

        def part(n, _):
            cols = pl.ds(pl.multiple_of(n * D, D), D)
            d = jnp.concatenate(
                [jnp.concatenate([p_buf[m, (3 * n + j) * 2], p_buf[m, (3 * n + j) * 2 + 1]], axis=1) for j in range(3)],
                axis=0,
            )
            dw[:, cols] = add(m, dw[:, cols], dot(a_t, d, NT))
            db[:, cols] += dot(jnp.ones((8, BLK), bf16), d, NT)
            return 0

        lax.fori_loop(0, 3, part, 0)
        o = jnp.concatenate([attended(m, 0), attended(m, 1)], axis=1)
        dw[:, 3 * D :] = add(m, dw[:, 3 * D :], dot(o, y_buf[m], NN))

    def feed_rows(m, c):
        arrive(m, c)
        rows = rows_of(c)
        a = a_buf[m, rows, :]
        u, hidden = None, {}
        for t in range(8):
            if t < 6:
                cols = slice(512 * t, 512 * (t + 1))
                hidden[t] = dot(a, wi[:, cols], NN) + vec_in[:, cols]
            n = t - 2
            if n >= 0:
                h = hidden.pop(n)
                h2 = h * h
                s = 0.5 * jnp.tanh(h * (K0 + K1 * h2)) + 0.5
                g = h * s
                slope = (s + g * (1.0 - s) * (2.0 * K0 + 6.0 * K1 * h2)).astype(bf16)
                g = g.astype(bf16)
                for j in range(2):
                    q_buf[m, c * 12 + 2 * n + j] = g[:, 256 * j : 256 * (j + 1)]
                    e_buf[m, 2 * n + j, rows, :] = slope[:, 256 * j : 256 * (j + 1)]
                x = dot(g, wd[512 * n : 512 * (n + 1), :], NN)
                u = x if u is None else u + x
        finish_forward(m, c, u + vec_out[:, 2 * D :] + a.astype(f32))

    def feed_forward(m):
        @pl.when(m == 0)
        def _():
            load_wi.wait()
            load_wd.wait()

        lax.fori_loop(0, 2, lambda c, _: (feed_rows(m, c), 0)[1], 0)

    def feed_open_back(m, c):
        arrive_back(m, c)
        start_backward(m, c)

    def feed_rows_back(m, c):
        rows = rows_of(c)
        du = y_buf[m, rows, :]
        da, grads = xh[m, rows, :], {}
        for t in range(5):
            if t < 4:
                grads[t] = dot(du, wd[D * t : D * (t + 1), :], NT)
            n = t - 1
            if n >= 0:
                slope = jnp.concatenate([e_buf[m, 3 * n + j, rows, :] for j in range(3)], axis=1)
                dh = (grads.pop(n) * slope.astype(f32)).astype(bf16)
                for j in range(3):
                    p_buf[m, c * 12 + 3 * n + j] = dh[:, 256 * j : 256 * (j + 1)]
                da = da + dot(dh, wi[:, D * n : D * (n + 1)], NT)
        finish_backward(m, c, da.astype(bf16))

    def tile(buf, m, n):
        return jnp.concatenate(
            [jnp.concatenate([buf[m, c * 12 + 3 * n + j] for j in range(3)], axis=1) for c in range(2)], axis=0
        )

    def feed_weights_down(m):
        def part(n, _):
            rows = pl.ds(pl.multiple_of(n * D, D), D)
            dv[rows, :] = add(m, dv[rows, :], dot(tile(q_buf, m, n), y_buf[m], TN))
            return 0

        lax.fori_loop(0, 4, part, 0)

    def feed_weights_in(m):
        def part(n, _):
            cols = pl.ds(pl.multiple_of(n * D, D), D)
            dh = tile(p_buf, m, n)
            dw[:, cols] = add(m, dw[:, cols], dot(a_buf[m], dh, TN))
            db[:, cols] += jnp.broadcast_to(jnp.sum(dh.astype(f32), axis=0, keepdims=True), (8, D))
            return 0

        lax.fori_loop(0, 4, part, 0)

    def part_of(number):
        if number in AWAY:
            return DOWN_PARTS[number - len(PARTS)], wd
        return PARTS[number], dv if PARTS[number][0] else dw

    def landing(number, slot):
        part, grad = part_of(number)
        if not part[0]:
            return wi.at[pl.ds(96 * slot, 96), pl.ds(part[1], part[2])]
        first = 0 if number in AWAY else 12
        number = number % len(PARTS)
        piece = (number // 2) * 7 + slot
        return e_buf.at[piece // 12, first + piece % 12, pl.ds(0, 384), pl.ds(128 * (number % 2), 128)]

    def own_rows(part, j):
        size = 384 if part[0] else 96
        return pl.ds(pl.multiple_of(j * size, size), size), pl.ds(part[1], part[2])

    def step_copies(number, step):
        part, grad = part_of(number)
        copies = []
        for k, j in enumerate(chunks(me, part[3], step, True)):
            slot = FIRST_SLOT[step] + k
            copies.append(
                pltpu.make_async_remote_copy(
                    src_ref=grad.at[own_rows(part, j)],
                    dst_ref=landing(number, slot),
                    send_sem=rs_send.at[number, slot],
                    recv_sem=rs_recv.at[number, slot],
                    device_id={"dp": peer(part[3][step])},
                    device_id_type=MESH,
                )
            )
        return copies

    def move_copies(p):
        copies = []
        for j in range(GROUP):
            index = own_rows(DOWN_PARTS[p], j)
            copies.append(
                pltpu.make_async_remote_copy(
                    src_ref=dv.at[index],
                    dst_ref=wd.at[index],
                    send_sem=move_send.at[p, j],
                    recv_sem=move_recv.at[p, j],
                    device_id={"section": sec + 2},
                    device_id_type=MESH,
                )
            )
        return copies

    def back_copy(p):
        return pltpu.make_async_remote_copy(
            src_ref=back.at[p],
            dst_ref=back.at[p],
            send_sem=back_send.at[p],
            recv_sem=back_recv.at[p],
            device_id={"section": sec - 2},
            device_id_type=MESH,
        )

    def send_step(number, step):
        if step == 0 and number in AWAY:
            for copy in move_copies(number - len(PARTS)):
                copy.wait_recv()
        for copy in step_copies(number, step):
            copy.start()

    def take_step(number, step):
        part, grad = part_of(number)
        copies = step_copies(number, step)
        for k, j in enumerate(chunks(me, part[3], step, False)):
            copies[k].wait_recv()
            index = own_rows(part, j)
            total = grad[index].astype(f32) + landing(number, FIRST_SLOT[step] + k)[...].astype(f32)
            if step < 2:
                grad[index] = total.astype(bf16)
        down, first, width, _ = part
        if step < 2:
            send_step(number, step + 1)
        elif number in AWAY:
            back[number - len(PARTS)] = total
            back_copy(number - len(PARTS)).start()
        elif down:
            xh[1, 0:384, first : first + width] = total
        else:
            q, off = first // D, first % D
            xh[0, 96 * q : 96 * (q + 1), off : off + width] = total

    def exchange(numbers, ahead, lag, started):
        n = len(numbers)
        for t in range(started, n + ahead + 2 * lag):
            for step in (2, 1, 0):
                i = t - ahead - lag * step
                if 0 <= i < n:
                    take_step(numbers[i], step)
            if t < n:
                send_step(numbers[t], 0)
        for number in numbers:
            for step in range(3):
                for copy in step_copies(number, step):
                    copy.wait_send()

    def weights_free():
        for b in range(3):
            pl.semaphore_signal(free_sem.at[b], inc=1, device_id={"dp": peer(b)}, device_id_type=MESH)

    def await_free():
        for b in range(3):
            pl.semaphore_wait(free_sem.at[b], 1)

    late = sec >= 2

    def span(m):
        return jnp.where(late, 0, m), jnp.where(late & (m == 0), 0, m + 1)

    def attention_backward(m):
        lax.fori_loop(0, 2, lambda c, _: (open_back(m, c), 0)[1], 0)
        heads_backward(m)
        lax.fori_loop(0, 2, lambda c, _: (close_back(m, c), 0)[1], 0)

        @pl.when(m == MICRO - 1)
        def _():
            weights_free()

        lax.fori_loop(*span(m), lambda i, _: (attention_weights(i), 0)[1], 0)

    def feed_backward(m):
        early = (sec == 1) & (m == MICRO - 1)
        begin, end = span(m)

        def down_products(begin, end):
            lax.fori_loop(begin, end, lambda i, _: (feed_weights_down(i), 0)[1], 0)

        def rows(c, _):
            feed_open_back(m, c)

            @pl.when(early & (c == 1))
            def _():
                down_products(begin, end)
                for number in DOWN[MOVED:]:
                    send_step(number, 0)
                pl.semaphore_wait(room_sem, 1)
                for p in range(MOVED):
                    for copy in move_copies(p):
                        copy.start()

            feed_rows_back(m, c)
            return 0

        lax.fori_loop(0, 2, rows, 0)

        @pl.when(m == MICRO - 1)
        def _():
            weights_free()

        @pl.when((sec == 3) & (m == MICRO - 1))
        def _():
            pl.semaphore_signal(room_sem, inc=1, device_id={"section": 1}, device_id_type=MESH)

        @pl.when(jnp.logical_not(early))
        def _():
            down_products(begin, end)

        @pl.when((sec == 3) & (m == MICRO - 1))
        def _():
            for number in DOWN:
                send_step(number, 0)

        lax.fori_loop(begin, end, lambda i, _: (feed_weights_in(i), 0)[1], 0)

    @pl.when(even)
    def _():
        attention_tables(0)
        for i in range(3):
            b = jnp.broadcast_to(vec_in[:, D * i : D * (i + 1)], (128, D))
            bias_t[D * i : D * (i + 1), :] = b.T

    pl.semaphore_wait(barrier, 3 + GROUP - 1)

    def task(t, _):
        forward = jnp.where(sec == 3, t % 2 == 0, t < 2)
        m = jnp.where(sec == 3, t // 2, t % 2)

        @pl.when(forward & even)
        def _():
            attention_forward(m)

        @pl.when(forward & odd)
        def _():
            feed_forward(m)

        @pl.when(jnp.logical_not(forward) & even)
        def _():
            attention_backward(m)

        @pl.when(jnp.logical_not(forward) & odd)
        def _():
            feed_backward(m)

        return 0

    lax.fori_loop(0, 2 * MICRO, task, 0)

    await_free()

    vec_send[...] = jnp.zeros_like(vec_send)
    outer = jnp.concatenate([acc[0:1, :], acc[1:2, :], acc[2:3, :]], axis=1)
    for j in range(GROUP):
        vec_send[j, 0:1, :] = db[0:1, 384 * j : 384 * (j + 1)]
        vec_send[j, 1:2, 0:288] = outer[:, 288 * j : 288 * (j + 1)]

    def vec_copy(k):
        there = (me + k) % GROUP
        return pltpu.make_async_remote_copy(
            src_ref=vec_send.at[there],
            dst_ref=vec_recv.at[k],
            send_sem=vec_ssem.at[k],
            recv_sem=vec_rsem.at[k],
            device_id={"dp": there * low + dp % low},
            device_id_type=MESH,
        )

    for k in range(1, GROUP):
        vec_copy(k).start()

    @pl.when(sec == 1)
    def _():
        exchange(DOWN[MOVED:] + IN, 6, 6, len(DOWN) - MOVED)
        for p in range(MOVED):
            back_copy(p).wait_recv()
            first, width = DOWN_PARTS[p][1], DOWN_PARTS[p][2]
            xh[1, 0:384, first : first + width] = back[p]
            for copy in move_copies(p):
                copy.wait_send()

    @pl.when(sec == 3)
    def _():
        exchange(DOWN + IN + AWAY, 6, 6, len(DOWN))
        for p in range(MOVED):
            back_copy(p).wait_send()

    @pl.when(even)
    def _():
        exchange(IN, 4, 4, 0)

    @pl.when(even)
    def _():
        xh[1, 0:384, :] = jnp.zeros((384, D), f32)

    outs = [pltpu.make_async_copy(xh.at[1, pl.ds(0, 384)], out_down.at[0], out_sem.at[4])]
    for i in range(4):
        outs.append(
            pltpu.make_async_copy(xh.at[0, pl.ds(96 * i, 96)], out_in.at[0, :, pl.ds(D * i, D)], out_sem.at[i])
        )
    for copy in outs:
        copy.start()
    total = vec_send[me]
    for k in range(1, GROUP):
        vec_copy(k).wait_recv()
        total = total + vec_recv[k]
    out_vec_in[...] = total[0:1, :]
    out_vec_out[...] = total[1:2, 0:288]

    for k in range(1, GROUP):
        vec_copy(k).wait_send()

    for m in range(MICRO):
        for c in range(2):

            @pl.when(sec > 0)
            def _():
                backward_copy(m, c).wait_send()
                share_copy(m, c, 0, in_grad, grad_recv).wait_recv()

            @pl.when(sec < 3)
            def _():
                share_copy(m, c, 0, mixed, mix_recv).wait_recv()

            @pl.when(sec == 0)
            def _():
                own_copy(m, c, 0, in_grad).wait()
                for k in range(1, 4):
                    share_copy(m, c, k, in_grad, grad_recv).wait_send()

            @pl.when(sec == 3)
            def _():
                own_copy(m, c, 3, mixed).wait()
                for k in range(3):
                    share_copy(m, c, k, mixed, mix_recv).wait_send()

    for copy in outs:
        copy.wait()


def settle(*refs):
    count = len(refs) // 2
    sems = refs[-1]
    copies = [pltpu.make_async_copy(refs[i], refs[count + i], sems.at[i]) for i in range(count)]
    for copy in copies:
        copy.start()
    for copy in copies:
        copy.wait()


def on_device(inputs, segment_ids, w_in, w_down, vec_in, vec_out, cotangent):
    world = lax.axis_size("dp")
    low = world // GROUP
    hbm = pl.BlockSpec(memory_space=pl.ANY)
    vmem = pl.BlockSpec(memory_space=pltpu.VMEM)
    V, S = pltpu.VMEM, pltpu.SemaphoreType.DMA
    parts = len(PARTS) + MOVED
    shapes = (
        jax.ShapeDtypeStruct((MICRO, D // 4, BLK), bf16),
        jax.ShapeDtypeStruct((MICRO, D // 4, BLK), bf16),
        jax.ShapeDtypeStruct((1, D // GROUP, FF), f32),
        jax.ShapeDtypeStruct((1, FF // GROUP, D), f32),
        jax.ShapeDtypeStruct((1, FF // GROUP), f32),
        jax.ShapeDtypeStruct((1, 3 * D // GROUP), f32),
    )
    results = pl.pallas_call(
        functools.partial(kernel, low),
        out_shape=shapes,
        in_specs=[hbm, vmem, hbm, hbm, vmem, vmem, hbm],
        out_specs=(hbm, hbm, hbm, hbm, vmem, vmem),
        scratch_shapes=[
            V((D, FF), bf16),
            V((FF, D), bf16),
            V((MICRO, BLK, D), bf16),
            V((MICRO, BLK, D), bf16),
            V((MICRO, BLK, D), bf16),
            V((MICRO, 24, 512, 256), bf16),
            V((MICRO, 24, 256, 256), bf16),
            V((MICRO, 24, 256, 256), bf16),
            V((MICRO, BLK, D), f32),
            V((MICRO, BLK, 1), f32),
            V((BLK, BLK), f32),
            V((MICRO, 2, HEAD_DIM // 2, BLK), f32),
            V((MICRO, HEADS, 8, BLK), f32),
            V((3 * D, 128), f32),
            V((D, FF), bf16),
            V((FF, D), bf16),
            V((4, MICRO, D // 4, BLK), bf16),
            V((8, D), f32),
            V((8, FF), f32),
            V((GROUP, 8, 384), f32),
            V((GROUP, 8, 384), f32),
            S((2,)),
            S((MICRO,)),
            S((MICRO, 2)),
            S((MICRO, 2)),
            S((MICRO, 2)),
            S((MICRO, 2)),
            S((4, MICRO, 2)),
            S((MICRO, 2)),
            S((MICRO, 2)),
            S((GROUP,)),
            S((GROUP,)),
            pltpu.SemaphoreType.REGULAR((3,)),
            S((parts, 7)),
            S((parts, 7)),
            S((5,)),
            V((MOVED, FF // GROUP, 128), f32),
            S((MOVED, GROUP)),
            S((MOVED, GROUP)),
            S((MOVED,)),
            S((MOVED,)),
            pltpu.SemaphoreType.REGULAR,
        ],
        compiler_params=pltpu.CompilerParams(
            collective_id=0, has_side_effects=True, vmem_limit_bytes=63 * MIB
        ),
    )(inputs, segment_ids, w_in, w_down, vec_in, vec_out, cotangent)
    mixed, in_grad, grad_in, grad_down, vec_a, vec_b = pl.pallas_call(
        settle,
        out_shape=shapes,
        in_specs=[vmem] * len(shapes),
        out_specs=(hbm,) * len(shapes),
        scratch_shapes=[S((len(shapes),))],
    )(*results)
    if low > 1:
        groups = [[g * low + i for i in range(low)] for g in range(GROUP)]

        def rest(value):
            return lax.psum_scatter(
                value, "dp", scatter_dimension=1, axis_index_groups=groups, tiled=True
            )

        grad_in, grad_down, vec_a, vec_b = rest(grad_in), rest(grad_down), rest(vec_a), rest(vec_b)
    mixed, in_grad = jnp.swapaxes(mixed, 1, 2), jnp.swapaxes(in_grad, 1, 2)
    return mixed, in_grad, grad_in, grad_down, vec_a, vec_b


def solution(mesh):
    placed = (
        P(None, "dp", None),
        P(None, "dp"),
        P("section", None, None),
        P("section", None, None),
        P("section", None),
        P("section", None),
        P(None, "dp", None),
    )
    return jax.shard_map(
        on_device,
        mesh=mesh,
        in_specs=placed,
        out_specs=(
            P(None, "dp", "section"),
            P(None, "dp", "section"),
            P("section", "dp", None),
            P("section", "dp", None),
            P("section", "dp"),
            P("section", "dp"),
        ),
        check_vma=False,
    )
```

```python
import functools
import math

import jax
import jax.numpy as jnp
from jax import lax
from jax.experimental import pallas as pl
from jax.experimental.pallas import tpu as pltpu
from jax.sharding import PartitionSpec as P

D = 768
HEADS = 12
HEAD_DIM = 64
FF = 3072
BLK = 512
MICRO = 2
CH = 256
GROUP = 8
EPS = 1e-06
NEG = -1e30
K0 = math.sqrt(2.0 / math.pi)
K1 = K0 * 0.044715
LN2 = math.log(2.0)
Q_SCALE = HEAD_DIM**-0.5 / LN2
MIB = 1 << 20
bf16, f32 = jnp.bfloat16, jnp.float32
MESH = pl.DeviceIdType.MESH
NN = (((1,), (0,)), ((), ()))
NT = (((1,), (1,)), ((), ()))
TN = (((0,), (0,)), ((), ()))
TT = (((0,), (1,)), ((), ()))
ORDER_A, ORDER_B = (0, 1, 2), (1, 0, 2)
DOWN_PARTS = [(True, 128 * i, 128, ORDER_A if i % 3 else ORDER_B) for i in range(6)]
IN_PARTS = [(False, 256 * i, 256, ORDER_A if i % 3 else ORDER_B) for i in range(12)]


def dot(a, b, dims):
    return lax.dot_general(a, b, dims, preferred_element_type=f32)


def bit(value, b):
    return (value // (1 << b)) % 2


PARTS = DOWN_PARTS + IN_PARTS
DOWN = list(range(len(DOWN_PARTS)))
IN = list(range(len(DOWN_PARTS), len(PARTS)))
MOVED = 3
AWAY = list(range(len(PARTS), len(PARTS) + MOVED))
ORDER_3 = DOWN + IN[:5] + AWAY[:1] + IN[5:7] + AWAY[1:2] + IN[7:9] + AWAY[2:] + IN[9:]


def kernel(
    low,
    inputs,
    seg,
    w_in,
    w_down,
    vec_in,
    vec_out,
    cotangent,
    mixed,
    in_grad,
    out_in,
    out_down,
    out_vec_in,
    out_vec_out,
    wi,
    wd,
    a_buf,
    d_buf,
    y_buf,
    e_buf,
    q_buf,
    p_buf,
    xh,
    rstd,
    bias,
    rope,
    inv,
    bias_t,
    dw,
    dv,
    split,
    acc,
    db,
    vec_send,
    vec_recv,
    w_sem,
    load_sem,
    fwd_send,
    fwd_recv,
    bwd_send,
    bwd_recv,
    mix_send,
    mix_recv,
    grad_recv,
    vec_ssem,
    vec_rsem,
    free_sem,
    rs_send,
    rs_recv,
    out_sem,
    back,
    move_send,
    move_recv,
    back_send,
    back_recv,
    room_sem,
):
    sec = lax.axis_index("section")
    dp = lax.axis_index("dp")
    me = dp // low
    even = sec % 2 == 0
    odd = sec % 2 == 1

    def peer(b):
        return dp + (1 - 2 * bit(me, b)) * (1 << b) * low

    load_wi = pltpu.make_async_copy(w_in, wi, w_sem.at[0])
    load_wd = pltpu.make_async_copy(w_down, wd, w_sem.at[1])

    def load_a(m):
        return pltpu.make_async_copy(inputs.at[m], a_buf.at[m], load_sem.at[m])

    def load_d(m):
        return pltpu.make_async_copy(cotangent.at[m], d_buf.at[m], load_sem.at[m])

    @pl.when(sec == 0)
    def _():
        for m in range(MICRO):
            load_a(m).start()

    load_wi.start()

    @pl.when(odd)
    def _():
        load_wd.start()

    @pl.when(sec == 3)
    def _():
        for m in range(MICRO):
            load_d(m).start()

    barrier = pltpu.get_barrier_semaphore()
    for k in range(1, 4):
        pl.semaphore_signal(barrier, inc=1, device_id={"section": (sec + k) % 4}, device_id_type=MESH)
    for k in range(1, GROUP):
        pl.semaphore_signal(barrier, inc=1, device_id={"dp": (dp + k * low) % (GROUP * low)}, device_id_type=MESH)

    acc[...] = jnp.zeros_like(acc)
    db[...] = jnp.zeros_like(db)

    def w_cols(first, last):
        return wi[:, :, :, :, first:last].reshape(D, last - first)

    def w_rows(first, last):
        pieces = []
        while first < last:
            j, start = first // 384, first % 384
            stop = min(384, start + last - first)
            pieces.append(wd[j // 4, j // 2 % 2, j % 2, start:stop, :])
            first += stop - start
        return jnp.concatenate(pieces, axis=0)

    def rows_of(c):
        return pl.ds(pl.multiple_of(c * CH, CH), CH)

    def forward_copy(m, c):
        rows = rows_of(c)
        return pltpu.make_async_remote_copy(
            src_ref=y_buf.at[m, rows],
            dst_ref=a_buf.at[m, rows],
            send_sem=fwd_send.at[m, c],
            recv_sem=fwd_recv.at[m, c],
            device_id={"section": sec + 1},
            device_id_type=MESH,
        )

    def backward_copy(m, c):
        rows = rows_of(c)
        return pltpu.make_async_remote_copy(
            src_ref=d_buf.at[m, rows],
            dst_ref=d_buf.at[m, rows],
            send_sem=bwd_send.at[m, c],
            recv_sem=bwd_recv.at[m, c],
            device_id={"section": sec - 1},
            device_id_type=MESH,
        )

    def share_copy(m, c, k, out, recv):
        cols = rows_of(c)
        return pltpu.make_async_remote_copy(
            src_ref=split.at[k, m, :, cols],
            dst_ref=out.at[m, :, cols],
            send_sem=mix_send.at[k, m, c],
            recv_sem=recv.at[m, c],
            device_id={"section": k},
            device_id_type=MESH,
        )

    def own_copy(m, c, k, out):
        cols = rows_of(c)
        return pltpu.make_async_copy(split.at[k, m, :, cols], out.at[m, :, cols], mix_send.at[k, m, c])

    def share(m, c, value, own, out, recv):
        flipped = value.T
        for k in range(4):
            split[k, m, :, rows_of(c)] = flipped[192 * k : 192 * (k + 1), :]
        for k in range(4):
            if k == own:
                own_copy(m, c, k, out).start()
            else:
                share_copy(m, c, k, out, recv).start()

    def arrive(m, c):
        @pl.when(sec == 0)
        def _():
            @pl.when(c == 0)
            def _():
                load_a(m).wait()

        @pl.when(sec > 0)
        def _():
            forward_copy(m, c).wait_recv()

    def arrive_back(m, c):
        @pl.when(sec == 3)
        def _():
            @pl.when(c == 0)
            def _():
                load_d(m).wait()

        @pl.when(sec < 3)
        def _():
            backward_copy(m, c).wait_recv()

    def finish_forward(m, c, z):
        rows = rows_of(c)
        mean = jnp.mean(z, axis=1, keepdims=True)
        centred = z - mean
        spread = jnp.mean(centred * centred, axis=1, keepdims=True)
        r = lax.rsqrt(spread + EPS)
        unit = centred * r
        xh[m, rows, :] = unit
        rstd[m, rows, :] = r
        y = (unit * vec_out[:, 0:D] + vec_out[:, D : 2 * D]).astype(bf16)

        @pl.when(sec < 3)
        def _():
            y_buf[m, rows, :] = y
            forward_copy(m, c).start()

        @pl.when(sec == 3)
        def _():
            share(m, c, y, 3, mixed, mix_recv)

    def start_backward(m, c):
        rows = rows_of(c)
        dy = d_buf[m, rows, :].astype(f32)
        unit = xh[m, rows, :]
        dyg = dy * vec_out[:, 0:D]
        m1 = jnp.mean(dyg, axis=1, keepdims=True)
        m2 = jnp.mean(dyg * unit, axis=1, keepdims=True)
        dz = rstd[m, rows, :] * (dyg - m1 - unit * m2)
        du = dz.astype(bf16)

        @pl.when(sec < 3)
        def _():
            forward_copy(m, c).wait_send()

        y_buf[m, rows, :] = du
        acc[0:1, :] += jnp.sum(dy * unit, axis=0, keepdims=True)
        acc[1:2, :] += jnp.sum(dy, axis=0, keepdims=True)
        acc[2:3, :] += jnp.sum(du.astype(f32), axis=0, keepdims=True)
        xh[m, rows, :] = dz
        return du

    def finish_backward(m, c, da):
        rows = rows_of(c)

        @pl.when(sec > 0)
        def _():
            d_buf[m, rows, :] = da
            backward_copy(m, c).start()

        @pl.when(sec == 0)
        def _():
            share(m, c, da, 0, in_grad, grad_recv)

    def attention_tables(m):
        row = seg[pl.ds(m, 1), :].astype(f32)
        column = jnp.concatenate([jnp.broadcast_to(row, (128, BLK)).T] * 4, axis=1)
        same = column == jnp.broadcast_to(row, (BLK, BLK))
        bias[...] = jnp.where(same, 0.0, NEG)
        index = lax.broadcasted_iota(jnp.int32, (BLK, BLK), 0).astype(f32)
        opener = jnp.min(jnp.where(same, index, float(BLK)), axis=0, keepdims=True)
        place = lax.broadcasted_iota(jnp.int32, (1, BLK), 1).astype(f32) - opener
        number = lax.broadcasted_iota(jnp.int32, (HEAD_DIM // 2, BLK), 0).astype(f32)
        angle = place * jnp.exp(number * (-2.0 * math.log(10000.0) / HEAD_DIM))
        rope[m, 0] = jnp.cos(angle)
        rope[m, 1] = jnp.sin(angle)

    def project(m, c):
        arrive(m, c)
        rows = rows_of(c)
        a = a_buf[m, rows, :]
        co, si = rope[m, 0, :, rows], rope[m, 1, :, rows]
        for part in range(3):
            p = dot(w_cols(D * part, D * (part + 1)), a, TT)
            b = bias_t[D * part : D * (part + 1), :]
            p = p + jnp.concatenate([b, b], axis=1)
            if part < 2:
                p4 = p.reshape(HEADS, 2, 32, CH)
                t1, t2 = p4[:, 0], p4[:, 1]
                r1 = t1 * co[None] - t2 * si[None]
                r2 = t2 * co[None] + t1 * si[None]
                if part == 0:
                    r1, r2 = r1 * Q_SCALE, r2 * Q_SCALE
                p = jnp.concatenate([r1[:, None], r2[:, None]], axis=1).reshape(D, CH)
            p = p.astype(bf16)
            for j in range(3):
                q_buf[m, (3 * part + j) * 2 + c] = p[256 * j : 256 * (j + 1), :]

    def both(buf, m, block, rows):
        return jnp.concatenate([buf[m, block * 2, rows, :], buf[m, block * 2 + 1, rows, :]], axis=1)

    def heads_forward(m):
        scores, weights = {}, {}
        for t in range(HEADS + 2):
            if t < HEADS:
                g, rows = t // 4, slice(64 * (t % 4), 64 * (t % 4) + 64)
                scores[t] = dot(both(q_buf, m, 3 + g, rows), both(q_buf, m, g, rows), TN) + bias[...]
            h = t - 1
            if 0 <= h < HEADS:
                st = scores.pop(h)
                peak = jnp.max(st, axis=0, keepdims=True)
                e = jnp.exp2(st - peak)
                r = 1.0 / jnp.sum(e, axis=0, keepdims=True)
                e = e.astype(bf16)
                e_buf[m, h // 6, h % 6 * 2] = e[:, 0:256]
                e_buf[m, h // 6, h % 6 * 2 + 1] = e[:, 256:512]
                inv[m, h] = jnp.broadcast_to(r, (8, BLK))
                weights[h] = (e, r)
            h = t - 2
            if 0 <= h:
                e, r = weights.pop(h)
                g, rows = h // 4, slice(64 * (h % 4), 64 * (h % 4) + 64)
                o = (dot(both(q_buf, m, 6 + g, rows), e, NN) * r).astype(bf16)
                q_buf[m, (9 + g) * 2, rows, :] = o[:, 0:256]
                q_buf[m, (9 + g) * 2 + 1, rows, :] = o[:, 256:512]

    def attended(m, c):
        return jnp.concatenate([q_buf[m, (9 + j) * 2 + c] for j in range(3)], axis=0)

    def close(m, c):
        rows = rows_of(c)
        u = dot(attended(m, c), w_cols(3 * D, FF), TN) + vec_out[:, 2 * D :]
        finish_forward(m, c, u + a_buf[m, rows, :].astype(f32))

    def attention_forward(m):
        @pl.when(m == 0)
        def _():
            load_wi.wait()

        @pl.when(m > 0)
        def _():
            attention_tables(m)

        lax.fori_loop(0, 2, lambda c, _: (project(m, c), 0)[1], 0)
        heads_forward(m)
        lax.fori_loop(0, 2, lambda c, _: (close(m, c), 0)[1], 0)

    def open_back(m, c):
        arrive_back(m, c)
        rows = rows_of(c)
        du = start_backward(m, c)
        do = dot(w_cols(3 * D, FF), du, NT).astype(bf16)
        for j in range(3):
            p_buf[m, (9 + j) * 2 + c] = do[256 * j : 256 * (j + 1), :]

    def heads_backward(m):
        co, si = rope[m, 0], rope[m, 1]
        pending = {}
        for t in range(HEADS + 1):
            if t < HEADS:
                g, rows = t // 4, slice(64 * (t % 4), 64 * (t % 4) + 64)
                do = (both(p_buf, m, 9 + g, rows).astype(f32) * inv[m, t, 0:1, :]).astype(bf16)
                o = both(q_buf, m, 9 + g, rows)
                inner = jnp.sum(do.astype(f32) * o.astype(f32), axis=0, keepdims=True)
                pending[t] = (do, inner, dot(both(q_buf, m, 6 + g, rows), do, TN))
            h = t - 1
            if 0 <= h:
                g, rows = h // 4, slice(64 * (h % 4), 64 * (h % 4) + 64)
                do, inner, dr = pending.pop(h)
                e = jnp.concatenate([e_buf[m, h // 6, h % 6 * 2], e_buf[m, h // 6, h % 6 * 2 + 1]], axis=1)
                ds = e * (dr - inner).astype(bf16)
                dvv = dot(do, e, NT)
                dq = dot(both(q_buf, m, 3 + g, rows), ds, NN)
                dk = dot(both(q_buf, m, g, rows), ds, NT)
                for part, x in ((0, dq * 0.125), (1, dk * LN2)):
                    t1, t2 = x[:32], x[32:]
                    x = jnp.concatenate([t1 * co + t2 * si, t2 * co - t1 * si], axis=0).astype(bf16)
                    p_buf[m, (3 * part + g) * 2, rows, :] = x[:, 0:256]
                    p_buf[m, (3 * part + g) * 2 + 1, rows, :] = x[:, 256:512]
                dvv = dvv.astype(bf16)
                p_buf[m, (6 + g) * 2, rows, :] = dvv[:, 0:256]
                p_buf[m, (6 + g) * 2 + 1, rows, :] = dvv[:, 256:512]

    def close_back(m, c):
        rows = rows_of(c)
        dp_t = jnp.concatenate([p_buf[m, fb * 2 + c] for fb in range(9)], axis=0)
        da = dot(dp_t, w_cols(0, 3 * D), TT) + xh[m, rows, :]
        finish_backward(m, c, da.astype(bf16))

    def add(m, ref, index, new):
        held = ref[index]
        new = new.reshape(held.shape)
        ref[index] = jnp.where(m == 0, new, held.astype(f32) + new).astype(bf16)

    def attention_weights(m):
        a_t = a_buf[m].T

        def part(n, _):
            cols = pl.ds(pl.multiple_of(n * D, D), D)
            d = jnp.concatenate(
                [jnp.concatenate([p_buf[m, (3 * n + j) * 2], p_buf[m, (3 * n + j) * 2 + 1]], axis=1) for j in range(3)],
                axis=0,
            )
            add(m, dw, (slice(None),) * 4 + (cols,), dot(a_t, d, NT))
            db[:, cols] += dot(jnp.ones((8, BLK), bf16), d, NT)
            return 0

        lax.fori_loop(0, 3, part, 0)
        o = jnp.concatenate([attended(m, 0), attended(m, 1)], axis=1)
        add(m, dw, (slice(None),) * 4 + (slice(3 * D, FF),), dot(o, y_buf[m], NN))

    def feed_rows(m, c):
        arrive(m, c)
        rows = rows_of(c)
        a = a_buf[m, rows, :]
        u, hidden = None, {}
        for t in range(8):
            if t < 6:
                cols = slice(512 * t, 512 * (t + 1))
                hidden[t] = dot(a, w_cols(512 * t, 512 * (t + 1)), NN) + vec_in[:, cols]
            n = t - 2
            if n >= 0:
                h = hidden.pop(n)
                h2 = h * h
                s = 0.5 * jnp.tanh(h * (K0 + K1 * h2)) + 0.5
                g = h * s
                slope = (s + g * (1.0 - s) * (2.0 * K0 + 6.0 * K1 * h2)).astype(bf16)
                g = g.astype(bf16)
                for j in range(2):
                    q_buf[m, c * 12 + 2 * n + j] = g[:, 256 * j : 256 * (j + 1)]
                    e_buf[m, 0, 2 * n + j, rows, :] = slope[:, 256 * j : 256 * (j + 1)]
                x = dot(g, w_rows(512 * n, 512 * (n + 1)), NN)
                u = x if u is None else u + x
        finish_forward(m, c, u + vec_out[:, 2 * D :] + a.astype(f32))

    def feed_forward(m):
        @pl.when(m == 0)
        def _():
            load_wi.wait()
            load_wd.wait()

        lax.fori_loop(0, 2, lambda c, _: (feed_rows(m, c), 0)[1], 0)

    def feed_open_back(m, c):
        arrive_back(m, c)
        start_backward(m, c)

    def feed_rows_back(m, c):
        rows = rows_of(c)
        du = y_buf[m, rows, :]
        da, grads = xh[m, rows, :], {}
        for t in range(5):
            if t < 4:
                grads[t] = dot(du, w_rows(D * t, D * (t + 1)), NT)
            n = t - 1
            if n >= 0:
                slope = jnp.concatenate([e_buf[m, 0, 3 * n + j, rows, :] for j in range(3)], axis=1)
                dh = (grads.pop(n) * slope.astype(f32)).astype(bf16)
                for j in range(3):
                    p_buf[m, c * 12 + 3 * n + j] = dh[:, 256 * j : 256 * (j + 1)]
                da = da + dot(dh, w_cols(D * n, D * (n + 1)), NT)
        finish_backward(m, c, da.astype(bf16))

    def tile(buf, m, n):
        return jnp.concatenate(
            [jnp.concatenate([buf[m, c * 12 + 3 * n + j] for j in range(3)], axis=1) for c in range(2)], axis=0
        )

    def feed_weights_down(m):
        def part(n, _):
            add(m, dv, (n // 2, n % 2), dot(tile(q_buf, m, n), y_buf[m], TN))
            return 0

        lax.fori_loop(0, 4, part, 0)

    def feed_weights_in(m):
        def part(n, _):
            cols = pl.ds(pl.multiple_of(n * D, D), D)
            dh = tile(p_buf, m, n)
            add(m, dw, (slice(None),) * 4 + (cols,), dot(a_buf[m], dh, TN))
            db[:, cols] += jnp.broadcast_to(jnp.sum(dh.astype(f32), axis=0, keepdims=True), (8, D))
            return 0

        lax.fori_loop(0, 4, part, 0)

    def part_of(number):
        if number in AWAY:
            return DOWN_PARTS[number - len(PARTS)], wd
        return PARTS[number], dv if PARTS[number][0] else dw

    def landing(number, step):
        part = part_of(number)[0]
        if not part[0]:
            place = ((0,), (1, 0), (1, 1, 0))[step]
            rest = (slice(None),) * (4 - len(place))
            return wi.at[place + rest + (pl.ds(part[1], part[2]),)]
        half = 0 if number in AWAY else 1
        number = number % len(PARTS)
        q, corner = number // 2, (pl.ds(0, 384), pl.ds(128 * (number % 2), 128))
        place = ((slice(None), half, pl.ds(2 * q, 2)), (0, half, pl.ds(6 + 2 * q, 2)), (1, half, 6 + q))[step]
        return e_buf.at[place + corner]

    def share_of(number, step, flip):
        part, grad = part_of(number)
        order = part[3]
        index = [slice(None)] * 3
        for i in range(step + 1):
            own = bit(me, order[i])
            index[2 - order[i]] = 1 - own if flip and i == step else own
        return grad.at[tuple(index) + (slice(None), pl.ds(part[1], part[2]))]

    def step_copy(number, step):
        return pltpu.make_async_remote_copy(
            src_ref=share_of(number, step, True),
            dst_ref=landing(number, step),
            send_sem=rs_send.at[number, step],
            recv_sem=rs_recv.at[number, step],
            device_id={"dp": peer(part_of(number)[0][3][step])},
            device_id_type=MESH,
        )

    def move_copy(p):
        index = (slice(None),) * 4 + (pl.ds(DOWN_PARTS[p][1], DOWN_PARTS[p][2]),)
        return pltpu.make_async_remote_copy(
            src_ref=dv.at[index],
            dst_ref=wd.at[index],
            send_sem=move_send.at[p],
            recv_sem=move_recv.at[p],
            device_id={"section": sec + 2},
            device_id_type=MESH,
        )

    def back_copy(p):
        return pltpu.make_async_remote_copy(
            src_ref=back.at[p],
            dst_ref=back.at[p],
            send_sem=back_send.at[p],
            recv_sem=back_recv.at[p],
            device_id={"section": sec - 2},
            device_id_type=MESH,
        )

    def result_copy(number):
        down, first, width, _ = PARTS[number]
        cols = pl.ds(first, width)
        if down:
            return pltpu.make_async_copy(xh.at[1, pl.ds(0, 384), cols], out_down.at[0, :, cols], out_sem.at[number])
        rows = pl.ds(96 * (first // D), 96)
        return pltpu.make_async_copy(xh.at[0, rows, pl.ds(first % D, width)], out_in.at[0, :, cols], out_sem.at[number])

    def send_step(number, step):
        if step == 0 and number in AWAY:
            move_copy(number - len(PARTS)).wait_recv()
        step_copy(number, step).start()

    def take_step(number, step):
        step_copy(number, step).wait_recv()
        down, first, width, _ = part_of(number)[0]
        share = share_of(number, step, False)
        total = share[...].astype(f32) + landing(number, step)[...].astype(f32)
        if step < 2:
            share[...] = total.astype(bf16)
            send_step(number, step + 1)
        elif number in AWAY:
            back[number - len(PARTS)] = total
            back_copy(number - len(PARTS)).start()
        elif down:
            xh[1, 0:384, first : first + width] = total
            result_copy(number).start()
        else:
            q, off = first // D, first % D
            xh[0, 96 * q : 96 * (q + 1), off : off + width] = total
            result_copy(number).start()

    def exchange(numbers, ahead, lag, started):
        n = len(numbers)
        for t in range(started, n + ahead + 2 * lag):
            for step in (2, 1, 0):
                i = t - ahead - lag * step
                if 0 <= i < n:
                    take_step(numbers[i], step)
            if t < n:
                send_step(numbers[t], 0)
        for number in numbers:
            for step in range(3):
                step_copy(number, step).wait_send()

    def weights_free():
        for b in range(3):
            pl.semaphore_signal(free_sem.at[b], inc=1, device_id={"dp": peer(b)}, device_id_type=MESH)

    def await_free():
        for b in range(3):
            pl.semaphore_wait(free_sem.at[b], 1)

    late = sec >= 2

    def span(m):
        return jnp.where(late, 0, m), jnp.where(late & (m == 0), 0, m + 1)

    def attention_backward(m):
        lax.fori_loop(0, 2, lambda c, _: (open_back(m, c), 0)[1], 0)
        heads_backward(m)
        lax.fori_loop(0, 2, lambda c, _: (close_back(m, c), 0)[1], 0)

        @pl.when(m == MICRO - 1)
        def _():
            weights_free()

        lax.fori_loop(*span(m), lambda i, _: (attention_weights(i), 0)[1], 0)

    def feed_backward(m):
        early = (sec == 1) & (m == MICRO - 1)
        begin, end = span(m)

        def down_products(begin, end):
            lax.fori_loop(begin, end, lambda i, _: (feed_weights_down(i), 0)[1], 0)

        def rows(c, _):
            feed_open_back(m, c)

            @pl.when(early & (c == 1))
            def _():
                down_products(begin, end)
                for number in DOWN[MOVED:]:
                    send_step(number, 0)
                pl.semaphore_wait(room_sem, 1)
                for p in range(MOVED):
                    move_copy(p).start()

            feed_rows_back(m, c)
            return 0

        lax.fori_loop(0, 2, rows, 0)

        @pl.when(m == MICRO - 1)
        def _():
            weights_free()

        @pl.when((sec == 3) & (m == MICRO - 1))
        def _():
            pl.semaphore_signal(room_sem, inc=1, device_id={"section": 1}, device_id_type=MESH)

        @pl.when(jnp.logical_not(early))
        def _():
            down_products(begin, end)

        @pl.when((sec == 3) & (m == MICRO - 1))
        def _():
            for number in DOWN:
                send_step(number, 0)

        lax.fori_loop(begin, end, lambda i, _: (feed_weights_in(i), 0)[1], 0)

    @pl.when(even)
    def _():
        attention_tables(0)
        for i in range(3):
            b = jnp.broadcast_to(vec_in[:, D * i : D * (i + 1)], (128, D))
            bias_t[D * i : D * (i + 1), :] = b.T

    pl.semaphore_wait(barrier, 3 + GROUP - 1)

    def task(t, _):
        forward = jnp.where(sec == 3, t % 2 == 0, t < 2)
        m = jnp.where(sec == 3, t // 2, t % 2)

        @pl.when(forward & even)
        def _():
            attention_forward(m)

        @pl.when(forward & odd)
        def _():
            feed_forward(m)

        @pl.when(jnp.logical_not(forward) & even)
        def _():
            attention_backward(m)

        @pl.when(jnp.logical_not(forward) & odd)
        def _():
            feed_backward(m)

        return 0

    lax.fori_loop(0, 2 * MICRO, task, 0)

    await_free()

    vec_send[...] = jnp.zeros_like(vec_send)
    outer = jnp.concatenate([acc[0:1, :], acc[1:2, :], acc[2:3, :]], axis=1)
    for j in range(GROUP):
        vec_send[j, 0:1, :] = db[0:1, 384 * j : 384 * (j + 1)]
        vec_send[j, 1:2, 0:288] = outer[:, 288 * j : 288 * (j + 1)]

    def vec_copy(k):
        there = (me + k) % GROUP
        return pltpu.make_async_remote_copy(
            src_ref=vec_send.at[there],
            dst_ref=vec_recv.at[k],
            send_sem=vec_ssem.at[k],
            recv_sem=vec_rsem.at[k],
            device_id={"dp": there * low + dp % low},
            device_id_type=MESH,
        )

    for k in range(1, GROUP):
        vec_copy(k).start()

    zeros = pltpu.make_async_copy(xh.at[1, pl.ds(0, 384)], out_down.at[0], out_sem.at[0])

    @pl.when(even)
    def _():
        xh[1, 0:384, :] = jnp.zeros((384, D), f32)
        zeros.start()

    @pl.when(sec == 1)
    def _():
        exchange(DOWN[MOVED:] + IN, 6, 6, len(DOWN) - MOVED)
        for p in range(MOVED):
            back_copy(p).wait_recv()
            first, width = DOWN_PARTS[p][1], DOWN_PARTS[p][2]
            xh[1, 0:384, first : first + width] = back[p]
            result_copy(p).start()
            move_copy(p).wait_send()

    @pl.when(sec == 3)
    def _():
        exchange(ORDER_3, 6, 6, len(DOWN))
        for p in range(MOVED):
            back_copy(p).wait_send()

    @pl.when(even)
    def _():
        exchange(IN, 4, 4, 0)

    total = vec_send[me]
    for k in range(1, GROUP):
        vec_copy(k).wait_recv()
        total = total + vec_recv[k]
    out_vec_in[...] = total[0:1, :]
    out_vec_out[...] = total[1:2, 0:288]

    for k in range(1, GROUP):
        vec_copy(k).wait_send()

    for m in range(MICRO):
        for c in range(2):

            @pl.when(sec > 0)
            def _():
                backward_copy(m, c).wait_send()
                share_copy(m, c, 0, in_grad, grad_recv).wait_recv()

            @pl.when(sec < 3)
            def _():
                share_copy(m, c, 0, mixed, mix_recv).wait_recv()

            @pl.when(sec == 0)
            def _():
                own_copy(m, c, 0, in_grad).wait()
                for k in range(1, 4):
                    share_copy(m, c, k, in_grad, grad_recv).wait_send()

            @pl.when(sec == 3)
            def _():
                own_copy(m, c, 3, mixed).wait()
                for k in range(3):
                    share_copy(m, c, k, mixed, mix_recv).wait_send()

    for number in IN:
        result_copy(number).wait()

    @pl.when(odd)
    def _():
        for number in DOWN:
            result_copy(number).wait()

    @pl.when(even)
    def _():
        zeros.wait()


def settle(*refs):
    count = (len(refs) - 2) // 3
    given, taken, held = refs[:count], refs[count : 2 * count], refs[2 * count : 3 * count]
    sem_in, sem_out = refs[-2:]
    steps = []
    for i in range(count):
        rows = given[i].shape[1]
        cut = rows // 2 if len(given[i].shape) == 3 else rows
        for k in range(rows // cut):
            index = (slice(None), pl.ds(k * cut, cut))
            n = len(steps)
            steps.append(
                (
                    pltpu.make_async_copy(given[i].at[index], held[i].at[index], sem_in.at[n]),
                    pltpu.make_async_copy(held[i].at[index], taken[i].at[index], sem_out.at[n]),
                )
            )
    for first, _ in steps:
        first.start()
    for first, second in steps:
        first.wait()
        second.start()
    for _, second in steps:
        second.wait()


def on_device(inputs, segment_ids, w_in, w_down, vec_in, vec_out, cotangent):
    world = lax.axis_size("dp")
    low = world // GROUP
    hbm = pl.BlockSpec(memory_space=pl.ANY)
    vmem = pl.BlockSpec(memory_space=pltpu.VMEM)
    V, S = pltpu.VMEM, pltpu.SemaphoreType.DMA
    parts = len(PARTS) + MOVED
    shapes = (
        jax.ShapeDtypeStruct((MICRO, D // 4, BLK), bf16),
        jax.ShapeDtypeStruct((MICRO, D // 4, BLK), bf16),
        jax.ShapeDtypeStruct((1, D // GROUP, FF), f32),
        jax.ShapeDtypeStruct((1, FF // GROUP, D), f32),
        jax.ShapeDtypeStruct((1, FF // GROUP), f32),
        jax.ShapeDtypeStruct((1, 3 * D // GROUP), f32),
    )
    results = pl.pallas_call(
        functools.partial(kernel, low),
        out_shape=shapes,
        in_specs=[hbm, vmem, hbm, hbm, vmem, vmem, hbm],
        out_specs=(hbm, hbm, hbm, hbm, vmem, vmem),
        scratch_shapes=[
            V((2, 2, 2, 96, FF), bf16),
            V((2, 2, 2, 384, D), bf16),
            V((MICRO, BLK, D), bf16),
            V((MICRO, BLK, D), bf16),
            V((MICRO, BLK, D), bf16),
            V((MICRO, 2, 12, 512, 256), bf16),
            V((MICRO, 24, 256, 256), bf16),
            V((MICRO, 24, 256, 256), bf16),
            V((MICRO, BLK, D), f32),
            V((MICRO, BLK, 1), f32),
            V((BLK, BLK), f32),
            V((MICRO, 2, HEAD_DIM // 2, BLK), f32),
            V((MICRO, HEADS, 8, BLK), f32),
            V((3 * D, 128), f32),
            V((2, 2, 2, 96, FF), bf16),
            V((2, 2, 2, 384, D), bf16),
            V((4, MICRO, D // 4, BLK), bf16),
            V((8, D), f32),
            V((8, FF), f32),
            V((GROUP, 8, 384), f32),
            V((GROUP, 8, 384), f32),
            S((2,)),
            S((MICRO,)),
            S((MICRO, 2)),
            S((MICRO, 2)),
            S((MICRO, 2)),
            S((MICRO, 2)),
            S((4, MICRO, 2)),
            S((MICRO, 2)),
            S((MICRO, 2)),
            S((GROUP,)),
            S((GROUP,)),
            pltpu.SemaphoreType.REGULAR((3,)),
            S((parts, 3)),
            S((parts, 3)),
            S((len(PARTS),)),
            V((MOVED, FF // GROUP, 128), f32),
            S((MOVED,)),
            S((MOVED,)),
            S((MOVED,)),
            S((MOVED,)),
            pltpu.SemaphoreType.REGULAR,
        ],
        compiler_params=pltpu.CompilerParams(
            collective_id=0, has_side_effects=True, vmem_limit_bytes=63 * MIB
        ),
    )(inputs, segment_ids, w_in.reshape(2, 2, 2, 96, FF), w_down.reshape(2, 2, 2, 384, D), vec_in, vec_out, cotangent)
    mixed, in_grad, grad_in, grad_down, vec_a, vec_b = pl.pallas_call(
        settle,
        out_shape=shapes,
        in_specs=[hbm] * len(shapes),
        out_specs=(hbm,) * len(shapes),
        scratch_shapes=[V(x.shape, x.dtype) for x in shapes] + [S((10,)), S((10,))],
    )(*results)
    if low > 1:
        groups = [[g * low + i for i in range(low)] for g in range(GROUP)]

        def rest(value):
            return lax.psum_scatter(
                value, "dp", scatter_dimension=1, axis_index_groups=groups, tiled=True
            )

        grad_in, grad_down, vec_a, vec_b = rest(grad_in), rest(grad_down), rest(vec_a), rest(vec_b)
    mixed, in_grad = jnp.swapaxes(mixed, 1, 2), jnp.swapaxes(in_grad, 1, 2)
    return mixed, in_grad, grad_in, grad_down, vec_a, vec_b


def solution(mesh):
    placed = (
        P(None, "dp", None),
        P(None, "dp"),
        P("section", None, None),
        P("section", None, None),
        P("section", None),
        P("section", None),
        P(None, "dp", None),
    )
    return jax.shard_map(
        on_device,
        mesh=mesh,
        in_specs=placed,
        out_specs=(
            P(None, "dp", "section"),
            P(None, "dp", "section"),
            P("section", "dp", None),
            P("section", "dp", None),
            P("section", "dp"),
            P("section", "dp"),
        ),
        check_vma=False,
    )
```

```python
import functools
import math

import jax
import jax.numpy as jnp
from jax import lax
from jax.experimental import pallas as pl
from jax.experimental.pallas import tpu as pltpu
from jax.sharding import PartitionSpec as P

D = 768
HEADS = 12
HEAD_DIM = 64
FF = 3072
BLK = 512
MICRO = 2
CH = 256
GROUP = 8
EPS = 1e-06
NEG = -1e30
K0 = math.sqrt(2.0 / math.pi)
K1 = K0 * 0.044715
LN2 = math.log(2.0)
Q_SCALE = HEAD_DIM**-0.5 / LN2
MIB = 1 << 20
bf16, f32 = jnp.bfloat16, jnp.float32
MESH = pl.DeviceIdType.MESH
NN = (((1,), (0,)), ((), ()))
NT = (((1,), (1,)), ((), ()))
TN = (((0,), (0,)), ((), ()))
TT = (((0,), (1,)), ((), ()))
ORDER_A, ORDER_B = (0, 1, 2), (1, 0, 2)
DOWN_PARTS = [(True, 128 * i, 128, ORDER_A if i % 3 else ORDER_B) for i in range(6)]
IN_PARTS = [(False, 256 * i, 256, ORDER_A if i % 3 else ORDER_B) for i in range(12)]


def dot(a, b, dims):
    return lax.dot_general(a, b, dims, preferred_element_type=f32)


def bit(value, b):
    return (value // (1 << b)) % 2


PARTS = DOWN_PARTS + IN_PARTS
DOWN = list(range(len(DOWN_PARTS)))
IN = list(range(len(DOWN_PARTS), len(PARTS)))
MOVED = 3
AWAY = list(range(len(PARTS), len(PARTS) + MOVED))
ORDER_3 = DOWN + IN[:4] + AWAY[:1] + IN[4:6] + AWAY[1:2] + IN[6:8] + AWAY[2:] + IN[8:]


def kernel(
    low,
    inputs,
    seg,
    w_in,
    w_down,
    vec_in,
    vec_out,
    cotangent,
    mixed,
    in_grad,
    out_in,
    out_down,
    out_vec_in,
    out_vec_out,
    wi,
    wd,
    a_buf,
    d_buf,
    y_buf,
    e_buf,
    q_buf,
    p_buf,
    xh,
    rstd,
    bias,
    rope,
    inv,
    bias_t,
    dw,
    dv,
    split,
    acc,
    db,
    vec_send,
    vec_recv,
    w_sem,
    load_sem,
    fwd_send,
    fwd_recv,
    bwd_send,
    bwd_recv,
    mix_send,
    mix_recv,
    grad_recv,
    vec_ssem,
    vec_rsem,
    free_sem,
    rs_send,
    rs_recv,
    out_sem,
    back,
    move_send,
    move_recv,
    back_send,
    back_recv,
    room_sem,
):
    sec = lax.axis_index("section")
    dp = lax.axis_index("dp")
    me = dp // low
    even = sec % 2 == 0
    odd = sec % 2 == 1

    def peer(b):
        return dp + (1 - 2 * bit(me, b)) * (1 << b) * low

    load_wi = pltpu.make_async_copy(w_in, wi, w_sem.at[0])
    load_wd = pltpu.make_async_copy(w_down, wd, w_sem.at[1])

    def load_a(m):
        return pltpu.make_async_copy(inputs.at[m], a_buf.at[m], load_sem.at[m])

    def load_d(m):
        return pltpu.make_async_copy(cotangent.at[m], d_buf.at[m], load_sem.at[m])

    @pl.when(sec == 0)
    def _():
        for m in range(MICRO):
            load_a(m).start()

    load_wi.start()

    @pl.when(odd)
    def _():
        load_wd.start()

    @pl.when(sec == 3)
    def _():
        for m in range(MICRO):
            load_d(m).start()

    barrier = pltpu.get_barrier_semaphore()
    for k in range(1, 4):
        pl.semaphore_signal(barrier, inc=1, device_id={"section": (sec + k) % 4}, device_id_type=MESH)
    for k in range(1, GROUP):
        pl.semaphore_signal(barrier, inc=1, device_id={"dp": (dp + k * low) % (GROUP * low)}, device_id_type=MESH)

    acc[...] = jnp.zeros_like(acc)
    db[...] = jnp.zeros_like(db)

    def w_cols(first, last):
        return wi[:, :, :, :, first:last].reshape(D, last - first)

    def w_rows(first, last):
        pieces = []
        while first < last:
            j, start = first // 384, first % 384
            stop = min(384, start + last - first)
            pieces.append(wd[j // 4, j // 2 % 2, j % 2, start:stop, :])
            first += stop - start
        return jnp.concatenate(pieces, axis=0)

    def rows_of(c):
        return pl.ds(pl.multiple_of(c * CH, CH), CH)

    def forward_copy(m, c):
        rows = rows_of(c)
        return pltpu.make_async_remote_copy(
            src_ref=y_buf.at[m, rows],
            dst_ref=a_buf.at[m, rows],
            send_sem=fwd_send.at[m, c],
            recv_sem=fwd_recv.at[m, c],
            device_id={"section": sec + 1},
            device_id_type=MESH,
        )

    def backward_copy(m, c):
        rows = rows_of(c)
        return pltpu.make_async_remote_copy(
            src_ref=d_buf.at[m, rows],
            dst_ref=d_buf.at[m, rows],
            send_sem=bwd_send.at[m, c],
            recv_sem=bwd_recv.at[m, c],
            device_id={"section": sec - 1},
            device_id_type=MESH,
        )

    def share_copy(m, c, k, out, recv):
        cols = rows_of(c)
        return pltpu.make_async_remote_copy(
            src_ref=split.at[k, m, :, cols],
            dst_ref=out.at[m, :, cols],
            send_sem=mix_send.at[k, m, c],
            recv_sem=recv.at[m, c],
            device_id={"section": k},
            device_id_type=MESH,
        )

    def own_copy(m, c, k, out):
        cols = rows_of(c)
        return pltpu.make_async_copy(split.at[k, m, :, cols], out.at[m, :, cols], mix_send.at[k, m, c])

    def fill(m, c, value):
        flipped = value.T
        for k in range(4):
            split[k, m, :, rows_of(c)] = flipped[192 * k : 192 * (k + 1), :]

    def share(m, c, own, out, recv):
        for k in range(4):
            if k == own:
                own_copy(m, c, k, out).start()
            else:
                share_copy(m, c, k, out, recv).start()

    def arrive(m, c):
        @pl.when(sec == 0)
        def _():
            @pl.when(c == 0)
            def _():
                load_a(m).wait()

        @pl.when(sec > 0)
        def _():
            forward_copy(m, c).wait_recv()

    def arrive_back(m, c):
        @pl.when(sec == 3)
        def _():
            @pl.when(c == 0)
            def _():
                load_d(m).wait()

        @pl.when(sec < 3)
        def _():
            backward_copy(m, c).wait_recv()

    def finish_forward(m, c, z):
        rows = rows_of(c)
        mean = jnp.mean(z, axis=1, keepdims=True)
        centred = z - mean
        spread = jnp.mean(centred * centred, axis=1, keepdims=True)
        r = lax.rsqrt(spread + EPS)
        unit = centred * r
        xh[m, rows, :] = unit
        rstd[m, rows, :] = r
        y = (unit * vec_out[:, 0:D] + vec_out[:, D : 2 * D]).astype(bf16)

        @pl.when(sec < 3)
        def _():
            y_buf[m, rows, :] = y
            forward_copy(m, c).start()

        @pl.when(sec == 3)
        def _():
            for k in range(4):
                dw[m, c, 0, 0:64, D * k : D * (k + 1)] = y[64 * k : 64 * (k + 1), :]

    def start_backward(m, c):
        rows = rows_of(c)
        dy = d_buf[m, rows, :].astype(f32)
        unit = xh[m, rows, :]
        dyg = dy * vec_out[:, 0:D]
        m1 = jnp.mean(dyg, axis=1, keepdims=True)
        m2 = jnp.mean(dyg * unit, axis=1, keepdims=True)
        dz = rstd[m, rows, :] * (dyg - m1 - unit * m2)
        du = dz.astype(bf16)

        @pl.when(sec < 3)
        def _():
            forward_copy(m, c).wait_send()

        y_buf[m, rows, :] = du
        acc[0:1, :] += jnp.sum(dy * unit, axis=0, keepdims=True)
        acc[1:2, :] += jnp.sum(dy, axis=0, keepdims=True)
        acc[2:3, :] += jnp.sum(du.astype(f32), axis=0, keepdims=True)
        xh[m, rows, :] = dz
        return du

    def finish_backward(m, c, da):
        rows = rows_of(c)

        @pl.when(sec > 0)
        def _():
            d_buf[m, rows, :] = da
            backward_copy(m, c).start()

        @pl.when(sec == 0)
        def _():
            fill(m, c, da)
            share(m, c, 0, in_grad, grad_recv)

    def attention_tables(m):
        row = seg[pl.ds(m, 1), :].astype(f32)
        column = jnp.concatenate([jnp.broadcast_to(row, (128, BLK)).T] * 4, axis=1)
        same = column == jnp.broadcast_to(row, (BLK, BLK))
        bias[...] = jnp.where(same, 0.0, NEG)
        index = lax.broadcasted_iota(jnp.int32, (BLK, BLK), 0).astype(f32)
        opener = jnp.min(jnp.where(same, index, float(BLK)), axis=0, keepdims=True)
        place = lax.broadcasted_iota(jnp.int32, (1, BLK), 1).astype(f32) - opener
        number = lax.broadcasted_iota(jnp.int32, (HEAD_DIM // 2, BLK), 0).astype(f32)
        angle = place * jnp.exp(number * (-2.0 * math.log(10000.0) / HEAD_DIM))
        rope[m, 0] = jnp.cos(angle)
        rope[m, 1] = jnp.sin(angle)

    def project(m, c):
        arrive(m, c)
        rows = rows_of(c)
        a = a_buf[m, rows, :]
        co, si = rope[m, 0, :, rows], rope[m, 1, :, rows]
        for part in range(3):
            p = dot(w_cols(D * part, D * (part + 1)), a, TT)
            b = bias_t[D * part : D * (part + 1), :]
            p = p + jnp.concatenate([b, b], axis=1)
            if part < 2:
                p4 = p.reshape(HEADS, 2, 32, CH)
                t1, t2 = p4[:, 0], p4[:, 1]
                r1 = t1 * co[None] - t2 * si[None]
                r2 = t2 * co[None] + t1 * si[None]
                if part == 0:
                    r1, r2 = r1 * Q_SCALE, r2 * Q_SCALE
                p = jnp.concatenate([r1[:, None], r2[:, None]], axis=1).reshape(D, CH)
            p = p.astype(bf16)
            for j in range(3):
                q_buf[m, (3 * part + j) * 2 + c] = p[256 * j : 256 * (j + 1), :]

    def both(buf, m, block, rows):
        return jnp.concatenate([buf[m, block * 2, rows, :], buf[m, block * 2 + 1, rows, :]], axis=1)

    def heads_forward(m):
        scores, weights = {}, {}
        for t in range(HEADS + 2):
            if t < HEADS:
                g, rows = t // 4, slice(64 * (t % 4), 64 * (t % 4) + 64)
                scores[t] = dot(both(q_buf, m, 3 + g, rows), both(q_buf, m, g, rows), TN) + bias[...]
            h = t - 1
            if 0 <= h < HEADS:
                st = scores.pop(h)
                peak = jnp.max(st, axis=0, keepdims=True)
                e = jnp.exp2(st - peak)
                r = 1.0 / jnp.sum(e, axis=0, keepdims=True)
                e = e.astype(bf16)
                e_buf[m, h // 6, h % 6 * 2] = e[:, 0:256]
                e_buf[m, h // 6, h % 6 * 2 + 1] = e[:, 256:512]
                inv[m, h] = jnp.broadcast_to(r, (8, BLK))
                weights[h] = (e, r)
            h = t - 2
            if 0 <= h:
                e, r = weights.pop(h)
                g, rows = h // 4, slice(64 * (h % 4), 64 * (h % 4) + 64)
                o = (dot(both(q_buf, m, 6 + g, rows), e, NN) * r).astype(bf16)
                q_buf[m, (9 + g) * 2, rows, :] = o[:, 0:256]
                q_buf[m, (9 + g) * 2 + 1, rows, :] = o[:, 256:512]

    def attended(m, c):
        return jnp.concatenate([q_buf[m, (9 + j) * 2 + c] for j in range(3)], axis=0)

    def close(m, c):
        rows = rows_of(c)
        u = dot(attended(m, c), w_cols(3 * D, FF), TN) + vec_out[:, 2 * D :]
        finish_forward(m, c, u + a_buf[m, rows, :].astype(f32))

    def attention_forward(m):
        @pl.when(m == 0)
        def _():
            load_wi.wait()

        @pl.when(m > 0)
        def _():
            attention_tables(m)

        lax.fori_loop(0, 2, lambda c, _: (project(m, c), 0)[1], 0)
        heads_forward(m)
        lax.fori_loop(0, 2, lambda c, _: (close(m, c), 0)[1], 0)

    def open_back(m, c):
        arrive_back(m, c)
        rows = rows_of(c)
        du = start_backward(m, c)
        do = dot(w_cols(3 * D, FF), du, NT).astype(bf16)
        for j in range(3):
            p_buf[m, (9 + j) * 2 + c] = do[256 * j : 256 * (j + 1), :]

    def heads_backward(m):
        co, si = rope[m, 0], rope[m, 1]
        pending = {}
        for t in range(HEADS + 1):
            if t < HEADS:
                g, rows = t // 4, slice(64 * (t % 4), 64 * (t % 4) + 64)
                do = (both(p_buf, m, 9 + g, rows).astype(f32) * inv[m, t, 0:1, :]).astype(bf16)
                o = both(q_buf, m, 9 + g, rows)
                inner = jnp.sum(do.astype(f32) * o.astype(f32), axis=0, keepdims=True)
                pending[t] = (do, inner, dot(both(q_buf, m, 6 + g, rows), do, TN))
            h = t - 1
            if 0 <= h:
                g, rows = h // 4, slice(64 * (h % 4), 64 * (h % 4) + 64)
                do, inner, dr = pending.pop(h)
                e = jnp.concatenate([e_buf[m, h // 6, h % 6 * 2], e_buf[m, h // 6, h % 6 * 2 + 1]], axis=1)
                ds = e * (dr - inner).astype(bf16)
                dvv = dot(do, e, NT)
                dq = dot(both(q_buf, m, 3 + g, rows), ds, NN)
                dk = dot(both(q_buf, m, g, rows), ds, NT)
                for part, x in ((0, dq * 0.125), (1, dk * LN2)):
                    t1, t2 = x[:32], x[32:]
                    x = jnp.concatenate([t1 * co + t2 * si, t2 * co - t1 * si], axis=0).astype(bf16)
                    p_buf[m, (3 * part + g) * 2, rows, :] = x[:, 0:256]
                    p_buf[m, (3 * part + g) * 2 + 1, rows, :] = x[:, 256:512]
                dvv = dvv.astype(bf16)
                p_buf[m, (6 + g) * 2, rows, :] = dvv[:, 0:256]
                p_buf[m, (6 + g) * 2 + 1, rows, :] = dvv[:, 256:512]

    def close_back(m, c):
        rows = rows_of(c)
        dp_t = jnp.concatenate([p_buf[m, fb * 2 + c] for fb in range(9)], axis=0)
        da = dot(dp_t, w_cols(0, 3 * D), TT) + xh[m, rows, :]
        finish_backward(m, c, da.astype(bf16))

    def add(m, ref, index, new):
        held = ref[index]
        new = new.reshape(held.shape)
        ref[index] = jnp.where(m == 0, new, held.astype(f32) + new).astype(bf16)

    def attention_weights(m):
        a_t = a_buf[m].T

        def part(n, _):
            cols = pl.ds(pl.multiple_of(n * D, D), D)
            d = jnp.concatenate(
                [jnp.concatenate([p_buf[m, (3 * n + j) * 2], p_buf[m, (3 * n + j) * 2 + 1]], axis=1) for j in range(3)],
                axis=0,
            )
            add(m, dw, (slice(None),) * 4 + (cols,), dot(a_t, d, NT))
            db[:, cols] += dot(jnp.ones((8, BLK), bf16), d, NT)
            return 0

        lax.fori_loop(0, 3, part, 0)
        o = jnp.concatenate([attended(m, 0), attended(m, 1)], axis=1)
        add(m, dw, (slice(None),) * 4 + (slice(3 * D, FF),), dot(o, y_buf[m], NN))

    def feed_rows(m, c):
        arrive(m, c)
        rows = rows_of(c)
        a = a_buf[m, rows, :]
        u, hidden = None, {}
        for t in range(8):
            if t < 6:
                cols = slice(512 * t, 512 * (t + 1))
                hidden[t] = dot(a, w_cols(512 * t, 512 * (t + 1)), NN) + vec_in[:, cols]
            n = t - 2
            if n >= 0:
                h = hidden.pop(n)
                h2 = h * h
                s = 0.5 * jnp.tanh(h * (K0 + K1 * h2)) + 0.5
                g = h * s
                slope = (s + g * (1.0 - s) * (2.0 * K0 + 6.0 * K1 * h2)).astype(bf16)
                g = g.astype(bf16)
                for j in range(2):
                    q_buf[m, c * 12 + 2 * n + j] = g[:, 256 * j : 256 * (j + 1)]
                    e_buf[m, 0, 2 * n + j, rows, :] = slope[:, 256 * j : 256 * (j + 1)]
                x = dot(g, w_rows(512 * n, 512 * (n + 1)), NN)
                u = x if u is None else u + x
        finish_forward(m, c, u + vec_out[:, 2 * D :] + a.astype(f32))

    def feed_forward(m):
        @pl.when(m == 0)
        def _():
            load_wi.wait()
            load_wd.wait()

        lax.fori_loop(0, 2, lambda c, _: (feed_rows(m, c), 0)[1], 0)

    def feed_open_back(m, c):
        arrive_back(m, c)
        start_backward(m, c)

    def feed_rows_back(m, c):
        rows = rows_of(c)
        du = y_buf[m, rows, :]
        da, grads = xh[m, rows, :], {}
        for t in range(5):
            if t < 4:
                grads[t] = dot(du, w_rows(D * t, D * (t + 1)), NT)
            n = t - 1
            if n >= 0:
                slope = jnp.concatenate([e_buf[m, 0, 3 * n + j, rows, :] for j in range(3)], axis=1)
                dh = (grads.pop(n) * slope.astype(f32)).astype(bf16)
                for j in range(3):
                    p_buf[m, c * 12 + 3 * n + j] = dh[:, 256 * j : 256 * (j + 1)]
                da = da + dot(dh, w_cols(D * n, D * (n + 1)), NT)
        finish_backward(m, c, da.astype(bf16))

    def tile(buf, m, n):
        return jnp.concatenate(
            [jnp.concatenate([buf[m, c * 12 + 3 * n + j] for j in range(3)], axis=1) for c in range(2)], axis=0
        )

    def feed_weights_down(m):
        def part(n, _):
            add(m, dv, (n // 2, n % 2), dot(tile(q_buf, m, n), y_buf[m], TN))
            return 0

        lax.fori_loop(0, 4, part, 0)

    def feed_weights_in(m):
        def part(n, _):
            cols = pl.ds(pl.multiple_of(n * D, D), D)
            dh = tile(p_buf, m, n)
            add(m, dw, (slice(None),) * 4 + (cols,), dot(a_buf[m], dh, TN))
            db[:, cols] += jnp.broadcast_to(jnp.sum(dh.astype(f32), axis=0, keepdims=True), (8, D))
            return 0

        lax.fori_loop(0, 4, part, 0)

    def part_of(number):
        if number in AWAY:
            return DOWN_PARTS[number - len(PARTS)], wd
        return PARTS[number], dv if PARTS[number][0] else dw

    def landing(number, step):
        part = part_of(number)[0]
        if not part[0]:
            place = ((0,), (1, 0), (1, 1, 0))[step]
            rest = (slice(None),) * (4 - len(place))
            return wi.at[place + rest + (pl.ds(part[1], part[2]),)]
        half = 0 if number in AWAY else 1
        number = number % len(PARTS)
        q, corner = number // 2, (pl.ds(0, 384), pl.ds(128 * (number % 2), 128))
        place = ((slice(None), half, pl.ds(2 * q, 2)), (0, half, pl.ds(6 + 2 * q, 2)), (1, half, 6 + q))[step]
        return e_buf.at[place + corner]

    def share_of(number, step, flip):
        part, grad = part_of(number)
        order = part[3]
        index = [slice(None)] * 3
        for i in range(step + 1):
            own = bit(me, order[i])
            index[2 - order[i]] = 1 - own if flip and i == step else own
        return grad.at[tuple(index) + (slice(None), pl.ds(part[1], part[2]))]

    def step_copy(number, step):
        return pltpu.make_async_remote_copy(
            src_ref=share_of(number, step, True),
            dst_ref=landing(number, step),
            send_sem=rs_send.at[number, step],
            recv_sem=rs_recv.at[number, step],
            device_id={"dp": peer(part_of(number)[0][3][step])},
            device_id_type=MESH,
        )

    def move_copy(p):
        index = (slice(None),) * 4 + (pl.ds(DOWN_PARTS[p][1], DOWN_PARTS[p][2]),)
        return pltpu.make_async_remote_copy(
            src_ref=dv.at[index],
            dst_ref=wd.at[index],
            send_sem=move_send.at[p],
            recv_sem=move_recv.at[p],
            device_id={"section": sec + 2},
            device_id_type=MESH,
        )

    def back_copy(p):
        return pltpu.make_async_remote_copy(
            src_ref=back.at[p],
            dst_ref=back.at[p],
            send_sem=back_send.at[p],
            recv_sem=back_recv.at[p],
            device_id={"section": sec - 2},
            device_id_type=MESH,
        )

    def result_copy(number):
        down, first, width, _ = PARTS[number]
        cols = pl.ds(first, width)
        if down:
            return pltpu.make_async_copy(xh.at[1, pl.ds(0, 384), cols], out_down.at[0, :, cols], out_sem.at[number])
        rows = pl.ds(96 * (first // D), 96)
        return pltpu.make_async_copy(xh.at[0, rows, pl.ds(first % D, width)], out_in.at[0, :, cols], out_sem.at[number])

    def send_step(number, step):
        if step == 0 and number in AWAY:
            move_copy(number - len(PARTS)).wait_recv()
        step_copy(number, step).start()

    def take_step(number, step):
        step_copy(number, step).wait_recv()
        down, first, width, _ = part_of(number)[0]
        share = share_of(number, step, False)
        total = share[...].astype(f32) + landing(number, step)[...].astype(f32)
        if step < 2:
            share[...] = total.astype(bf16)
            send_step(number, step + 1)
        elif number in AWAY:
            back[number - len(PARTS)] = total
            back_copy(number - len(PARTS)).start()
        elif down:
            xh[1, 0:384, first : first + width] = total
            result_copy(number).start()
        else:
            q, off = first // D, first % D
            xh[0, 96 * q : 96 * (q + 1), off : off + width] = total
            result_copy(number).start()

    def exchange(numbers, ahead, lag, started, also=None):
        n = len(numbers)
        for t in range(started, n + ahead + 2 * lag):
            for step in (2, 1, 0):
                i = t - ahead - lag * step
                if 0 <= i < n:
                    take_step(numbers[i], step)
            if t < n:
                send_step(numbers[t], 0)
            if also is not None and t == started + 7:
                also()
        for number in numbers:
            for step in range(3):
                step_copy(number, step).wait_send()

    def weights_free():
        for b in range(3):
            pl.semaphore_signal(free_sem.at[b], inc=1, device_id={"dp": peer(b)}, device_id_type=MESH)

    def await_free():
        for b in range(3):
            pl.semaphore_wait(free_sem.at[b], 1)

    late = sec >= 2

    def span(m):
        return jnp.where(late, 0, m), jnp.where(late & (m == 0), 0, m + 1)

    def attention_backward(m):
        lax.fori_loop(0, 2, lambda c, _: (open_back(m, c), 0)[1], 0)
        heads_backward(m)
        lax.fori_loop(0, 2, lambda c, _: (close_back(m, c), 0)[1], 0)

        @pl.when(m == MICRO - 1)
        def _():
            weights_free()

        lax.fori_loop(*span(m), lambda i, _: (attention_weights(i), 0)[1], 0)

    def feed_backward(m):
        early = (sec == 1) & (m == MICRO - 1)
        begin, end = span(m)

        def down_products(begin, end):
            lax.fori_loop(begin, end, lambda i, _: (feed_weights_down(i), 0)[1], 0)

        def rows(c, _):
            feed_open_back(m, c)

            @pl.when(early & (c == 1))
            def _():
                down_products(begin, end)
                for number in DOWN[MOVED:]:
                    send_step(number, 0)
                pl.semaphore_wait(room_sem, 1)
                for p in range(MOVED):
                    move_copy(p).start()

            feed_rows_back(m, c)
            return 0

        lax.fori_loop(0, 2, rows, 0)

        @pl.when(m == MICRO - 1)
        def _():
            weights_free()

        @pl.when((sec == 3) & (m == MICRO - 1))
        def _():
            pl.semaphore_signal(room_sem, inc=1, device_id={"section": 1}, device_id_type=MESH)

        @pl.when(jnp.logical_not(early))
        def _():
            down_products(begin, end)

        @pl.when((sec == 3) & (m == MICRO - 1))
        def _():
            for number in DOWN:
                send_step(number, 0)

            def give(i, _):
                y = [dw[i // 2, i % 2, 0, 0:64, D * k : D * (k + 1)] for k in range(4)]
                fill(i // 2, i % 2, jnp.concatenate(y, axis=0))
                return 0

            lax.fori_loop(0, 4, give, 0)

        lax.fori_loop(begin, end, lambda i, _: (feed_weights_in(i), 0)[1], 0)

    @pl.when(even)
    def _():
        attention_tables(0)
        for i in range(3):
            b = jnp.broadcast_to(vec_in[:, D * i : D * (i + 1)], (128, D))
            bias_t[D * i : D * (i + 1), :] = b.T

    pl.semaphore_wait(barrier, 3 + GROUP - 1)

    def task(t, _):
        forward = jnp.where(sec == 3, t % 2 == 0, t < 2)
        m = jnp.where(sec == 3, t // 2, t % 2)

        @pl.when(forward & even)
        def _():
            attention_forward(m)

        @pl.when(forward & odd)
        def _():
            feed_forward(m)

        @pl.when(jnp.logical_not(forward) & even)
        def _():
            attention_backward(m)

        @pl.when(jnp.logical_not(forward) & odd)
        def _():
            feed_backward(m)

        return 0

    lax.fori_loop(0, 2 * MICRO, task, 0)

    await_free()

    vec_send[...] = jnp.zeros_like(vec_send)
    outer = jnp.concatenate([acc[0:1, :], acc[1:2, :], acc[2:3, :]], axis=1)
    for j in range(GROUP):
        vec_send[j, 0:1, :] = db[0:1, 384 * j : 384 * (j + 1)]
        vec_send[j, 1:2, 0:288] = outer[:, 288 * j : 288 * (j + 1)]

    def vec_copy(k):
        there = (me + k) % GROUP
        return pltpu.make_async_remote_copy(
            src_ref=vec_send.at[there],
            dst_ref=vec_recv.at[k],
            send_sem=vec_ssem.at[k],
            recv_sem=vec_rsem.at[k],
            device_id={"dp": there * low + dp % low},
            device_id_type=MESH,
        )

    for k in range(1, GROUP):
        vec_copy(k).start()

    zeros = pltpu.make_async_copy(xh.at[1, pl.ds(0, 384)], out_down.at[0], out_sem.at[0])

    @pl.when(even)
    def _():
        xh[1, 0:384, :] = jnp.zeros((384, D), f32)
        zeros.start()

    @pl.when(sec == 1)
    def _():
        exchange(DOWN[MOVED:] + IN, 6, 6, len(DOWN) - MOVED)
        for p in range(MOVED):
            back_copy(p).wait_recv()
            first, width = DOWN_PARTS[p][1], DOWN_PARTS[p][2]
            xh[1, 0:384, first : first + width] = back[p]
            result_copy(p).start()
            move_copy(p).wait_send()

    @pl.when(sec == 3)
    def _():
        def shares():
            for m in range(MICRO):
                for c in range(2):
                    share(m, c, 3, mixed, mix_recv)

        exchange(ORDER_3, 6, 6, len(DOWN), shares)
        for p in range(MOVED):
            back_copy(p).wait_send()

    @pl.when(even)
    def _():
        exchange(IN, 5, 5, 0)

    total = vec_send[me]
    for k in range(1, GROUP):
        vec_copy(k).wait_recv()
        total = total + vec_recv[k]
    out_vec_in[...] = total[0:1, :]
    out_vec_out[...] = total[1:2, 0:288]

    for k in range(1, GROUP):
        vec_copy(k).wait_send()

    for m in range(MICRO):
        for c in range(2):

            @pl.when(sec > 0)
            def _():
                backward_copy(m, c).wait_send()
                share_copy(m, c, 0, in_grad, grad_recv).wait_recv()

            @pl.when(sec < 3)
            def _():
                share_copy(m, c, 0, mixed, mix_recv).wait_recv()

            @pl.when(sec == 0)
            def _():
                own_copy(m, c, 0, in_grad).wait()
                for k in range(1, 4):
                    share_copy(m, c, k, in_grad, grad_recv).wait_send()

            @pl.when(sec == 3)
            def _():
                own_copy(m, c, 3, mixed).wait()
                for k in range(3):
                    share_copy(m, c, k, mixed, mix_recv).wait_send()

    for number in IN:
        result_copy(number).wait()

    @pl.when(odd)
    def _():
        for number in DOWN:
            result_copy(number).wait()

    @pl.when(even)
    def _():
        zeros.wait()


def settle(*refs):
    count = (len(refs) - 2) // 3
    given, taken, held = refs[:count], refs[count : 2 * count], refs[2 * count : 3 * count]
    sem_in, sem_out = refs[-2:]
    steps = []
    for i in range(count):
        rows = given[i].shape[1]
        cut = rows // 2 if len(given[i].shape) == 3 else rows
        for k in range(rows // cut):
            index = (slice(None), pl.ds(k * cut, cut))
            n = len(steps)
            steps.append(
                (
                    pltpu.make_async_copy(given[i].at[index], held[i].at[index], sem_in.at[n]),
                    pltpu.make_async_copy(held[i].at[index], taken[i].at[index], sem_out.at[n]),
                )
            )
    for first, _ in steps:
        first.start()
    for first, second in steps:
        first.wait()
        second.start()
    for _, second in steps:
        second.wait()


def on_device(inputs, segment_ids, w_in, w_down, vec_in, vec_out, cotangent):
    world = lax.axis_size("dp")
    low = world // GROUP
    hbm = pl.BlockSpec(memory_space=pl.ANY)
    vmem = pl.BlockSpec(memory_space=pltpu.VMEM)
    V, S = pltpu.VMEM, pltpu.SemaphoreType.DMA
    parts = len(PARTS) + MOVED
    shapes = (
        jax.ShapeDtypeStruct((MICRO, D // 4, BLK), bf16),
        jax.ShapeDtypeStruct((MICRO, D // 4, BLK), bf16),
        jax.ShapeDtypeStruct((1, D // GROUP, FF), f32),
        jax.ShapeDtypeStruct((1, FF // GROUP, D), f32),
        jax.ShapeDtypeStruct((1, FF // GROUP), f32),
        jax.ShapeDtypeStruct((1, 3 * D // GROUP), f32),
    )
    results = pl.pallas_call(
        functools.partial(kernel, low),
        out_shape=shapes,
        in_specs=[hbm, vmem, hbm, hbm, vmem, vmem, hbm],
        out_specs=(hbm, hbm, hbm, hbm, vmem, vmem),
        scratch_shapes=[
            V((2, 2, 2, 96, FF), bf16),
            V((2, 2, 2, 384, D), bf16),
            V((MICRO, BLK, D), bf16),
            V((MICRO, BLK, D), bf16),
            V((MICRO, BLK, D), bf16),
            V((MICRO, 2, 12, 512, 256), bf16),
            V((MICRO, 24, 256, 256), bf16),
            V((MICRO, 24, 256, 256), bf16),
            V((MICRO, BLK, D), f32),
            V((MICRO, BLK, 1), f32),
            V((BLK, BLK), f32),
            V((MICRO, 2, HEAD_DIM // 2, BLK), f32),
            V((MICRO, HEADS, 8, BLK), f32),
            V((3 * D, 128), f32),
            V((2, 2, 2, 96, FF), bf16),
            V((2, 2, 2, 384, D), bf16),
            V((4, MICRO, D // 4, BLK), bf16),
            V((8, D), f32),
            V((8, FF), f32),
            V((GROUP, 8, 384), f32),
            V((GROUP, 8, 384), f32),
            S((2,)),
            S((MICRO,)),
            S((MICRO, 2)),
            S((MICRO, 2)),
            S((MICRO, 2)),
            S((MICRO, 2)),
            S((4, MICRO, 2)),
            S((MICRO, 2)),
            S((MICRO, 2)),
            S((GROUP,)),
            S((GROUP,)),
            pltpu.SemaphoreType.REGULAR((3,)),
            S((parts, 3)),
            S((parts, 3)),
            S((len(PARTS),)),
            V((MOVED, FF // GROUP, 128), f32),
            S((MOVED,)),
            S((MOVED,)),
            S((MOVED,)),
            S((MOVED,)),
            pltpu.SemaphoreType.REGULAR,
        ],
        compiler_params=pltpu.CompilerParams(
            collective_id=0, has_side_effects=True, vmem_limit_bytes=63 * MIB
        ),
    )(inputs, segment_ids, w_in.reshape(2, 2, 2, 96, FF), w_down.reshape(2, 2, 2, 384, D), vec_in, vec_out, cotangent)
    mixed, in_grad, grad_in, grad_down, vec_a, vec_b = pl.pallas_call(
        settle,
        out_shape=shapes,
        in_specs=[hbm] * len(shapes),
        out_specs=(hbm,) * len(shapes),
        scratch_shapes=[V(x.shape, x.dtype) for x in shapes] + [S((10,)), S((10,))],
    )(*results)
    if low > 1:
        groups = [[g * low + i for i in range(low)] for g in range(GROUP)]

        def rest(value):
            return lax.psum_scatter(
                value, "dp", scatter_dimension=1, axis_index_groups=groups, tiled=True
            )

        grad_in, grad_down, vec_a, vec_b = rest(grad_in), rest(grad_down), rest(vec_a), rest(vec_b)
    mixed, in_grad = jnp.swapaxes(mixed, 1, 2), jnp.swapaxes(in_grad, 1, 2)
    return mixed, in_grad, grad_in, grad_down, vec_a, vec_b


def solution(mesh):
    placed = (
        P(None, "dp", None),
        P(None, "dp"),
        P("section", None, None),
        P("section", None, None),
        P("section", None),
        P("section", None),
        P(None, "dp", None),
    )
    return jax.shard_map(
        on_device,
        mesh=mesh,
        in_specs=placed,
        out_specs=(
            P(None, "dp", "section"),
            P(None, "dp", "section"),
            P("section", "dp", None),
            P("section", "dp", None),
            P("section", "dp"),
            P("section", "dp"),
        ),
        check_vma=False,
    )
```

```python
import functools
import math

import jax
import jax.numpy as jnp
from jax import lax
from jax.experimental import pallas as pl
from jax.experimental.pallas import tpu as pltpu
from jax.sharding import PartitionSpec as P

D = 768
HEADS = 12
HEAD_DIM = 64
FF = 3072
BLK = 512
MICRO = 2
CH = 256
GROUP = 8
EPS = 1e-06
NEG = -1e30
K0 = math.sqrt(2.0 / math.pi)
K1 = K0 * 0.044715
LN2 = math.log(2.0)
Q_SCALE = HEAD_DIM**-0.5 / LN2
MIB = 1 << 20
bf16, f32 = jnp.bfloat16, jnp.float32
MESH = pl.DeviceIdType.MESH
NN = (((1,), (0,)), ((), ()))
NT = (((1,), (1,)), ((), ()))
TN = (((0,), (0,)), ((), ()))
TT = (((0,), (1,)), ((), ()))
ORDER_A, ORDER_B = (0, 1, 2), (1, 0, 2)
DOWN_PARTS = [(True, 128 * i, 128, ORDER_A if i % 3 else ORDER_B) for i in range(6)]
IN_PARTS = [(False, 256 * i, 256, ORDER_A if i % 3 else ORDER_B) for i in range(12)]


def dot(a, b, dims):
    return lax.dot_general(a, b, dims, preferred_element_type=f32)


def bit(value, b):
    return (value // (1 << b)) % 2


PARTS = DOWN_PARTS + IN_PARTS
DOWN = list(range(len(DOWN_PARTS)))
IN = list(range(len(DOWN_PARTS), len(PARTS)))
MOVED = 3
AWAY = list(range(len(PARTS), len(PARTS) + MOVED))
ORDER_3 = DOWN + IN[:4] + AWAY[:1] + IN[4:6] + AWAY[1:2] + IN[6:8] + AWAY[2:] + IN[8:]


def kernel(
    low,
    inputs,
    seg,
    w_in,
    w_down,
    vec_in,
    vec_out,
    cotangent,
    mixed,
    in_grad,
    out_in,
    out_down,
    out_vec_in,
    out_vec_out,
    wi,
    wd,
    a_buf,
    d_buf,
    y_buf,
    e_buf,
    q_buf,
    p_buf,
    xh,
    rstd,
    bias,
    rope,
    inv,
    bias_t,
    dw,
    dv,
    split,
    acc,
    db,
    vec_send,
    vec_recv,
    w_sem,
    load_sem,
    fwd_send,
    fwd_recv,
    bwd_send,
    bwd_recv,
    mix_send,
    mix_recv,
    grad_recv,
    vec_ssem,
    vec_rsem,
    free_sem,
    rs_send,
    rs_recv,
    out_sem,
    back,
    move_send,
    move_recv,
    back_send,
    back_recv,
    room_sem,
):
    sec = lax.axis_index("section")
    dp = lax.axis_index("dp")
    me = dp // low
    even = sec % 2 == 0
    odd = sec % 2 == 1

    def peer(b):
        return dp + (1 - 2 * bit(me, b)) * (1 << b) * low

    def load_cols(first, last, n):
        cols = (slice(None),) * 4 + (pl.ds(first, last - first),)
        return pltpu.make_async_copy(w_in.at[cols], wi.at[cols], w_sem.at[n])

    load_wi, load_wo = load_cols(0, 3 * D, 0), load_cols(3 * D, FF, 2)
    load_wd = pltpu.make_async_copy(w_down, wd, w_sem.at[1])

    def load_a(m):
        return pltpu.make_async_copy(inputs.at[m], a_buf.at[m], load_sem.at[m])

    def load_d(m):
        return pltpu.make_async_copy(cotangent.at[m], d_buf.at[m], load_sem.at[m])

    @pl.when(sec == 0)
    def _():
        for m in range(MICRO):
            load_a(m).start()

    load_wi.start()
    load_wo.start()

    @pl.when(odd)
    def _():
        load_wd.start()

    @pl.when(sec == 3)
    def _():
        for m in range(MICRO):
            load_d(m).start()

    barrier = pltpu.get_barrier_semaphore()
    for k in range(1, 4):
        pl.semaphore_signal(barrier, inc=1, device_id={"section": (sec + k) % 4}, device_id_type=MESH)
    for k in range(1, GROUP):
        pl.semaphore_signal(barrier, inc=1, device_id={"dp": (dp + k * low) % (GROUP * low)}, device_id_type=MESH)

    acc[...] = jnp.zeros_like(acc)
    db[...] = jnp.zeros_like(db)

    def w_cols(first, last):
        return wi[:, :, :, :, first:last].reshape(D, last - first)

    def w_rows(first, last):
        pieces = []
        while first < last:
            j, start = first // 384, first % 384
            stop = min(384, start + last - first)
            pieces.append(wd[j // 4, j // 2 % 2, j % 2, start:stop, :])
            first += stop - start
        return jnp.concatenate(pieces, axis=0)

    def rows_of(c):
        return pl.ds(pl.multiple_of(c * CH, CH), CH)

    def forward_copy(m, c):
        rows = rows_of(c)
        return pltpu.make_async_remote_copy(
            src_ref=y_buf.at[m, rows],
            dst_ref=a_buf.at[m, rows],
            send_sem=fwd_send.at[m, c],
            recv_sem=fwd_recv.at[m, c],
            device_id={"section": sec + 1},
            device_id_type=MESH,
        )

    def backward_copy(m, c):
        rows = rows_of(c)
        return pltpu.make_async_remote_copy(
            src_ref=d_buf.at[m, rows],
            dst_ref=d_buf.at[m, rows],
            send_sem=bwd_send.at[m, c],
            recv_sem=bwd_recv.at[m, c],
            device_id={"section": sec - 1},
            device_id_type=MESH,
        )

    def share_copy(m, c, k, out, recv):
        cols = rows_of(c)
        return pltpu.make_async_remote_copy(
            src_ref=split.at[k, m, :, cols],
            dst_ref=out.at[m, :, cols],
            send_sem=mix_send.at[k, m, c],
            recv_sem=recv.at[m, c],
            device_id={"section": k},
            device_id_type=MESH,
        )

    def own_copy(m, c, k, out):
        cols = rows_of(c)
        return pltpu.make_async_copy(split.at[k, m, :, cols], out.at[m, :, cols], mix_send.at[k, m, c])

    def fill(m, c, value):
        flipped = value.T
        for k in range(4):
            split[k, m, :, rows_of(c)] = flipped[192 * k : 192 * (k + 1), :]

    def share(m, c, own, out, recv):
        for k in range(4):
            if k == own:
                own_copy(m, c, k, out).start()
            else:
                share_copy(m, c, k, out, recv).start()

    def arrive(m, c):
        @pl.when(sec == 0)
        def _():
            @pl.when(c == 0)
            def _():
                load_a(m).wait()

        @pl.when(sec > 0)
        def _():
            forward_copy(m, c).wait_recv()

    def arrive_back(m, c):
        @pl.when(sec == 3)
        def _():
            @pl.when(c == 0)
            def _():
                load_d(m).wait()

        @pl.when(sec < 3)
        def _():
            backward_copy(m, c).wait_recv()

    def finish_forward(m, c, z):
        rows = rows_of(c)
        mean = jnp.mean(z, axis=1, keepdims=True)
        centred = z - mean
        spread = jnp.mean(centred * centred, axis=1, keepdims=True)
        r = lax.rsqrt(spread + EPS)
        unit = centred * r
        xh[m, rows, :] = unit
        rstd[m, rows, :] = r
        y = (unit * vec_out[:, 0:D] + vec_out[:, D : 2 * D]).astype(bf16)

        @pl.when(sec < 3)
        def _():
            y_buf[m, rows, :] = y
            forward_copy(m, c).start()

        @pl.when(sec == 3)
        def _():
            for k in range(4):
                dw[m, c, 0, 0:64, D * k : D * (k + 1)] = y[64 * k : 64 * (k + 1), :]

    def start_backward(m, c):
        rows = rows_of(c)
        dy = d_buf[m, rows, :].astype(f32)
        unit = xh[m, rows, :]
        dyg = dy * vec_out[:, 0:D]
        m1 = jnp.mean(dyg, axis=1, keepdims=True)
        m2 = jnp.mean(dyg * unit, axis=1, keepdims=True)
        dz = rstd[m, rows, :] * (dyg - m1 - unit * m2)
        du = dz.astype(bf16)

        @pl.when(sec < 3)
        def _():
            forward_copy(m, c).wait_send()

        y_buf[m, rows, :] = du
        acc[0:1, :] += jnp.sum(dy * unit, axis=0, keepdims=True)
        acc[1:2, :] += jnp.sum(dy, axis=0, keepdims=True)
        acc[2:3, :] += jnp.sum(du.astype(f32), axis=0, keepdims=True)
        xh[m, rows, :] = dz
        return du

    def finish_backward(m, c, da):
        rows = rows_of(c)

        @pl.when(sec > 0)
        def _():
            d_buf[m, rows, :] = da
            backward_copy(m, c).start()

        @pl.when(sec == 0)
        def _():
            fill(m, c, da)
            share(m, c, 0, in_grad, grad_recv)

    def attention_tables(m):
        row = seg[pl.ds(m, 1), :].astype(f32)
        column = jnp.concatenate([jnp.broadcast_to(row, (128, BLK)).T] * 4, axis=1)
        same = column == jnp.broadcast_to(row, (BLK, BLK))
        bias[...] = jnp.where(same, 0.0, NEG)
        index = lax.broadcasted_iota(jnp.int32, (BLK, BLK), 0).astype(f32)
        opener = jnp.min(jnp.where(same, index, float(BLK)), axis=0, keepdims=True)
        place = lax.broadcasted_iota(jnp.int32, (1, BLK), 1).astype(f32) - opener
        number = lax.broadcasted_iota(jnp.int32, (HEAD_DIM // 2, BLK), 0).astype(f32)
        angle = place * jnp.exp(number * (-2.0 * math.log(10000.0) / HEAD_DIM))
        rope[m, 0] = jnp.cos(angle)
        rope[m, 1] = jnp.sin(angle)

    def project(m, c):
        arrive(m, c)
        rows = rows_of(c)
        a = a_buf[m, rows, :]
        co, si = rope[m, 0, :, rows], rope[m, 1, :, rows]
        for part in range(3):
            p = dot(w_cols(D * part, D * (part + 1)), a, TT)
            b = bias_t[D * part : D * (part + 1), :]
            p = p + jnp.concatenate([b, b], axis=1)
            if part < 2:
                p4 = p.reshape(HEADS, 2, 32, CH)
                t1, t2 = p4[:, 0], p4[:, 1]
                r1 = t1 * co[None] - t2 * si[None]
                r2 = t2 * co[None] + t1 * si[None]
                if part == 0:
                    r1, r2 = r1 * Q_SCALE, r2 * Q_SCALE
                p = jnp.concatenate([r1[:, None], r2[:, None]], axis=1).reshape(D, CH)
            p = p.astype(bf16)
            for j in range(3):
                q_buf[m, (3 * part + j) * 2 + c] = p[256 * j : 256 * (j + 1), :]

    def both(buf, m, block, rows):
        return jnp.concatenate([buf[m, block * 2, rows, :], buf[m, block * 2 + 1, rows, :]], axis=1)

    def heads_forward(m):
        scores, weights = {}, {}
        for t in range(HEADS + 2):
            if t < HEADS:
                g, rows = t // 4, slice(64 * (t % 4), 64 * (t % 4) + 64)
                scores[t] = dot(both(q_buf, m, 3 + g, rows), both(q_buf, m, g, rows), TN) + bias[...]
            h = t - 1
            if 0 <= h < HEADS:
                st = scores.pop(h)
                peak = jnp.max(st, axis=0, keepdims=True)
                e = jnp.exp2(st - peak)
                r = 1.0 / jnp.sum(e, axis=0, keepdims=True)
                e = e.astype(bf16)
                e_buf[m, h // 6, h % 6 * 2] = e[:, 0:256]
                e_buf[m, h // 6, h % 6 * 2 + 1] = e[:, 256:512]
                inv[m, h] = jnp.broadcast_to(r, (8, BLK))
                weights[h] = (e, r)
            h = t - 2
            if 0 <= h:
                e, r = weights.pop(h)
                g, rows = h // 4, slice(64 * (h % 4), 64 * (h % 4) + 64)
                o = (dot(both(q_buf, m, 6 + g, rows), e, NN) * r).astype(bf16)
                q_buf[m, (9 + g) * 2, rows, :] = o[:, 0:256]
                q_buf[m, (9 + g) * 2 + 1, rows, :] = o[:, 256:512]

    def attended(m, c):
        return jnp.concatenate([q_buf[m, (9 + j) * 2 + c] for j in range(3)], axis=0)

    def close(m, c):
        rows = rows_of(c)
        u = dot(attended(m, c), w_cols(3 * D, FF), TN) + vec_out[:, 2 * D :]
        finish_forward(m, c, u + a_buf[m, rows, :].astype(f32))

    def attention_forward(m):
        @pl.when(m == 0)
        def _():
            load_wi.wait()

        @pl.when(m > 0)
        def _():
            attention_tables(m)

        lax.fori_loop(0, 2, lambda c, _: (project(m, c), 0)[1], 0)
        heads_forward(m)

        @pl.when(m == 0)
        def _():
            load_wo.wait()

        lax.fori_loop(0, 2, lambda c, _: (close(m, c), 0)[1], 0)

    def open_back(m, c):
        arrive_back(m, c)
        rows = rows_of(c)
        du = start_backward(m, c)
        do = dot(w_cols(3 * D, FF), du, NT).astype(bf16)
        for j in range(3):
            p_buf[m, (9 + j) * 2 + c] = do[256 * j : 256 * (j + 1), :]

    def heads_backward(m):
        co, si = rope[m, 0], rope[m, 1]
        pending = {}
        for t in range(HEADS + 1):
            if t < HEADS:
                g, rows = t // 4, slice(64 * (t % 4), 64 * (t % 4) + 64)
                do = (both(p_buf, m, 9 + g, rows).astype(f32) * inv[m, t, 0:1, :]).astype(bf16)
                o = both(q_buf, m, 9 + g, rows)
                inner = jnp.sum(do.astype(f32) * o.astype(f32), axis=0, keepdims=True)
                pending[t] = (do, inner, dot(both(q_buf, m, 6 + g, rows), do, TN))
            h = t - 1
            if 0 <= h:
                g, rows = h // 4, slice(64 * (h % 4), 64 * (h % 4) + 64)
                do, inner, dr = pending.pop(h)
                e = jnp.concatenate([e_buf[m, h // 6, h % 6 * 2], e_buf[m, h // 6, h % 6 * 2 + 1]], axis=1)
                ds = e * (dr - inner).astype(bf16)
                dvv = dot(do, e, NT)
                dq = dot(both(q_buf, m, 3 + g, rows), ds, NN)
                dk = dot(both(q_buf, m, g, rows), ds, NT)
                for part, x in ((0, dq * 0.125), (1, dk * LN2)):
                    t1, t2 = x[:32], x[32:]
                    x = jnp.concatenate([t1 * co + t2 * si, t2 * co - t1 * si], axis=0).astype(bf16)
                    p_buf[m, (3 * part + g) * 2, rows, :] = x[:, 0:256]
                    p_buf[m, (3 * part + g) * 2 + 1, rows, :] = x[:, 256:512]
                dvv = dvv.astype(bf16)
                p_buf[m, (6 + g) * 2, rows, :] = dvv[:, 0:256]
                p_buf[m, (6 + g) * 2 + 1, rows, :] = dvv[:, 256:512]

    def close_back(m, c):
        rows = rows_of(c)
        dp_t = jnp.concatenate([p_buf[m, fb * 2 + c] for fb in range(9)], axis=0)
        da = dot(dp_t, w_cols(0, 3 * D), TT) + xh[m, rows, :]
        finish_backward(m, c, da.astype(bf16))

    def add(m, ref, index, new):
        held = ref[index]
        new = new.reshape(held.shape)
        ref[index] = jnp.where(m == 0, new, held.astype(f32) + new).astype(bf16)

    def attention_weights(m):
        a_t = a_buf[m].T

        def part(n, _):
            cols = pl.ds(pl.multiple_of(n * D, D), D)
            d = jnp.concatenate(
                [jnp.concatenate([p_buf[m, (3 * n + j) * 2], p_buf[m, (3 * n + j) * 2 + 1]], axis=1) for j in range(3)],
                axis=0,
            )
            add(m, dw, (slice(None),) * 4 + (cols,), dot(a_t, d, NT))
            db[:, cols] += dot(jnp.ones((8, BLK), bf16), d, NT)
            return 0

        lax.fori_loop(0, 3, part, 0)
        o = jnp.concatenate([attended(m, 0), attended(m, 1)], axis=1)
        add(m, dw, (slice(None),) * 4 + (slice(3 * D, FF),), dot(o, y_buf[m], NN))

    def feed_rows(m, c):
        arrive(m, c)
        rows = rows_of(c)
        a = a_buf[m, rows, :]
        u, hidden = None, {}
        for t in range(8):
            if t < 6:
                cols = slice(512 * t, 512 * (t + 1))
                hidden[t] = dot(a, w_cols(512 * t, 512 * (t + 1)), NN) + vec_in[:, cols]
            n = t - 2
            if n >= 0:
                h = hidden.pop(n)
                h2 = h * h
                s = 0.5 * jnp.tanh(h * (K0 + K1 * h2)) + 0.5
                g = h * s
                slope = (s + g * (1.0 - s) * (2.0 * K0 + 6.0 * K1 * h2)).astype(bf16)
                g = g.astype(bf16)
                for j in range(2):
                    q_buf[m, c * 12 + 2 * n + j] = g[:, 256 * j : 256 * (j + 1)]
                    e_buf[m, 0, 2 * n + j, rows, :] = slope[:, 256 * j : 256 * (j + 1)]
                x = dot(g, w_rows(512 * n, 512 * (n + 1)), NN)
                u = x if u is None else u + x
        finish_forward(m, c, u + vec_out[:, 2 * D :] + a.astype(f32))

    def feed_forward(m):
        @pl.when(m == 0)
        def _():
            load_wi.wait()
            load_wo.wait()
            load_wd.wait()

        lax.fori_loop(0, 2, lambda c, _: (feed_rows(m, c), 0)[1], 0)

    def feed_open_back(m, c):
        arrive_back(m, c)
        start_backward(m, c)

    def feed_rows_back(m, c):
        rows = rows_of(c)
        du = y_buf[m, rows, :]
        da, grads = xh[m, rows, :], {}
        for t in range(8):
            if t < 6:
                grads[t] = dot(du, w_rows(512 * t, 512 * (t + 1)), NT)
            n = t - 2
            if n >= 0:
                slope = jnp.concatenate([e_buf[m, 0, 2 * n + j, rows, :] for j in range(2)], axis=1)
                dh = (grads.pop(n) * slope.astype(f32)).astype(bf16)
                for j in range(2):
                    p_buf[m, c * 12 + 2 * n + j] = dh[:, 256 * j : 256 * (j + 1)]
                da = da + dot(dh, w_cols(512 * n, 512 * (n + 1)), NT)
        finish_backward(m, c, da.astype(bf16))

    def tile(buf, m, n):
        return jnp.concatenate(
            [jnp.concatenate([buf[m, c * 12 + 3 * n + j] for j in range(3)], axis=1) for c in range(2)], axis=0
        )

    def feed_weights_down(m):
        def part(n, _):
            add(m, dv, (n // 2, n % 2), dot(tile(q_buf, m, n), y_buf[m], TN))
            return 0

        lax.fori_loop(0, 4, part, 0)

    def feed_weights_in(m):
        def part(n, _):
            cols = pl.ds(pl.multiple_of(n * D, D), D)
            dh = tile(p_buf, m, n)
            add(m, dw, (slice(None),) * 4 + (cols,), dot(a_buf[m], dh, TN))
            db[:, cols] += jnp.broadcast_to(jnp.sum(dh.astype(f32), axis=0, keepdims=True), (8, D))
            return 0

        lax.fori_loop(0, 4, part, 0)

    def part_of(number):
        if number in AWAY:
            return DOWN_PARTS[number - len(PARTS)], wd
        return PARTS[number], dv if PARTS[number][0] else dw

    def landing(number, step):
        part = part_of(number)[0]
        if not part[0]:
            place = ((0,), (1, 0), (1, 1, 0))[step]
            rest = (slice(None),) * (4 - len(place))
            return wi.at[place + rest + (pl.ds(part[1], part[2]),)]
        half = 0 if number in AWAY else 1
        number = number % len(PARTS)
        q, corner = number // 2, (pl.ds(0, 384), pl.ds(128 * (number % 2), 128))
        place = ((slice(None), half, pl.ds(2 * q, 2)), (0, half, pl.ds(6 + 2 * q, 2)), (1, half, 6 + q))[step]
        return e_buf.at[place + corner]

    def share_of(number, step, flip):
        part, grad = part_of(number)
        order = part[3]
        index = [slice(None)] * 3
        for i in range(step + 1):
            own = bit(me, order[i])
            index[2 - order[i]] = 1 - own if flip and i == step else own
        return grad.at[tuple(index) + (slice(None), pl.ds(part[1], part[2]))]

    def step_copy(number, step):
        return pltpu.make_async_remote_copy(
            src_ref=share_of(number, step, True),
            dst_ref=landing(number, step),
            send_sem=rs_send.at[number, step],
            recv_sem=rs_recv.at[number, step],
            device_id={"dp": peer(part_of(number)[0][3][step])},
            device_id_type=MESH,
        )

    def move_copy(p):
        index = (slice(None),) * 4 + (pl.ds(DOWN_PARTS[p][1], DOWN_PARTS[p][2]),)
        return pltpu.make_async_remote_copy(
            src_ref=dv.at[index],
            dst_ref=wd.at[index],
            send_sem=move_send.at[p],
            recv_sem=move_recv.at[p],
            device_id={"section": sec + 2},
            device_id_type=MESH,
        )

    def back_copy(p):
        return pltpu.make_async_remote_copy(
            src_ref=back.at[p],
            dst_ref=back.at[p],
            send_sem=back_send.at[p],
            recv_sem=back_recv.at[p],
            device_id={"section": sec - 2},
            device_id_type=MESH,
        )

    def result_copy(number):
        down, first, width, _ = PARTS[number]
        cols = pl.ds(first, width)
        if down:
            return pltpu.make_async_copy(xh.at[1, pl.ds(0, 384), cols], out_down.at[0, :, cols], out_sem.at[number])
        rows = pl.ds(96 * (first // D), 96)
        return pltpu.make_async_copy(xh.at[0, rows, pl.ds(first % D, width)], out_in.at[0, :, cols], out_sem.at[number])

    def send_step(number, step):
        if step == 0 and number in AWAY:
            move_copy(number - len(PARTS)).wait_recv()
        step_copy(number, step).start()

    def take_step(number, step):
        step_copy(number, step).wait_recv()
        down, first, width, _ = part_of(number)[0]
        share = share_of(number, step, False)
        total = share[...].astype(f32) + landing(number, step)[...].astype(f32)
        if step < 2:
            share[...] = total.astype(bf16)
            send_step(number, step + 1)
        elif number in AWAY:
            back[number - len(PARTS)] = total
            back_copy(number - len(PARTS)).start()
        elif down:
            xh[1, 0:384, first : first + width] = total
            result_copy(number).start()
        else:
            q, off = first // D, first % D
            xh[0, 96 * q : 96 * (q + 1), off : off + width] = total
            result_copy(number).start()

    def exchange(numbers, ahead, lag, started, also=None):
        n = len(numbers)
        for t in range(started, n + ahead + 2 * lag):
            for step in (2, 1, 0):
                i = t - ahead - lag * step
                if 0 <= i < n:
                    take_step(numbers[i], step)
            if t < n:
                send_step(numbers[t], 0)
            if also is not None and t == started + 7:
                also()
        for number in numbers:
            for step in range(3):
                step_copy(number, step).wait_send()

    def weights_free():
        for b in range(3):
            pl.semaphore_signal(free_sem.at[b], inc=1, device_id={"dp": peer(b)}, device_id_type=MESH)

    def await_free():
        for b in range(3):
            pl.semaphore_wait(free_sem.at[b], 1)

    late = sec >= 2

    def span(m):
        return jnp.where(late, 0, m), jnp.where(late & (m == 0), 0, m + 1)

    def attention_backward(m):
        lax.fori_loop(0, 2, lambda c, _: (open_back(m, c), 0)[1], 0)
        heads_backward(m)
        lax.fori_loop(0, 2, lambda c, _: (close_back(m, c), 0)[1], 0)

        @pl.when(m == MICRO - 1)
        def _():
            weights_free()

        lax.fori_loop(*span(m), lambda i, _: (attention_weights(i), 0)[1], 0)

    def feed_backward(m):
        early = (sec == 1) & (m == MICRO - 1)
        begin, end = span(m)

        def down_products(begin, end):
            lax.fori_loop(begin, end, lambda i, _: (feed_weights_down(i), 0)[1], 0)

        def rows(c, _):
            feed_open_back(m, c)

            @pl.when(early & (c == 1))
            def _():
                down_products(begin, end)
                for number in DOWN[MOVED:]:
                    send_step(number, 0)
                pl.semaphore_wait(room_sem, 1)
                for p in range(MOVED):
                    move_copy(p).start()

            feed_rows_back(m, c)
            return 0

        lax.fori_loop(0, 2, rows, 0)

        @pl.when(m == MICRO - 1)
        def _():
            weights_free()

        @pl.when((sec == 3) & (m == MICRO - 1))
        def _():
            pl.semaphore_signal(room_sem, inc=1, device_id={"section": 1}, device_id_type=MESH)

        @pl.when(jnp.logical_not(early))
        def _():
            down_products(begin, end)

        @pl.when((sec == 3) & (m == MICRO - 1))
        def _():
            for number in DOWN:
                send_step(number, 0)

            def give(i, _):
                y = [dw[i // 2, i % 2, 0, 0:64, D * k : D * (k + 1)] for k in range(4)]
                fill(i // 2, i % 2, jnp.concatenate(y, axis=0))
                return 0

            lax.fori_loop(0, 4, give, 0)

        lax.fori_loop(begin, end, lambda i, _: (feed_weights_in(i), 0)[1], 0)

    @pl.when(even)
    def _():
        attention_tables(0)
        for i in range(3):
            b = jnp.broadcast_to(vec_in[:, D * i : D * (i + 1)], (128, D))
            bias_t[D * i : D * (i + 1), :] = b.T

    pl.semaphore_wait(barrier, 3 + GROUP - 1)

    def task(t, _):
        forward = jnp.where(sec == 3, t % 2 == 0, t < 2)
        m = jnp.where(sec == 3, t // 2, t % 2)

        @pl.when(forward & even)
        def _():
            attention_forward(m)

        @pl.when(forward & odd)
        def _():
            feed_forward(m)

        @pl.when(jnp.logical_not(forward) & even)
        def _():
            attention_backward(m)

        @pl.when(jnp.logical_not(forward) & odd)
        def _():
            feed_backward(m)

        return 0

    lax.fori_loop(0, 2 * MICRO, task, 0)

    await_free()

    vec_send[...] = jnp.zeros_like(vec_send)
    outer = jnp.concatenate([acc[0:1, :], acc[1:2, :], acc[2:3, :]], axis=1)
    for j in range(GROUP):
        vec_send[j, 0:1, :] = db[0:1, 384 * j : 384 * (j + 1)]
        vec_send[j, 1:2, 0:288] = outer[:, 288 * j : 288 * (j + 1)]

    def vec_copy(k):
        there = (me + k) % GROUP
        return pltpu.make_async_remote_copy(
            src_ref=vec_send.at[there],
            dst_ref=vec_recv.at[k],
            send_sem=vec_ssem.at[k],
            recv_sem=vec_rsem.at[k],
            device_id={"dp": there * low + dp % low},
            device_id_type=MESH,
        )

    for k in range(1, GROUP):
        vec_copy(k).start()

    zeros = pltpu.make_async_copy(xh.at[1, pl.ds(0, 384)], out_down.at[0], out_sem.at[0])

    @pl.when(even)
    def _():
        xh[1, 0:384, :] = jnp.zeros((384, D), f32)
        zeros.start()

    @pl.when(sec == 1)
    def _():
        exchange(DOWN[MOVED:] + IN, 6, 6, len(DOWN) - MOVED)
        for p in range(MOVED):
            back_copy(p).wait_recv()
            first, width = DOWN_PARTS[p][1], DOWN_PARTS[p][2]
            xh[1, 0:384, first : first + width] = back[p]
            result_copy(p).start()
            move_copy(p).wait_send()

    @pl.when(sec == 3)
    def _():
        def shares():
            for m in range(MICRO):
                for c in range(2):
                    share(m, c, 3, mixed, mix_recv)

        exchange(ORDER_3, 6, 6, len(DOWN), shares)
        for p in range(MOVED):
            back_copy(p).wait_send()

    @pl.when(even)
    def _():
        exchange(IN, 5, 5, 0)

    total = vec_send[me]
    for k in range(1, GROUP):
        vec_copy(k).wait_recv()
        total = total + vec_recv[k]
    out_vec_in[...] = total[0:1, :]
    out_vec_out[...] = total[1:2, 0:288]

    for k in range(1, GROUP):
        vec_copy(k).wait_send()

    for m in range(MICRO):
        for c in range(2):

            @pl.when(sec > 0)
            def _():
                backward_copy(m, c).wait_send()
                share_copy(m, c, 0, in_grad, grad_recv).wait_recv()

            @pl.when(sec < 3)
            def _():
                share_copy(m, c, 0, mixed, mix_recv).wait_recv()

            @pl.when(sec == 0)
            def _():
                own_copy(m, c, 0, in_grad).wait()
                for k in range(1, 4):
                    share_copy(m, c, k, in_grad, grad_recv).wait_send()

            @pl.when(sec == 3)
            def _():
                own_copy(m, c, 3, mixed).wait()
                for k in range(3):
                    share_copy(m, c, k, mixed, mix_recv).wait_send()

    for number in IN:
        result_copy(number).wait()

    @pl.when(odd)
    def _():
        for number in DOWN:
            result_copy(number).wait()

    @pl.when(even)
    def _():
        zeros.wait()


def settle(*refs):
    count = (len(refs) - 2) // 3
    given, taken, held = refs[:count], refs[count : 2 * count], refs[2 * count : 3 * count]
    sem_in, sem_out = refs[-2:]
    steps = []
    for i in range(count):
        rows = given[i].shape[1]
        cut = rows // 2 if len(given[i].shape) == 3 else rows
        for k in range(rows // cut):
            index = (slice(None), pl.ds(k * cut, cut))
            n = len(steps)
            steps.append(
                (
                    pltpu.make_async_copy(given[i].at[index], held[i].at[index], sem_in.at[n]),
                    pltpu.make_async_copy(held[i].at[index], taken[i].at[index], sem_out.at[n]),
                )
            )
    for first, _ in steps:
        first.start()
    for first, second in steps:
        first.wait()
        second.start()
    for _, second in steps:
        second.wait()


def on_device(inputs, segment_ids, w_in, w_down, vec_in, vec_out, cotangent):
    world = lax.axis_size("dp")
    low = world // GROUP
    hbm = pl.BlockSpec(memory_space=pl.ANY)
    vmem = pl.BlockSpec(memory_space=pltpu.VMEM)
    V, S = pltpu.VMEM, pltpu.SemaphoreType.DMA
    parts = len(PARTS) + MOVED
    shapes = (
        jax.ShapeDtypeStruct((MICRO, D // 4, BLK), bf16),
        jax.ShapeDtypeStruct((MICRO, D // 4, BLK), bf16),
        jax.ShapeDtypeStruct((1, D // GROUP, FF), f32),
        jax.ShapeDtypeStruct((1, FF // GROUP, D), f32),
        jax.ShapeDtypeStruct((1, FF // GROUP), f32),
        jax.ShapeDtypeStruct((1, 3 * D // GROUP), f32),
    )
    results = pl.pallas_call(
        functools.partial(kernel, low),
        out_shape=shapes,
        in_specs=[hbm, vmem, hbm, hbm, vmem, vmem, hbm],
        out_specs=(hbm, hbm, hbm, hbm, vmem, vmem),
        scratch_shapes=[
            V((2, 2, 2, 96, FF), bf16),
            V((2, 2, 2, 384, D), bf16),
            V((MICRO, BLK, D), bf16),
            V((MICRO, BLK, D), bf16),
            V((MICRO, BLK, D), bf16),
            V((MICRO, 2, 12, 512, 256), bf16),
            V((MICRO, 24, 256, 256), bf16),
            V((MICRO, 24, 256, 256), bf16),
            V((MICRO, BLK, D), f32),
            V((MICRO, BLK, 1), f32),
            V((BLK, BLK), f32),
            V((MICRO, 2, HEAD_DIM // 2, BLK), f32),
            V((MICRO, HEADS, 8, BLK), f32),
            V((3 * D, 128), f32),
            V((2, 2, 2, 96, FF), bf16),
            V((2, 2, 2, 384, D), bf16),
            V((4, MICRO, D // 4, BLK), bf16),
            V((8, D), f32),
            V((8, FF), f32),
            V((GROUP, 8, 384), f32),
            V((GROUP, 8, 384), f32),
            S((3,)),
            S((MICRO,)),
            S((MICRO, 2)),
            S((MICRO, 2)),
            S((MICRO, 2)),
            S((MICRO, 2)),
            S((4, MICRO, 2)),
            S((MICRO, 2)),
            S((MICRO, 2)),
            S((GROUP,)),
            S((GROUP,)),
            pltpu.SemaphoreType.REGULAR((3,)),
            S((parts, 3)),
            S((parts, 3)),
            S((len(PARTS),)),
            V((MOVED, FF // GROUP, 128), f32),
            S((MOVED,)),
            S((MOVED,)),
            S((MOVED,)),
            S((MOVED,)),
            pltpu.SemaphoreType.REGULAR,
        ],
        compiler_params=pltpu.CompilerParams(
            collective_id=0, has_side_effects=True, vmem_limit_bytes=63 * MIB
        ),
    )(inputs, segment_ids, w_in.reshape(2, 2, 2, 96, FF), w_down.reshape(2, 2, 2, 384, D), vec_in, vec_out, cotangent)
    mixed, in_grad, grad_in, grad_down, vec_a, vec_b = pl.pallas_call(
        settle,
        out_shape=shapes,
        in_specs=[hbm] * len(shapes),
        out_specs=(hbm,) * len(shapes),
        scratch_shapes=[V(x.shape, x.dtype) for x in shapes] + [S((10,)), S((10,))],
    )(*results)
    if low > 1:
        groups = [[g * low + i for i in range(low)] for g in range(GROUP)]

        def rest(value):
            return lax.psum_scatter(
                value, "dp", scatter_dimension=1, axis_index_groups=groups, tiled=True
            )

        grad_in, grad_down, vec_a, vec_b = rest(grad_in), rest(grad_down), rest(vec_a), rest(vec_b)
    mixed, in_grad = jnp.swapaxes(mixed, 1, 2), jnp.swapaxes(in_grad, 1, 2)
    return mixed, in_grad, grad_in, grad_down, vec_a, vec_b


def solution(mesh):
    placed = (
        P(None, "dp", None),
        P(None, "dp"),
        P("section", None, None),
        P("section", None, None),
        P("section", None),
        P("section", None),
        P(None, "dp", None),
    )
    return jax.shard_map(
        on_device,
        mesh=mesh,
        in_specs=placed,
        out_specs=(
            P(None, "dp", "section"),
            P(None, "dp", "section"),
            P("section", "dp", None),
            P("section", "dp", None),
            P("section", "dp"),
            P("section", "dp"),
        ),
        check_vma=False,
    )
```
